32 devices in a mesh: dp: 16 (over z, y, x), head: 2 (over core).
Axes of the slice: x: 2, y: 2, z: 4, core: 2. Of those that a mesh axis runs over, the one named last changes fastest.
Arguments:
- tokens: bfloat16 [8192, 768], P('dp'), may hold values from -6 to 6
- memory: bfloat16 [32768, 768], P(('dp', 'head')), may hold values from -12 to 12
- cotangent: bfloat16 [8192, 768], P('dp'), may hold values from -12 to 12
- patch_item: int32 [32768], P('dp'), may hold values from 0 to 3, as said below
- patch_mask: int32 [32768], P('dp'), may hold values from 0 to 1, as said below
- text_item: int32 [32], P('dp'), may hold values from 0 to 3, as said below
- text_len: int32 [32], P('dp'), may hold values from 1 to 256
- norm_gains: float32 [3, 768], P(None, 'dp'), may hold values from 0.3 to 2.3
- gains_mean: float32 [3, 768], P(None, 'dp'), may hold values from -0.001953125 to 0.001953125
- gains_square: float32 [3, 768], P(None, 'dp'), may hold values from 4.4493937e-08 to 3.6018903e-07
- self_proj: float32 [3, 768, 768], P(None, 'dp', 'head'), may hold values from -0.21875 to 0.21875
- self_proj_mean: float32 [3, 768, 768], P(None, 'dp', 'head'), may hold values from -0.00048828125 to 0.00048828125
- self_proj_square: float32 [3, 768, 768], P(None, 'dp', 'head'), may hold values from 2.7543867e-09 to 2.2246969e-08
- query_cross: float32 [768, 768], P('dp', 'head'), may hold values from -0.21875 to 0.21875
- query_cross_mean: float32 [768, 768], P('dp', 'head'), may hold values from -0.00048828125 to 0.00048828125
- query_cross_square: float32 [768, 768], P('dp', 'head'), may hold values from 2.7543867e-09 to 2.2246969e-08
- keyval_cross: float32 [2, 768, 768], P(None, ('dp', 'head')), may hold values from -0.21875 to 0.21875
- keyval_cross_mean: float32 [2, 768, 768], P(None, ('dp', 'head')), may hold values from -0.00048828125 to 0.00048828125
- keyval_cross_square: float32 [2, 768, 768], P(None, ('dp', 'head')), may hold values from 2.7543867e-09 to 2.2246969e-08
- out_proj: float32 [2, 768, 768], P(None, 'head', 'dp'), may hold values from -0.875 to 0.875
- out_proj_mean: float32 [2, 768, 768], P(None, 'head', 'dp'), may hold values from -0.00048828125 to 0.00048828125
- out_proj_square: float32 [2, 768, 768], P(None, 'head', 'dp'), may hold values from 2.7543867e-09 to 2.2246969e-08
- mlp_input: float32 [2, 768, 2048], P(None, 'dp', 'head'), may hold values from -0.21875 to 0.21875
- mlp_input_mean: float32 [2, 768, 2048], P(None, 'dp', 'head'), may hold values from -0.00048828125 to 0.00048828125
- mlp_input_square: float32 [2, 768, 2048], P(None, 'dp', 'head'), may hold values from 2.7543867e-09 to 2.2246969e-08
- mlp_output: float32 [2048, 768], P('head', 'dp'), may hold values from -0.125 to 0.125
- mlp_output_mean: float32 [2048, 768], P('head', 'dp'), may hold values from -0.00048828125 to 0.00048828125
- mlp_output_square: float32 [2048, 768], P('head', 'dp'), may hold values from 2.7543867e-09 to 2.2246969e-08
Outputs:
- output: bfloat16 [8192, 768], P('dp')
- tokens_grad: float32 [8192, 768], P('dp')
- memory_grad: float32 [32768, 768], P(('dp', 'head'))
- grad_norm: float32 [], replicated
- new_gains: float32 [3, 768], P(None, 'dp')
- new_gains_mean: float32 [3, 768], P(None, 'dp')
- new_gains_square: float32 [3, 768], P(None, 'dp')
- new_self_proj: float32 [3, 768, 768], P(None, 'dp', 'head')
- new_self_proj_mean: float32 [3, 768, 768], P(None, 'dp', 'head')
- new_self_proj_square: float32 [3, 768, 768], P(None, 'dp', 'head')
- new_query_cross: float32 [768, 768], P('dp', 'head')
- new_query_cross_mean: float32 [768, 768], P('dp', 'head')
- new_query_cross_square: float32 [768, 768], P('dp', 'head')
- new_keyval_cross: float32 [2, 768, 768], P(None, ('dp', 'head'))
- new_keyval_cross_mean: float32 [2, 768, 768], P(None, ('dp', 'head'))
- new_keyval_cross_square: float32 [2, 768, 768], P(None, ('dp', 'head'))
- new_out_proj: float32 [2, 768, 768], P(None, 'head', 'dp')
- new_out_proj_mean: float32 [2, 768, 768], P(None, 'head', 'dp')
- new_out_proj_square: float32 [2, 768, 768], P(None, 'head', 'dp')
- new_mlp_input: float32 [2, 768, 2048], P(None, 'dp', 'head')
- new_mlp_input_mean: float32 [2, 768, 2048], P(None, 'dp', 'head')
- new_mlp_input_square: float32 [2, 768, 2048], P(None, 'dp', 'head')
- new_mlp_output: float32 [2048, 768], P('head', 'dp')
- new_mlp_output_mean: float32 [2048, 768], P('head', 'dp')
- new_mlp_output_square: float32 [2048, 768], P('head', 'dp')
The draws below stay inside these ranges and needn't reach their ends.
Inputs may be any that keep to these rules, and one draw needn't show every extreme that they name: `patch_item`: each group of 2048 patches consists of units of 512 patches; its items take 1, 2 or 4 units, are aligned to their size and never cross a boundary of 4 units; every patch holds the first unit of its item, counted from 0 within the group. `patch_mask`: the first patch of every unit is 1. `text_item`: text s holds the first unit of one of the items of group s // 2.
All inputs are finite; a program needn't handle non-finite values.
Results may differ from the reference program's by a relative error of at most 0.03.
Values may be sent and summed in bfloat16 or wider, within the bound.
A program may use at most 128 MiB of HBM per device.

```python
import math
import jax
import jax.numpy as jnp
from jax import lax

D = 768
HD = 64
FF = 2048
TXT = 256
SEQ_DEV = 2
UNIT = 512
UNITS_DP = 4
STEP = 10
TOK_DEV = 512
TOKENS = 8192
PATCH_DP = 2048
PATCHES = 32768
PARAMS = 9439488
N_DP = 16


ITEM_PATTERNS = ((0, 0, 0, 0), (0, 0, 2, 2), (0, 0, 2, 3), (0, 1, 2, 2), (0, 1, 2, 3))


def forced_group(key):
    pattern_key, forced_key = jax.random.split(jax.random.fold_in(key, 101))
    return (pattern_key, jax.random.randint(forced_key, (), 0, N_DP))


def unit_starts(key):
    quarters = UNITS_DP // 4
    pattern_key, forced = forced_group(key)
    picked = jax.random.randint(pattern_key, (N_DP, quarters), 0, 5)
    group_index = jnp.arange(N_DP, dtype=jnp.int32)[:, None]
    block_index = jnp.arange(quarters, dtype=jnp.int32)[None, :]
    picked = jnp.where((group_index == forced) & (block_index == quarters - 1), 4, picked)
    table = jnp.array(ITEM_PATTERNS, dtype=jnp.int32)
    starts = table[picked] + 4 * block_index[:, :, None]
    return starts.reshape(N_DP, UNITS_DP).astype(jnp.int32)


def draw_patch_item(key, part):
    return jnp.repeat(unit_starts(key), UNIT, axis=1).reshape(N_DP * UNIT * UNITS_DP)


def draw_text_item(key, part):
    starts = unit_starts(key)
    pattern_key, forced = forced_group(key)
    units = jax.random.randint(jax.random.fold_in(key, 202), (N_DP, SEQ_DEV), 0, UNITS_DP)
    group_index = jnp.arange(N_DP, dtype=jnp.int32)[:, None]
    text_index = jnp.arange(SEQ_DEV, dtype=jnp.int32)[None, :]
    other = (forced + 1) % N_DP
    units = jnp.where((group_index == forced) & (text_index == 0), UNITS_DP - 1, units)
    units = jnp.where((group_index == other) & (group_index != forced) & (text_index == 0), 0, units)
    return jnp.take_along_axis(starts, units, axis=1).reshape(N_DP * SEQ_DEV).astype(jnp.int32)


def draw_patch_mask(key, part):
    total_patches = N_DP * UNIT * UNITS_DP
    drawn = jax.random.randint(jax.random.fold_in(key, 303), (total_patches,), 0, 8)
    leading = jnp.arange(total_patches, dtype=jnp.int32) % UNIT == 0
    return jnp.where(leading | (drawn < 7), 1, 0).astype(jnp.int32)


def draw_text_len(key, part):
    texts = N_DP * SEQ_DEV
    drawn = jax.random.randint(jax.random.fold_in(key, 404), (texts,), 1, TXT + 1)
    forced = jax.random.randint(jax.random.fold_in(key, 405), (), 0, texts)
    return jnp.where(jnp.arange(texts, dtype=jnp.int32) == forced, TXT, drawn).astype(jnp.int32)


def width_ramp():
    place = jnp.arange(D, dtype=jnp.float32) / D
    return 0.5 + place


def ramped_normal(key, rows):
    base = jnp.clip(jax.random.normal(key, (rows, D), jnp.float32), -6.0, 6.0)
    return base * width_ramp()[None, :]


def draw_memory(key, part):
    return ramped_normal(jax.random.fold_in(key, 501), PATCHES).astype(jnp.bfloat16)


def draw_cotangent(key, part):
    return ramped_normal(jax.random.fold_in(key, 502), TOKENS).astype(jnp.bfloat16)


def draw_norm_gains(key, part):
    noise = jax.random.uniform(jax.random.fold_in(key, 503), (3, D), jnp.float32, -0.15, 0.15)
    return ((1.0 + noise) * width_ramp()[None, :]).astype(jnp.float32)


def block_scale(key, extent, cuts, smallest, largest):
    def one(dim, parts):
        heights = jax.random.uniform(jax.random.fold_in(jax.random.fold_in(key, 6), dim), (parts,), jnp.float32, smallest / len(cuts), largest / len(cuts))
        return jnp.repeat(jnp.exp(heights), extent[dim] // parts).reshape((-1,) + (1,) * (len(extent) - dim - 1))

    level = one(*cuts[0])
    for cut in cuts[1:]:
        level = level * one(*cut)
    return level


def gaussian(rng, dims, deviation, bound, pieces=(), held_as=jnp.bfloat16):
    values = jax.random.normal(rng, dims, jnp.float32) * deviation
    if len(pieces) > 0:
        values = block_scale(rng, dims, pieces, -0.22, 0.18) * values
    return jnp.clip(values, min=-bound, max=bound).astype(held_as)


def setup_inputs(seed: int = 0) -> dict:
    splits = jax.random.split(jax.random.key(seed), 29)
    return {
        "tokens": gaussian(splits[0], (TOKENS, D), 1.0, 6.0, ((0, 16),)),
        "memory": draw_memory(jax.random.fold_in(splits[28], 71), 0),
        "cotangent": draw_cotangent(jax.random.fold_in(splits[28], 71), 0),
        "patch_item": draw_patch_item(jax.random.fold_in(splits[28], 71), 0),
        "patch_mask": draw_patch_mask(jax.random.fold_in(splits[28], 71), 0),
        "text_item": draw_text_item(jax.random.fold_in(splits[28], 71), 0),
        "text_len": draw_text_len(jax.random.fold_in(splits[28], 71), 0),
        "norm_gains": draw_norm_gains(jax.random.fold_in(splits[28], 71), 0),
        "gains_mean": gaussian(splits[8], (3, D), (0.44 * PARAMS ** -0.5), 0.001953125, ((1, 16),), jnp.float32),
        "gains_square": jnp.clip(jnp.exp(math.log(3.6018903415424575e-07) - 2.091276 * jax.random.uniform(splits[9], (3, D), jnp.float32) ** block_scale(splits[9], (3, D), ((1, 16),), -0.2, 0.2)), 4.449393742333996e-08, 3.6018903415424575e-07),
        "self_proj": gaussian(splits[10], (3, D, D), D ** -0.5, 0.21875, ((1, 16), (2, 2)), jnp.float32),
        "self_proj_mean": gaussian(splits[11], (3, D, D), (0.11 * PARAMS ** -0.5), 0.00048828125, ((1, 16), (2, 2)), jnp.float32),
        "self_proj_square": jnp.clip(jnp.exp(math.log(2.224696871166998e-08) - 2.089011 * jax.random.uniform(splits[12], (3, D, D), jnp.float32) ** block_scale(splits[12], (3, D, D), ((1, 16), (2, 2)), -0.2, 0.2)), 2.7543867187063142e-09, 2.224696871166998e-08),
        "query_cross": gaussian(splits[13], (D, D), D ** -0.5, 0.21875, ((0, 16), (1, 2)), jnp.float32),
        "query_cross_mean": gaussian(splits[14], (D, D), (0.11 * PARAMS ** -0.5), 0.00048828125, ((0, 16), (1, 2)), jnp.float32),
        "query_cross_square": jnp.clip(jnp.exp(math.log(2.224696871166998e-08) - 2.089011 * jax.random.uniform(splits[15], (D, D), jnp.float32) ** block_scale(splits[15], (D, D), ((0, 16), (1, 2)), -0.2, 0.2)), 2.7543867187063142e-09, 2.224696871166998e-08),
        "keyval_cross": gaussian(splits[16], (2, D, D), D ** -0.5, 0.21875, ((1, 32),), jnp.float32),
        "keyval_cross_mean": gaussian(splits[17], (2, D, D), (0.11 * PARAMS ** -0.5), 0.00048828125, ((1, 32),), jnp.float32),
        "keyval_cross_square": jnp.clip(jnp.exp(math.log(2.224696871166998e-08) - 2.089011 * jax.random.uniform(splits[18], (2, D, D), jnp.float32) ** block_scale(splits[18], (2, D, D), ((1, 32),), -0.2, 0.2)), 2.7543867187063142e-09, 2.224696871166998e-08),
        "out_proj": gaussian(splits[19], (2, D, D), (D // 16) ** -0.5, 0.875, ((1, 2), (2, 16)), jnp.float32),
        "out_proj_mean": gaussian(splits[20], (2, D, D), (0.11 * PARAMS ** -0.5), 0.00048828125, ((1, 2), (2, 16)), jnp.float32),
        "out_proj_square": jnp.clip(jnp.exp(math.log(2.224696871166998e-08) - 2.089011 * jax.random.uniform(splits[21], (2, D, D), jnp.float32) ** block_scale(splits[21], (2, D, D), ((1, 2), (2, 16)), -0.2, 0.2)), 2.7543867187063142e-09, 2.224696871166998e-08),
        "mlp_input": gaussian(splits[22], (2, D, FF), D ** -0.5, 0.21875, ((1, 16), (2, 2)), jnp.float32),
        "mlp_input_mean": gaussian(splits[23], (2, D, FF), (0.11 * PARAMS ** -0.5), 0.00048828125, ((1, 16), (2, 2)), jnp.float32),
        "mlp_input_square": jnp.clip(jnp.exp(math.log(2.224696871166998e-08) - 2.089011 * jax.random.uniform(splits[24], (2, D, FF), jnp.float32) ** block_scale(splits[24], (2, D, FF), ((1, 16), (2, 2)), -0.2, 0.2)), 2.7543867187063142e-09, 2.224696871166998e-08),
        "mlp_output": gaussian(splits[25], (FF, D), FF ** -0.5, 0.125, ((0, 2), (1, 16)), jnp.float32),
        "mlp_output_mean": gaussian(splits[26], (FF, D), (0.11 * PARAMS ** -0.5), 0.00048828125, ((0, 2), (1, 16)), jnp.float32),
        "mlp_output_square": jnp.clip(jnp.exp(math.log(2.224696871166998e-08) - 2.089011 * jax.random.uniform(splits[27], (FF, D), jnp.float32) ** block_scale(splits[27], (FF, D), ((0, 2), (1, 16)), -0.2, 0.2)), 2.7543867187063142e-09, 2.224696871166998e-08),
    }


@jax.custom_vjp
def low(v):
    return lax.optimization_barrier(v.astype(jnp.bfloat16)).astype(jnp.float32)

@jax.custom_vjp
def low_back(v):
    return v

def low_keep(v):
    return (low(v), None)

def low_pass(kept, grad):
    return (grad,)

def back_keep(v):
    return (v, None)

def back_low(kept, grad):
    return (low(grad),)
low.defvjp(low_keep, low_pass)
low_back.defvjp(back_keep, back_low)
BETA1 = 0.9
BETA2 = 0.95
ADAM_EPS = 1e-08
DECAY = 0.1
CLIP = 1.0
NORM_EPS = 1e-06
MASKED = -1e+30
HIGHEST = lax.Precision.HIGHEST

def product(left, right):
    return jnp.dot(left, right, precision=HIGHEST)

def rms_gain(values, gain):
    inverse = lax.rsqrt(lax.optimization_barrier(jnp.mean(values * values, axis=-1, keepdims=True)) + NORM_EPS)
    return values * inverse * gain

def layer_masks(text_item, text_len, patch_item, patch_mask, count_rows):
    positions = jnp.arange(count_rows, dtype=jnp.int32)
    sequence = positions // TXT
    place = positions - sequence * TXT
    slots = jnp.arange(text_len.shape[0], dtype=jnp.int32)
    member = sequence[:, None] == slots[None, :]
    own_length = lax.optimization_barrier(jnp.sum(jnp.where(member, text_len[None, :], 0), axis=1))
    own_item = lax.optimization_barrier(jnp.sum(jnp.where(member, text_item[None, :], 0), axis=1))
    self_allowed = (sequence[:, None] == sequence[None, :]) & (place[None, :] <= place[:, None]) & (place[None, :] < own_length[None, :])
    cross_allowed = (own_item[:, None] == patch_item[None, :]) & (patch_mask[None, :] == 1)
    return (self_allowed, cross_allowed)

def attention(query, keys, values, allowed):
    length = query.shape[0]
    width = query.shape[1]
    heads = width // HD
    query_heads = query.reshape(length, heads, HD)
    key_heads = keys.reshape(keys.shape[0], heads, HD)
    value_heads = values.reshape(values.shape[0], heads, HD)
    scores = jnp.einsum('qhd,khd->hqk', query_heads, key_heads, precision=HIGHEST) * HD ** (-0.5)
    scores = low_back(jnp.where(allowed[None, :, :], scores, MASKED))
    probs = low(jax.nn.softmax(scores, axis=-1))
    mixed = jnp.einsum('hqk,khd->qhd', probs, value_heads, precision=HIGHEST)
    return low_back(low(mixed.reshape(length, width)))

def group_forward(weights, tokens, memory, patch_item, patch_mask, text_item, text_len):
    gains, self_proj, query_cross, keyval_cross, out_proj, mlp_input, mlp_output = weights
    self_allowed, cross_allowed = layer_masks(text_item, text_len, patch_item, patch_mask, tokens.shape[0])
    normed_one = low(rms_gain(tokens, gains[0]))
    query = low_back(low(product(normed_one, self_proj[0])))
    keys = low_back(low(product(normed_one, self_proj[1])))
    values = low_back(low(product(normed_one, self_proj[2])))
    first = tokens + low_back(product(attention(query, keys, values, self_allowed), out_proj[0]))
    normed_two = low(rms_gain(first, gains[1]))
    cross_query = low_back(low(product(normed_two, query_cross)))
    memory_keys = low_back(low(product(memory, keyval_cross[0])))
    memory_values = low_back(low(product(memory, keyval_cross[1])))
    second = first + low_back(product(attention(cross_query, memory_keys, memory_values, cross_allowed), out_proj[1]))
    normed_three = low(rms_gain(second, gains[2]))
    gate = low_back(product(normed_three, mlp_input[0]))
    up_part = low_back(product(normed_three, mlp_input[1]))
    hidden = low(jax.nn.gelu(gate, approximate=True) * up_part)
    return second + low_back(product(hidden, mlp_output))

def adam_step(weight, first, second, grad, rate, decay):
    first_new = BETA1 * first + (1.0 - BETA1) * grad
    second_new = BETA2 * second + (1.0 - BETA2) * grad * grad
    mean_hat = first_new / (1.0 - BETA1 ** STEP)
    square_hat = second_new / (1.0 - BETA2 ** STEP)
    weight_new = weight - rate * (mean_hat / (jnp.sqrt(square_hat) + ADAM_EPS) + decay * weight)
    return (weight_new, first_new, second_new)

def reference(tokens, memory, cotangent, patch_item, patch_mask, text_item, text_len, norm_gains, gains_mean, gains_square, self_proj, self_proj_mean, self_proj_square, query_cross, query_cross_mean, query_cross_square, keyval_cross, keyval_cross_mean, keyval_cross_square, out_proj, out_proj_mean, out_proj_square, mlp_input, mlp_input_mean, mlp_input_square, mlp_output, mlp_output_mean, mlp_output_square):
    masters = (norm_gains, self_proj, query_cross, keyval_cross, out_proj, mlp_input, mlp_output)
    grouped_ints = (patch_item.reshape(N_DP, PATCH_DP), patch_mask.reshape(N_DP, PATCH_DP), text_item.reshape(N_DP, SEQ_DEV), text_len.reshape(N_DP, SEQ_DEV))

    def forward(token_rows, memory_rows, weights_master):
        weights = tuple((low(weight) for weight in weights_master))

        def one_group(pack):
            return group_forward(weights, *pack)
        grouped = lax.map(jax.checkpoint(one_group), (token_rows.reshape(N_DP, TOK_DEV, D), memory_rows.reshape(N_DP, PATCH_DP, D)) + grouped_ints)
        return grouped.reshape(N_DP * TOK_DEV, D)
    result, pull = jax.vjp(forward, tokens.astype(jnp.float32), memory.astype(jnp.float32), masters)
    tokens_grad, memory_grad, weight_grads = pull(cotangent.astype(jnp.float32))
    total = jnp.float32(0.0)
    for grad in weight_grads:
        total = total + jnp.sum(grad * grad)
    grad_norm = jnp.sqrt(total)
    factor = jnp.minimum(1.0, CLIP / (grad_norm + NORM_EPS))
    rates = (0.5, 2.0 * D ** (-0.5), 2.0 * D ** (-0.5), 2.0 * D ** (-0.5), 2.0 * (D // 16) ** (-0.5), 2.0 * D ** (-0.5), 2.0 * FF ** (-0.5))
    decays = (0.0, DECAY, DECAY, DECAY, DECAY, DECAY, DECAY)
    states = ((gains_mean, gains_square), (self_proj_mean, self_proj_square), (query_cross_mean, query_cross_square), (keyval_cross_mean, keyval_cross_square), (out_proj_mean, out_proj_square), (mlp_input_mean, mlp_input_square), (mlp_output_mean, mlp_output_square))
    updated = []
    for index in range(7):
        updated.extend(adam_step(masters[index], states[index][0], states[index][1], weight_grads[index] * factor, rates[index], decays[index]))
    return (result.astype(jnp.bfloat16), tokens_grad, memory_grad, grad_norm, updated[0], updated[1], updated[2], updated[3], updated[4], updated[5], updated[6], updated[7], updated[8], updated[9], updated[10], updated[11], updated[12], updated[13], updated[14], updated[15], updated[16], updated[17], updated[18], updated[19], updated[20])
```

```python
import functools

import jax
import jax.numpy as jnp
from jax import lax
from jax.experimental import pallas as pl
from jax.experimental.pallas import tpu as pltpu
from jax.sharding import PartitionSpec as P

D = 768
HD = 64
FF = 2048
TXT = 256
STEP = 10

BETA1 = 0.9
BETA2 = 0.95
ADAM_EPS = 1e-08
DECAY = 0.1
CLIP = 1.0
NORM_EPS = 1e-06
MASKED = -1e30

MESH = pl.DeviceIdType.MESH
BF = jnp.bfloat16
F32 = jnp.float32
VMEM_BYTES = 63 * 2**20

HALF = D // 2
FT = 256
FH = FF // 2
GAIN = 0
CQ = 128
CKV = CQ + 3 * HALF
COS = CKV + 2 * HALF
CQC = COS + HALF
COC = CQC + HALF
CM = COC + HALF
PACK = CM + 3 * FH


def as_bf(value):
    return value.astype(BF)


def as_f32(value):
    return value.astype(F32)


def nn(left, right):
    return lax.dot_general(left, right, (((1,), (0,)), ((), ())), preferred_element_type=F32)


def nt(left, right):
    return lax.dot_general(left, right, (((1,), (1,)), ((), ())), preferred_element_type=F32)


def tn(left, right):
    return lax.dot_general(left, right, (((0,), (0,)), ((), ())), preferred_element_type=F32)


def bit_count(n):
    return n.bit_length() - 1


def gather_jobs(bits):
    if bits == 4:
        first = ((3, 2, 0, 1), (3, 2, 1, 0))
        later = ((0, 3, 2, 1), (1, 3, 2, 0))
    else:
        plain = tuple(range(bits))
        first = later = (plain, plain[::-1])
    bounds = [0, CKV, COS, CM]
    while bounds[-1] < PACK:
        bounds.append(bounds[-1] + 3 * FT)
    jobs = []
    for number, (low, high) in enumerate(zip(bounds[:-1], bounds[1:])):
        middle = low + (high - low) // 256 * 128
        orders = first if number % 3 == 0 else later
        jobs.append((low, middle, orders[0]))
        jobs.append((middle, high, orders[1]))
    return jobs


def block_index(bits, me, free, fixed=None):
    fixed = fixed or {}
    out = []
    for bit in reversed(range(bits)):
        if bit in free:
            out.append(slice(None))
        elif bit in fixed:
            out.append(fixed[bit])
        else:
            out.append((me >> bit) & 1)
    return tuple(out)


def greet(me, head, bits):
    barrier = pltpu.get_barrier_semaphore()
    for bit in range(bits):
        pl.semaphore_signal(barrier, inc=1, device_id=(me ^ (1 << bit), head), device_id_type=MESH)
    pl.semaphore_signal(barrier, inc=1, device_id=(me, 1 - head), device_id_type=MESH)
    pl.semaphore_wait(barrier, bits + 1)


class Gather:
    def __init__(self, bits, me, head, wall, send_sem, recv_sem):
        self.bits, self.me, self.head = bits, me, head
        self.wall, self.send_sem, self.recv_sem = wall, send_sem, recv_sem
        self.jobs = gather_jobs(bits)

    def copy(self, number, phase, received=False):
        low, high, order = self.jobs[number]
        bit = order[phase]
        mine = (self.me >> bit) & 1
        fixed = {bit: 1 - mine if received else mine}
        index = block_index(self.bits, self.me, order[:phase], fixed)
        ref = self.wall.at[index + (slice(None), slice(low, high))]
        return pltpu.make_async_remote_copy(
            src_ref=ref,
            dst_ref=ref,
            send_sem=self.send_sem.at[number, phase],
            recv_sem=self.recv_sem.at[number, phase],
            device_id=(self.me ^ (1 << bit), self.head),
            device_id_type=MESH,
        )

    def start(self, number, phase):
        self.copy(number, phase).start()

    def wait(self, number, phase):
        self.copy(number, phase, True).wait_recv()

    def finish(self):
        for number in range(len(self.jobs)):
            for phase in range(self.bits):
                self.copy(number, phase).wait_send()


def gather_kernel(bits, pack_ref, mem_ref, wall_ref, memall_ref, send_sem, recv_sem, local_sem, mem_sem):
    me, head = lax.axis_index("dp"), lax.axis_index("head")
    greet(me, head, bits)
    own = pltpu.make_async_copy(
        pack_ref, wall_ref.at[block_index(bits, me, ())], local_sem.at[0]
    )
    own.start()
    mem_copy = pltpu.make_async_remote_copy(
        src_ref=mem_ref,
        dst_ref=memall_ref.at[head],
        send_sem=mem_sem.at[0],
        recv_sem=mem_sem.at[1],
        device_id=(me, 1 - head),
        device_id_type=MESH,
    )
    mem_copy.start()
    mem_local = pltpu.make_async_copy(mem_ref, memall_ref.at[head], local_sem.at[1])
    mem_local.start()
    own.wait()
    gather = Gather(bits, me, head, wall_ref, send_sem, recv_sem)
    count = len(gather.jobs)
    groups = count // 2
    for turn in range(groups + bits):
        for group in range(groups):
            phase = turn - group
            for number in (2 * group, 2 * group + 1):
                if 1 <= phase <= bits:
                    gather.wait(number, phase - 1)
                if 0 <= phase < bits:
                    gather.start(number, phase)
    gather.finish()
    mem_local.wait()
    mem_copy.wait_send()
    pltpu.make_async_remote_copy(
        src_ref=mem_ref,
        dst_ref=memall_ref.at[1 - head],
        send_sem=mem_sem.at[0],
        recv_sem=mem_sem.at[1],
        device_id=(me, 1 - head),
        device_id_type=MESH,
    ).wait_recv()


def gather_weights(pack, memory, count):
    bits = bit_count(count)
    rows = pack.shape[0]
    jobs = len(gather_jobs(bits))
    wall, memall = pl.pallas_call(
        functools.partial(gather_kernel, bits),
        out_shape=(
            jax.ShapeDtypeStruct((2,) * bits + (rows, PACK), BF),
            jax.ShapeDtypeStruct((2,) + memory.shape, BF),
        ),
        in_specs=[pl.BlockSpec(memory_space=pl.ANY)] * 2,
        out_specs=(pl.BlockSpec(memory_space=pl.ANY),) * 2,
        scratch_shapes=[
            pltpu.SemaphoreType.DMA((jobs, bits)),
            pltpu.SemaphoreType.DMA((jobs, bits)),
            pltpu.SemaphoreType.DMA((2,)),
            pltpu.SemaphoreType.DMA((2,)),
        ],
        name="gather",
        compiler_params=pltpu.CompilerParams(
            collective_id=1, has_side_effects=True, vmem_limit_bytes=VMEM_BYTES
        ),
    )(pack, memory)
    return wall.reshape(count * rows, PACK), memall.reshape(2 * memory.shape[0], D)


class Exchange:
    def __init__(self, me, head, send, recv, send_sem, recv_sem):
        self.me, self.head = me, head
        self.send, self.recv, self.send_sem, self.recv_sem = send, recv, send_sem, recv_sem

    def copy(self, number):
        slot = number % 2
        return pltpu.make_async_remote_copy(
            src_ref=self.send.at[slot],
            dst_ref=self.recv.at[slot],
            send_sem=self.send_sem.at[number],
            recv_sem=self.recv_sem.at[number],
            device_id=(self.me, 1 - self.head),
            device_id_type=MESH,
        )

    def start(self, number, value):
        self.send[number % 2] = as_bf(value)
        self.copy(number).start()

    def wait(self, number):
        self.copy(number).wait()

    def total(self, number, rows=slice(None)):
        slot = number % 2
        return as_f32(self.send[slot, rows]) + as_f32(self.recv[slot, rows])


def inverse_rms(values):
    return lax.rsqrt(jnp.mean(values * values, axis=-1, keepdims=True) + NORM_EPS)


def norm_back(values, gain, grad):
    inverse = inverse_rms(values)
    scaled = grad * gain
    inner = jnp.mean(scaled * values, axis=-1, keepdims=True)
    grad_values = inverse * scaled - values * (inverse * inverse * inverse * inner)
    grad_gain = jnp.sum(grad * values * inverse, axis=0, keepdims=True)
    return grad_values, grad_gain


def layer_kernel(
    tok, mem, cot, cbias, sbias, wall,
    out, tgrad, mgrad, dwall,
    ws, gains, dgains, n1, n2, n3, x1, x2, q3, k3, v3, o3, oT, qc3, oc3, ocT,
    kext, mv3, mT, exps, sexps, linv, slinv, st, acc, do3, dqc3, dT4, q4,
    esend, erecv, osend, orecv, msend, mrecv,
    send_sem, recv_sem, side_sem, wsem, msem,
):
    me, head = lax.axis_index("dp"), lax.axis_index("head")
    load = pltpu.make_async_copy(wall, ws, wsem.at[0])
    load.start()
    barrier = pltpu.get_barrier_semaphore()
    pl.semaphore_signal(barrier, inc=1, device_id=(me, 1 - head), device_id_type=MESH)
    pl.semaphore_wait(barrier, 1)
    load.wait()
    ex = Exchange(me, head, esend, erecv, send_sem, recv_sem)

    def w(column, width):
        return ws[:, pl.ds(column, width)]

    patches = mem.shape[0]
    lane = lax.broadcasted_iota(jnp.int32, (TXT, 128), 1)
    mask = [as_bf(jnp.where(lane < HD, 1.0, 0.0)), as_bf(jnp.where(lane < HD, 0.0, 1.0))]
    texts = [slice(0, TXT), slice(TXT, 2 * TXT)]
    pairs = 3

    gains[...] = as_f32(ws[:, 0:128]).T[0:8]
    dgains[...] = jnp.zeros_like(dgains)

    for rows in texts:
        x = as_f32(tok[rows])
        n1[rows] = as_bf(x * inverse_rms(x) * gains[0:1])
    for number, target in enumerate((q3, k3, v3)):
        value = as_bf(nn(n1[...], w(CQ + number * HALF, HALF)))
        if number == 0:
            value = value * jnp.asarray(HD**-0.5, BF)
        for j in range(pairs):
            target[j] = value[:, j * 128 : (j + 1) * 128]

    def softmax_parts(scores):
        top = jnp.max(scores, axis=0, keepdims=True)
        expo = jnp.exp(scores - top)
        return expo, jnp.sum(expo, axis=0, keepdims=True)

    def self_forward(j, carry):
        for t in range(2):
            query, key = q3[j, texts[t]], k3[j, texts[t]]
            turned = v3[j, texts[t]].T
            parts = []
            for a in range(2):
                scores = nt(key, query * mask[a]) + as_f32(sbias[t])
                expo, total = softmax_parts(scores)
                low = as_bf(expo)
                sexps[j, t, a] = low
                inverse = 1.0 / total
                slinv[j, t, a] = jnp.broadcast_to(inverse, (8, TXT))
                parts.append(nn(turned[a * HD : (a + 1) * HD], low) * inverse)
            both = jnp.concatenate(parts, axis=0)
            oT[j, t] = as_bf(both)
            o3[j, texts[t]] = as_bf(both.T)
        return carry

    lax.fori_loop(0, pairs, self_forward, 0)

    def joined(ref, rows=slice(None)):
        return jnp.concatenate([ref[j, rows] for j in range(pairs)], axis=1)

    ex.start(0, nt(joined(o3), w(COS, HALF)))

    def project(c, carry):
        rows = pl.ds(pl.multiple_of(c * 512, 512), 512)
        both = as_bf(nn(mem[rows], w(CKV, 2 * HALF)))
        for j in range(pairs):
            kext[j, rows, 0:128] = both[:, j * 128 : (j + 1) * 128]
            kext[j, rows, 128:256] = cbias[rows]
            mv3[j, rows] = both[:, HALF + j * 128 : HALF + (j + 1) * 128]
        return carry

    lax.fori_loop(0, patches // 512, project, 0)
    for j in range(pairs):
        mT[j] = mv3[j].T

    ex.wait(0)
    for rows in texts:
        value = as_f32(tok[rows]) + ex.total(0, rows)
        x1[rows] = value
        n2[rows] = as_bf(value * inverse_rms(value) * gains[1:2])
    value = as_bf(nn(n2[...], w(CQC, HALF))) * jnp.asarray(HD**-0.5, BF)
    for j in range(pairs):
        qc3[j] = value[:, j * 128 : (j + 1) * 128]

    def cross_forward(jt, carry):
        j, t = jt // 2, jt % 2
        rows = pl.ds(pl.multiple_of(t * TXT, TXT), TXT)
        query = qc3[j, rows]
        pick = as_bf(jnp.where(lane == t, 1.0, 0.0))
        parts = []
        for a in range(2):
            wide = jnp.concatenate([query * mask[a], pick], axis=1)
            top = jnp.full((8, TXT), -3e38, F32)
            for c in range(patches // 256):
                scores = nt(kext[j, c * 256 : (c + 1) * 256], wide)
                st[c * 256 : (c + 1) * 256] = scores
                top = jnp.maximum(top, jnp.max(scores.reshape(32, 8, TXT), axis=0))
            top = jnp.max(top, axis=0, keepdims=True)
            total = jnp.zeros((8, TXT), F32)
            for c in range(patches // 128):
                expo = jnp.exp(st[c * 128 : (c + 1) * 128] - top)
                total = total + jnp.sum(expo.reshape(16, 8, TXT), axis=0)
                exps[jt, a, c * 128 : (c + 1) * 128] = as_bf(expo)
            inverse = 1.0 / jnp.sum(total, axis=0, keepdims=True)
            linv[jt, a] = jnp.broadcast_to(inverse, (8, TXT))
            parts.append(nn(mT[j, a * HD : (a + 1) * HD], exps[jt, a]) * inverse)
        both = jnp.concatenate(parts, axis=0)
        ocT[jt] = as_bf(both)
        oc3[j, rows] = as_bf(both.T)
        return carry

    lax.fori_loop(0, 2 * pairs, cross_forward, 0)
    ex.start(1, nt(joined(oc3), w(COC, HALF)))
    for j in range(pairs):
        mT[j] = kext[j, :, 0:128].T
    ex.wait(1)
    for rows in texts:
        value = x1[rows] + ex.total(1, rows)
        x2[rows] = value
        n3[rows] = as_bf(value * inverse_rms(value) * gains[2:3])

    acc[...] = jnp.zeros_like(acc)
    tgrad[...] = jnp.zeros_like(tgrad)
    root = (2.0 / jnp.pi) ** 0.5

    def mlp(f, carry):
        base = pl.multiple_of(CM + f * (3 * FT), 128)
        gate_w, up_w, down_w = (ws[:, pl.ds(base + k * FT, FT)] for k in range(3))
        for rows in texts:
            gate, up = nn(n3[rows], gate_w), nn(n3[rows], up_w)
            grad = nn(cot[rows], down_w)
            square = gate * gate
            tanh = jnp.tanh(root * gate * (1.0 + 0.044715 * square))
            half = 0.5 * (1.0 + tanh)
            slope = half + 0.5 * gate * (1.0 - tanh * tanh) * (root * (1.0 + 3 * 0.044715 * square))
            active = gate * half
            osend[rows, 0:FT] = as_bf(active * up)
            osend[rows, FT : 2 * FT] = as_bf(grad * up * slope)
            osend[rows, 2 * FT : 3 * FT] = as_bf(grad * active)
        for rows in texts:
            acc[rows] += nt(osend[rows, 0:FT], down_w)
            tgrad[rows] += nt(osend[rows, FT : 2 * FT], gate_w) + nt(osend[rows, 2 * FT : 3 * FT], up_w)
        ws[:, pl.ds(base, FT)] = as_bf(tn(n3[...], osend[:, FT : 2 * FT]))
        ws[:, pl.ds(base + FT, FT)] = as_bf(tn(n3[...], osend[:, 2 * FT : 3 * FT]))
        ws[:, pl.ds(base + 2 * FT, FT)] = as_bf(tn(cot[...], osend[:, 0:FT]))
        return carry

    lax.fori_loop(0, FH // FT, mlp, 0)
    ex.start(2, tgrad[...])
    osend[...] = as_bf(acc[...])
    side = pltpu.make_async_remote_copy(
        src_ref=osend, dst_ref=orecv, send_sem=side_sem.at[0], recv_sem=side_sem.at[1],
        device_id=(me, 1 - head), device_id_type=MESH,
    )
    side.start()
    ex.wait(2)
    side.wait()
    for rows in texts:
        out[rows] = as_bf(x2[rows] + (as_f32(osend[rows]) + as_f32(orecv[rows])))
        grad, grad_gain = norm_back(x2[rows], gains[2:3], ex.total(2, rows))
        value = as_f32(cot[rows]) + grad
        x2[rows] = value
        dgains[2:3] += grad_gain
        back = as_bf(value)
        n3[rows] = back
        turned = as_bf(nn(back, w(COC, HALF)))
        for j in range(pairs):
            do3[j, rows] = turned[:, j * 128 : (j + 1) * 128]

    def split_grad(grad, attended, inverse, a):
        part = grad[a * HD : (a + 1) * HD] * inverse
        low = as_bf(part)
        inner = jnp.sum(as_f32(low) * attended[a * HD : (a + 1) * HD], axis=0, keepdims=True)
        empty = jnp.zeros_like(low)
        return jnp.concatenate([low, empty] if a == 0 else [empty, low], axis=0), inner

    def cross_back(j, carry):
        def one_text(t, inner_carry):
            jt = 2 * j + t
            rows = pl.ds(pl.multiple_of(t * TXT, TXT), TXT)
            grad = as_f32(do3[j, rows]).T
            attended = as_f32(ocT[jt])
            query = qc3[j, rows]
            parts = []
            for a in range(2):
                low, inner = split_grad(grad, attended, linv[jt, a, 0:1], a)
                dT4[2 * t + a] = low
                q4[2 * t + a] = query * mask[a]
            return inner_carry

        lax.fori_loop(0, 2, one_text, 0)
        turned = [dT4[i] for i in range(4)]
        for c in range(patches // 512):
            rows = slice(c * 512, (c + 1) * 512)
            total = nt(exps[2 * j, 0, rows], turned[0])
            for i in range(1, 4):
                total = total + nt(exps[2 * j + i // 2, i % 2, rows], turned[i])
            st[rows, 0:128] = total

        def back_text(t, inner_carry):
            jt = 2 * j + t
            rows = pl.ds(pl.multiple_of(t * TXT, TXT), TXT)
            attended = as_f32(ocT[jt])
            parts = []
            for a in range(2):
                low = dT4[2 * t + a]
                inner = jnp.sum(
                    as_f32(low[a * HD : (a + 1) * HD]) * attended[a * HD : (a + 1) * HD], axis=0, keepdims=True
                )
                for c in range(patches // 128):
                    keys = slice(c * 128, (c + 1) * 128)
                    grad_probs = nn(mv3[j, keys], low)
                    exps[jt, a, keys] = as_bf(as_f32(exps[jt, a, keys]) * (grad_probs - inner))
                parts.append(nn(mT[j, a * HD : (a + 1) * HD], exps[jt, a]))
            dqc3[j, rows] = as_bf((jnp.concatenate(parts, axis=0) * HD**-0.5).T)
            return inner_carry

        lax.fori_loop(0, 2, back_text, 0)
        queries = [q4[i] for i in range(4)]
        for c in range(patches // 512):
            rows = slice(c * 512, (c + 1) * 512)
            mv3[j, rows] = as_bf(st[rows, 0:128])
            total = nn(exps[2 * j, 0, rows], queries[0])
            for i in range(1, 4):
                total = total + nn(exps[2 * j + i // 2, i % 2, rows], queries[i])
            kext[j, rows, 0:128] = as_bf(total)
        return carry

    lax.fori_loop(0, pairs, cross_back, 0)
    ex.start(3, nt(joined(dqc3), w(CQC, HALF)))

    half_rows = patches // 2

    def memory_back(c, start):
        rows = pl.ds(pl.multiple_of(start + c * 256, 256), 256)
        both = jnp.concatenate(
            [kext[j, rows, 0:128] for j in range(pairs)] + [mv3[j, rows] for j in range(pairs)], axis=1
        )
        return nt(both, w(CKV, 2 * HALF))

    def send_part(c, carry):
        msend[pl.ds(pl.multiple_of(c * 256, 256), 256)] = as_bf(memory_back(c, (1 - head) * half_rows))
        return carry

    lax.fori_loop(0, half_rows // 256, send_part, 0)
    mside = pltpu.make_async_remote_copy(
        src_ref=msend, dst_ref=mrecv, send_sem=side_sem.at[2], recv_sem=side_sem.at[3],
        device_id=(me, 1 - head), device_id_type=MESH,
    )
    mside.start()
    ws[:, COC : COC + HALF] = as_bf(tn(n3[...], joined(oc3)))
    ws_query = as_bf(tn(n2[...], joined(dqc3)))
    mside.wait()
    stores = []
    for c in range(half_rows // 256):
        if c >= 2:
            stores[c - 2].wait()
        slot = slice((c % 2) * 256, (c % 2 + 1) * 256)
        acc[slot] = memory_back(c, head * half_rows) + as_f32(mrecv[c * 256 : (c + 1) * 256])
        store = pltpu.make_async_copy(acc.at[slot], mgrad.at[pl.ds(c * 256, 256)], msem.at[c])
        store.start()
        stores.append(store)
    for number in range(2):
        total = jnp.zeros((D, HALF), F32)
        source = kext if number == 0 else mv3
        for c in range(patches // 512):
            rows = slice(c * 512, (c + 1) * 512)
            both = jnp.concatenate([source[j, rows, 0:128] for j in range(pairs)], axis=1)
            total = total + tn(mem[rows], both)
        ws[:, CKV + number * HALF : CKV + (number + 1) * HALF] = as_bf(total)
    ex.wait(3)
    ws[:, CQC : CQC + HALF] = ws_query
    for rows in texts:
        grad, grad_gain = norm_back(x1[rows], gains[1:2], ex.total(3, rows))
        value = x2[rows] + grad
        x1[rows] = value
        dgains[1:2] += grad_gain
        back = as_bf(value)
        n3[rows] = back
        turned = as_bf(nn(back, w(COS, HALF)))
        for j in range(pairs):
            do3[j, rows] = turned[:, j * 128 : (j + 1) * 128]

    def self_back(j, carry):
        for t in range(2):
            rows = texts[t]
            grad = as_f32(do3[j, rows]).T
            attended = as_f32(oT[j, t])
            query, key, value = q3[j, rows], k3[j, rows], v3[j, rows]
            key_turned = key.T
            parts = []
            grad_key = jnp.zeros((TXT, 128), F32)
            grad_value = jnp.zeros((TXT, 128), F32)
            for a in range(2):
                low, inner = split_grad(grad, attended, slinv[j, t, a, 0:1], a)
                expo = sexps[j, t, a]
                grad_scores = as_bf(as_f32(expo) * (nn(value, low) - inner))
                grad_value = grad_value + nt(expo, low)
                grad_key = grad_key + nn(grad_scores, query * mask[a])
                parts.append(nn(key_turned[a * HD : (a + 1) * HD], grad_scores))
            q3[j, rows] = as_bf((jnp.concatenate(parts, axis=0) * HD**-0.5).T)
            k3[j, rows] = as_bf(grad_key)
            v3[j, rows] = as_bf(grad_value)
        return carry

    lax.fori_loop(0, pairs, self_back, 0)
    ex.start(
        4,
        nt(joined(q3), w(CQ, HALF)) + nt(joined(k3), w(CQ + HALF, HALF)) + nt(joined(v3), w(CQ + 2 * HALF, HALF)),
    )
    ws[:, COS : COS + HALF] = as_bf(tn(n3[...], joined(o3)))
    for number, source in enumerate((q3, k3, v3)):
        column = CQ + number * HALF
        ws[:, column : column + HALF] = as_bf(tn(n1[...], joined(source)))
    ex.wait(4)
    for rows in texts:
        grad, grad_gain = norm_back(as_f32(tok[rows]), gains[0:1], ex.total(4, rows))
        tgrad[rows] = x1[rows] + grad
        dgains[0:1] += grad_gain
    ws[:, 0:128] = as_bf(dgains[...].T)
    store = pltpu.make_async_copy(ws, dwall, wsem.at[1])
    store.start()
    for number in (-2, -1):
        stores[number].wait()
    store.wait()


def layer(tokens, memory, cotangent, cbias, sbias, wall):
    rows, patches = tokens.shape[0], memory.shape[0]
    vm = pl.BlockSpec(memory_space=pltpu.VMEM)
    anywhere = pl.BlockSpec(memory_space=pl.ANY)
    S = pltpu.VMEM
    scratch = [
        S((D, PACK), BF), S((8, D), F32), S((128, D), F32),
        S((rows, D), BF), S((rows, D), BF), S((rows, D), BF),
        S((rows, D), F32), S((rows, D), F32),
        S((3, rows, 128), BF), S((3, rows, 128), BF), S((3, rows, 128), BF), S((3, rows, 128), BF),
        S((3, 2, 128, TXT), BF), S((3, rows, 128), BF), S((3, rows, 128), BF), S((6, 128, TXT), BF),
        S((3, patches, 256), BF), S((3, patches, 128), BF), S((3, 128, patches), BF),
        S((6, 2, patches, TXT), BF), S((3, 2, 2, TXT, TXT), BF),
        S((6, 2, 8, TXT), F32), S((3, 2, 2, 8, TXT), F32),
        S((patches, TXT), F32),
        S((rows, D), F32),
        S((3, rows, 128), BF), S((3, rows, 128), BF), S((4, 128, TXT), BF), S((4, TXT, 128), BF),
        S((2, rows, D), BF), S((2, rows, D), BF), S((rows, D), BF), S((rows, D), BF),
        S((patches // 2, D), BF), S((patches // 2, D), BF),
        pltpu.SemaphoreType.DMA((5,)), pltpu.SemaphoreType.DMA((5,)), pltpu.SemaphoreType.DMA((4,)),
        pltpu.SemaphoreType.DMA((2,)), pltpu.SemaphoreType.DMA((patches // 512,)),
    ]
    return pl.pallas_call(
        layer_kernel,
        out_shape=(
            jax.ShapeDtypeStruct((rows, D), BF),
            jax.ShapeDtypeStruct((rows, D), F32),
            jax.ShapeDtypeStruct((patches // 2, D), F32),
            jax.ShapeDtypeStruct((D, PACK), BF),
        ),
        in_specs=[vm] * 5 + [anywhere],
        out_specs=(vm, vm, anywhere, anywhere),
        scratch_shapes=scratch,
        name="layer",
        compiler_params=pltpu.CompilerParams(
            collective_id=2, has_side_effects=True, vmem_limit_bytes=VMEM_BYTES
        ),
    )(tokens, memory, cotangent, cbias, sbias, wall)


class Scatter:
    def __init__(self, bits, me, head, wall, slots, send_sem, recv_sem):
        self.bits, self.me, self.head = bits, me, head
        self.wall, self.slots = wall, slots
        self.send_sem, self.recv_sem = send_sem, recv_sem
        self.jobs = [(low, high, order[::-1]) for low, high, order in gather_jobs(bits)]

    def copy(self, number, phase):
        low, high, order = self.jobs[number]
        bit = order[phase]
        index = block_index(self.bits, self.me, order[phase + 1 :], {bit: 1 - ((self.me >> bit) & 1)})
        columns = (slice(None), slice(low, high))
        left = self.bits - 1 - phase
        return pltpu.make_async_remote_copy(
            src_ref=self.wall.at[index + columns],
            dst_ref=self.slots[phase].at[(slice(None),) * left + columns],
            send_sem=self.send_sem.at[number, phase],
            recv_sem=self.recv_sem.at[number, phase],
            device_id=(self.me ^ (1 << bit), self.head),
            device_id_type=MESH,
        )

    def start(self, number, phase):
        self.copy(number, phase).start()

    def add(self, number, phase, final=None):
        self.copy(number, phase).wait_recv()
        low, high, order = self.jobs[number]
        left = [bit for bit in reversed(range(self.bits)) if bit in order[phase + 1 :]]
        for block in range(1 << len(left)):
            fixed = {bit: (block >> (len(left) - 1 - place)) & 1 for place, bit in enumerate(left)}
            here = block_index(self.bits, self.me, (), fixed) + (slice(None), slice(low, high))
            there = tuple(fixed[bit] for bit in left) + (slice(None), slice(low, high))
            if final is None:
                self.wall[here] = self.wall[here] + self.slots[phase][there]
            else:
                final[:, low:high] = as_f32(self.wall[here]) + as_f32(self.slots[phase][there])

    def finish(self):
        for number in range(len(self.jobs)):
            for phase in range(self.bits):
                self.copy(number, phase).wait_send()


def scatter_kernel(bits, dwall, red, total, *rest):
    ws, slots = rest[0], rest[1 : 1 + bits]
    sums, others, send_sem, recv_sem, local_sem, sum_send, sum_recv = rest[1 + bits :]
    me, head = lax.axis_index("dp"), lax.axis_index("head")
    load = pltpu.make_async_copy(dwall, ws, local_sem.at[0])
    load.start()
    greet(me, head, bits)
    load.wait()
    scatter = Scatter(bits, me, head, ws, slots, send_sem, recv_sem)
    groups = len(scatter.jobs) // 2
    for turn in range(groups + bits):
        for place in range(groups):
            group = groups - 1 - place
            phase = turn - place
            for number in (2 * group, 2 * group + 1):
                if 1 <= phase <= bits:
                    scatter.add(number, phase - 1, red if phase == bits else None)
                if 0 <= phase < bits:
                    scatter.start(number, phase)
    first = red[:, 0:128]
    first = jnp.sum(first * first, axis=0, keepdims=True)
    value = jnp.where(head == 0, first, jnp.zeros_like(first))
    for column in range(128, PACK, 128):
        part = red[:, column : column + 128]
        value = value + jnp.sum(part * part, axis=0, keepdims=True)
    value = jnp.broadcast_to(jnp.sum(value, axis=1, keepdims=True), (8, 128))
    for step in range(bits + 1):
        sums[step] = value
        peer = (me, 1 - head) if step == bits else (me ^ (1 << step), head)
        copy = pltpu.make_async_remote_copy(
            src_ref=sums.at[step], dst_ref=others.at[step], send_sem=sum_send.at[step], recv_sem=sum_recv.at[step],
            device_id=peer, device_id_type=MESH,
        )
        copy.start()
        copy.wait()
        value = value + others[step]
    total[...] = value
    scatter.finish()


def scatter_grads(dwall, count):
    bits = bit_count(count)
    rows = D // count
    jobs = len(gather_jobs(bits))
    S = pltpu.VMEM
    vm = pl.BlockSpec(memory_space=pltpu.VMEM)
    red, total = pl.pallas_call(
        functools.partial(scatter_kernel, bits),
        out_shape=(
            jax.ShapeDtypeStruct((rows, PACK), F32),
            jax.ShapeDtypeStruct((8, 128), F32),
        ),
        in_specs=[pl.BlockSpec(memory_space=pl.ANY)],
        out_specs=(vm, vm),
        scratch_shapes=[S((2,) * bits + (rows, PACK), BF)]
        + [S((2,) * (bits - 1 - phase) + (rows, PACK), BF) for phase in range(bits)]
        + [
            S((bits + 1, 8, 128), F32), S((bits + 1, 8, 128), F32),
            pltpu.SemaphoreType.DMA((jobs, bits)), pltpu.SemaphoreType.DMA((jobs, bits)),
            pltpu.SemaphoreType.DMA((1,)),
            pltpu.SemaphoreType.DMA((bits + 1,)), pltpu.SemaphoreType.DMA((bits + 1,)),
        ],
        name="scatter",
        compiler_params=pltpu.CompilerParams(
            collective_id=3, has_side_effects=True, vmem_limit_bytes=VMEM_BYTES
        ),
    )(dwall.reshape((2,) * bits + (rows, PACK)))
    return red, total[0, 0]


def adam_step(weight, first, second, grad, rate, decay):
    first_new = BETA1 * first + (1.0 - BETA1) * grad
    second_new = BETA2 * second + (1.0 - BETA2) * grad * grad
    mean_hat = first_new / (1.0 - BETA1**STEP)
    square_hat = second_new / (1.0 - BETA2**STEP)
    weight_new = weight - rate * (mean_hat / (jnp.sqrt(square_hat) + ADAM_EPS) + decay * weight)
    return (weight_new, first_new, second_new)


def pack_weights(gains, self_proj, query, keyval, out_proj, mlp_input, mlp_output):
    rows = gains.shape[1]
    turned_out = jnp.swapaxes(out_proj, 1, 2)
    turned_down = mlp_output.T
    pieces = [jnp.pad(gains.T, ((0, 0), (0, 125)))]
    pieces += [self_proj[0], self_proj[1], self_proj[2], keyval[0], keyval[1]]
    pieces += [turned_out[0], query, turned_out[1]]
    for tile in range(FH // FT):
        columns = slice(tile * FT, (tile + 1) * FT)
        pieces += [mlp_input[0][:, columns], mlp_input[1][:, columns], turned_down[:, columns]]
    return jnp.concatenate([piece.astype(BF) for piece in pieces], axis=1)


def unpack_grads(red):
    def cut(start, width):
        return red[:, start : start + width]

    gains = cut(GAIN, 3).T
    self_proj = jnp.stack([cut(CQ + i * HALF, HALF) for i in range(3)])
    keyval = jnp.stack([cut(CKV + i * HALF, HALF) for i in range(2)])
    query = cut(CQC, HALF)
    out_proj = jnp.stack([cut(COS, HALF).T, cut(COC, HALF).T])
    tiles = FH // FT
    mlp = [jnp.concatenate([cut(CM + (3 * tile + k) * FT, FT) for tile in range(tiles)], axis=1) for k in range(3)]
    return gains, self_proj, query, keyval, out_proj, jnp.stack(mlp[:2]), mlp[2].T


def per_device(
    tokens, memory, cotangent, patch_item, patch_mask, text_item, text_len,
    norm_gains, gains_mean, gains_square,
    self_proj, self_proj_mean, self_proj_square,
    query_cross, query_cross_mean, query_cross_square,
    keyval_cross, keyval_cross_mean, keyval_cross_square,
    out_proj, out_proj_mean, out_proj_square,
    mlp_input, mlp_input_mean, mlp_input_square,
    mlp_output, mlp_output_mean, mlp_output_square,
):
    count = lax.axis_size("dp")
    rows = D // count
    direct = rows % 16 == 0 and count & (count - 1) == 0
    keyval_own = lax.all_to_all(keyval_cross.astype(BF), "head", split_axis=2, concat_axis=1, tiled=True)
    pack = pack_weights(norm_gains, self_proj, query_cross, keyval_own, out_proj, mlp_input, mlp_output)
    if direct:
        wall, memall = gather_weights(pack, memory, count)
    else:
        wall = lax.all_gather(pack, "dp", axis=0, tiled=True)
        memall = lax.all_gather(memory, "head", axis=0, tiled=True)
    seen = (text_item[None, :] == patch_item[:, None]) & (patch_mask[:, None] == 1)
    cbias = jnp.pad(jnp.where(seen, 0.0, MASKED), ((0, 0), (0, 126))).astype(BF)
    place = jnp.arange(TXT, dtype=jnp.int32)
    allowed = (place[None, :, None] <= place[None, None, :]) & (place[None, :, None] < text_len[:, None, None])
    sbias = jnp.where(allowed, 0.0, MASKED).astype(BF)
    output, tokens_grad, memory_grad, dwall = layer(tokens, memall, cotangent, cbias, sbias, wall)
    if direct:
        red, total = scatter_grads(dwall, count)
    else:
        red = lax.psum_scatter(dwall.astype(F32), "dp", scatter_dimension=0, tiled=True)
        squares = jnp.sum(red[:, 128:] ** 2)
        squares = squares + jnp.where(lax.axis_index("head") == 0, jnp.sum(red[:, :128] ** 2), 0.0)
        total = lax.psum(squares, ("dp", "head"))
    gains_g, self_g, query_g, keyval_g, out_g, input_g, output_g = unpack_grads(red)
    keyval_g = lax.all_to_all(keyval_g, "head", split_axis=1, concat_axis=2, tiled=True)
    grad_norm = jnp.sqrt(total)
    factor = jnp.minimum(1.0, CLIP / (grad_norm + NORM_EPS))
    wide_rate = 2.0 * D ** (-0.5)
    results = [output, tokens_grad, memory_grad, grad_norm]
    for weight, first, second, grad, rate, decay in (
        (norm_gains, gains_mean, gains_square, gains_g, 0.5, 0.0),
        (self_proj, self_proj_mean, self_proj_square, self_g, wide_rate, DECAY),
        (query_cross, query_cross_mean, query_cross_square, query_g, wide_rate, DECAY),
        (keyval_cross, keyval_cross_mean, keyval_cross_square, keyval_g, wide_rate, DECAY),
        (out_proj, out_proj_mean, out_proj_square, out_g, 2.0 * (D // 16) ** (-0.5), DECAY),
        (mlp_input, mlp_input_mean, mlp_input_square, input_g, wide_rate, DECAY),
        (mlp_output, mlp_output_mean, mlp_output_square, output_g, 2.0 * FF ** (-0.5), DECAY),
    ):
        results += adam_step(weight, first, second, grad * factor, rate, decay)
    return tuple(results)


def solution(mesh):
    in_specs = (
        P("dp", None),
        P(("dp", "head"), None),
        P("dp", None),
        P("dp"),
        P("dp"),
        P("dp"),
        P("dp"),
        P(None, "dp"),
        P(None, "dp"),
        P(None, "dp"),
        P(None, "dp", "head"),
        P(None, "dp", "head"),
        P(None, "dp", "head"),
        P("dp", "head"),
        P("dp", "head"),
        P("dp", "head"),
        P(None, ("dp", "head"), None),
        P(None, ("dp", "head"), None),
        P(None, ("dp", "head"), None),
        P(None, "head", "dp"),
        P(None, "head", "dp"),
        P(None, "head", "dp"),
        P(None, "dp", "head"),
        P(None, "dp", "head"),
        P(None, "dp", "head"),
        P("head", "dp"),
        P("head", "dp"),
        P("head", "dp"),
    )
    out_specs = (
        P("dp", None),
        P("dp", None),
        P(("dp", "head"), None),
        P(),
        P(None, "dp"),
        P(None, "dp"),
        P(None, "dp"),
        P(None, "dp", "head"),
        P(None, "dp", "head"),
        P(None, "dp", "head"),
        P("dp", "head"),
        P("dp", "head"),
        P("dp", "head"),
        P(None, ("dp", "head"), None),
        P(None, ("dp", "head"), None),
        P(None, ("dp", "head"), None),
        P(None, "head", "dp"),
        P(None, "head", "dp"),
        P(None, "head", "dp"),
        P(None, "dp", "head"),
        P(None, "dp", "head"),
        P(None, "dp", "head"),
        P("head", "dp"),
        P("head", "dp"),
        P("head", "dp"),
    )
    return jax.shard_map(
        per_device, mesh=mesh, in_specs=in_specs, out_specs=out_specs, check_vma=False
    )
```

```python
import functools

import jax
import jax.numpy as jnp
from jax import lax
from jax.experimental import pallas as pl
from jax.experimental.pallas import tpu as pltpu
from jax.sharding import PartitionSpec as P

D = 768
HD = 64
FF = 2048
TXT = 256
STEP = 10

BETA1 = 0.9
BETA2 = 0.95
ADAM_EPS = 1e-08
DECAY = 0.1
CLIP = 1.0
NORM_EPS = 1e-06
MASKED = -1e30

MESH = pl.DeviceIdType.MESH
BF = jnp.bfloat16
F32 = jnp.float32
VMEM_BYTES = 63 * 2**20

HALF = D // 2
FT = 256
FH = FF // 2
GAIN = 0
CQ = 128
CKV = CQ + 3 * HALF
COS = CKV + 2 * HALF
CQC = COS + HALF
COC = CQC + HALF
CM = COC + HALF
PACK = CM + 3 * FH


def as_bf(value):
    return value.astype(BF)


def as_f32(value):
    return value.astype(F32)


def nn(left, right):
    return lax.dot_general(left, right, (((1,), (0,)), ((), ())), preferred_element_type=F32)


def nt(left, right):
    return lax.dot_general(left, right, (((1,), (1,)), ((), ())), preferred_element_type=F32)


def tn(left, right):
    return lax.dot_general(left, right, (((0,), (0,)), ((), ())), preferred_element_type=F32)


ZN, YN, XN = 4, 2, 2
BLOCK = D // (ZN * YN * XN)


def middle(low, high):
    return low + (high - low) // 256 * 128 if high - low >= 256 else high


class Links:
    def __init__(self):
        self.me, self.head = lax.axis_index("dp"), lax.axis_index("head")
        self.x, self.y, self.z = self.me & 1, (self.me >> 1) & 1, self.me >> 2

    def device(self, z, y, x):
        return ((z * YN + y) * XN + x, self.head)

    def peers(self):
        z, y, x = self.z, self.y, self.x
        return [self.device((z + k) & 3, y, x) for k in (1, 2, 3)] + [
            self.device(z, y, 1 - x),
            self.device(z, 1 - y, x),
            (self.me, 1 - self.head),
        ]


def remote(source, target, send, recv, device):
    return pltpu.make_async_remote_copy(
        src_ref=source, dst_ref=target, send_sem=send, recv_sem=recv, device_id=device, device_id_type=MESH
    )


GATHER = ((0, CKV), (CKV, COS), (COS, CM)) + tuple(
    (CM + f * 3 * FT, CM + (f + 1) * 3 * FT) for f in range(FH // FT)
)
LAST = len(GATHER) - 1


class Gather:
    def __init__(self, links, wall, send_sem, recv_sem):
        self.links, self.wall, self.send_sem, self.recv_sem = links, wall, send_sem, recv_sem

    def at(self, z, y, x, low, high):
        return self.wall.at[z, y, x, :, low:high]

    def send(self, n, k):
        low, high = GATHER[n]
        half = middle(low, high)
        z, y, x = self.links.z, self.links.y, self.links.x
        every = slice(None)
        to_x, to_y = self.links.device(z, y, 1 - x), self.links.device(z, 1 - y, x)
        if n == LAST:
            if k < 2:
                ref, device = self.at(z, y, x, low, high), (to_x, to_y)[k]
            elif k == 2:
                ref, device = self.at(z, y, 1 - x, low, half), to_y
            elif k == 3:
                ref, device = self.at(z, 1 - y, x, half, high), to_x
            else:
                ref, device = self.at(z, every, every, low, high), self.links.device((z + k - 3) & 3, y, x)
        elif k < 3:
            ref, device = self.at(z, y, x, low, high), self.links.device((z + k + 1) & 3, y, x)
        elif k < 5:
            ref, device = self.at(every, y, x, low, high), (to_x, to_y)[k - 3]
        elif k == 5:
            ref, device = self.at(every, y, 1 - x, low, half), to_y
        else:
            ref, device = self.at(every, 1 - y, x, half, high), to_x
        return remote(ref, ref, self.send_sem.at[n, k], self.recv_sem.at[n, k], device)

    def wait(self, n, k):
        low, high = GATHER[n]
        half = middle(low, high)
        z, y, x = self.links.z, self.links.y, self.links.x
        every = slice(None)
        if n == LAST:
            if k == 0:
                ref = self.at(z, y, 1 - x, low, high)
            elif k == 1:
                ref = self.at(z, 1 - y, x, low, high)
            elif k == 2:
                ref = self.at(z, 1 - y, 1 - x, low, half)
            elif k == 3:
                ref = self.at(z, 1 - y, 1 - x, half, high)
            else:
                ref = self.at((z - k + 3) & 3, every, every, low, high)
        elif k < 3:
            ref = self.at((z - k - 1) & 3, y, x, low, high)
        elif k == 3:
            ref = self.at(every, y, 1 - x, low, high)
        elif k == 4:
            ref = self.at(every, 1 - y, x, low, high)
        elif k == 5:
            ref = self.at(every, 1 - y, 1 - x, low, half)
        else:
            ref = self.at(every, 1 - y, 1 - x, half, high)
        remote(ref, ref, self.send_sem.at[n, k], self.recv_sem.at[n, k], (self.links.me, self.links.head)).wait_recv()

    def step(self, n, number):
        if n == LAST:
            waits = ((), (0, 1), (2, 3), (4, 5, 6))[number]
            starts = ((0, 1), (2, 3), (4, 5, 6), ())[number]
        else:
            waits = ((), (0, 1, 2), (3, 4), (5, 6))[number]
            starts = ((0, 1, 2), (3, 4), (5, 6), ())[number]
        for k in waits:
            self.wait(n, k)
        for k in starts:
            self.send(n, k).start()

    def sent(self, n):
        for k in range(7):
            self.send(n, k).wait_send()


SCATTER = GATHER[3:] + (
    (COC, COC + HALF),
    (CKV, COS),
    (CQC, CQC + HALF),
    (COS, COS + HALF),
    (CQ, CKV),
    (GAIN, CQ),
)


class Scatter:
    def __init__(self, links, wall, slot1, slot2, slot3, red, send_sem, recv_sem):
        self.links, self.wall, self.red = links, wall, red
        self.slot1, self.slot2, self.slot3 = slot1, slot2, slot3
        self.send_sem, self.recv_sem = send_sem, recv_sem

    def parts(self, n):
        low, high = SCATTER[n]
        return (0, 2, 3, 4, 5, 6) if middle(low, high) == high else range(7)

    def copy(self, n, k):
        low, high = SCATTER[n]
        half = middle(low, high)
        z, y, x = self.links.z, self.links.y, self.links.x
        every = slice(None)
        to_x, to_y = self.links.device(z, y, 1 - x), self.links.device(z, 1 - y, x)
        if k == 0:
            source, target = self.wall.at[:, 1 - y, 1 - x, :, low:half], self.slot1.at[:, :, low:half]
        elif k == 1:
            source, target = self.wall.at[:, 1 - y, 1 - x, :, half:high], self.slot1.at[:, :, half:high]
        elif k == 2:
            source, target = self.wall.at[:, y, 1 - x, :, low:high], self.slot2.at[0, :, :, low:high]
        elif k == 3:
            source, target = self.wall.at[:, 1 - y, x, :, low:high], self.slot2.at[1, :, :, low:high]
        else:
            there = (z + k - 3) & 3
            source, target = self.wall.at[there, y, x, :, low:high], self.slot3.at[k - 4, :, low:high]
            return remote(
                source, target, self.send_sem.at[n, k], self.recv_sem.at[n, k], self.links.device(there, y, x)
            )
        return remote(source, target, self.send_sem.at[n, k], self.recv_sem.at[n, k], (to_y, to_x, to_x, to_y)[k])

    def step(self, n, number):
        low, high = SCATTER[n]
        half = middle(low, high)
        z, y, x = self.links.z, self.links.y, self.links.x
        parts = self.parts(n)
        waits = [k for k in ((), (0, 1), (2, 3), (4, 5, 6))[number] if k in parts]
        starts = [k for k in ((0, 1), (2, 3), (4, 5, 6), ())[number] if k in parts]
        for k in waits:
            self.copy(n, k).wait_recv()
        wall, cols, left, right = self.wall, slice(low, high), slice(low, half), slice(half, high)
        if number == 1:
            for b in range(ZN):
                wall[b, y, 1 - x, :, left] = wall[b, y, 1 - x, :, left] + self.slot1[b, :, left]
                if half < high:
                    wall[b, 1 - y, x, :, right] = wall[b, 1 - y, x, :, right] + self.slot1[b, :, right]
        elif number == 2:
            for b in range(ZN):
                wall[b, y, x, :, cols] = as_bf(
                    as_f32(wall[b, y, x, :, cols])
                    + as_f32(self.slot2[0, b, :, cols])
                    + as_f32(self.slot2[1, b, :, cols])
                )
        elif number == 3:
            value = as_f32(wall[z, y, x, :, cols])
            for k in range(3):
                value = value + as_f32(self.slot3[k, :, cols])
            self.red[:, cols] = value
        for k in starts:
            self.copy(n, k).start()

    def sent(self):
        for n in range(len(SCATTER)):
            for k in self.parts(n):
                self.copy(n, k).wait_send()


class Exchange:
    def __init__(self, links, send, recv, send_sem, recv_sem):
        self.links = links
        self.send, self.recv, self.send_sem, self.recv_sem = send, recv, send_sem, recv_sem

    def copy(self, number):
        slot = number % 2
        return remote(
            self.send.at[slot],
            self.recv.at[slot],
            self.send_sem.at[number],
            self.recv_sem.at[number],
            (self.links.me, 1 - self.links.head),
        )

    def start(self, number, value):
        self.send[number % 2] = as_bf(value)
        self.copy(number).start()

    def wait(self, number):
        self.copy(number).wait()

    def total(self, number, rows=slice(None)):
        slot = number % 2
        return as_f32(self.send[slot, rows]) + as_f32(self.recv[slot, rows])


def inverse_rms(values):
    return lax.rsqrt(jnp.mean(values * values, axis=-1, keepdims=True) + NORM_EPS)


def norm_back(values, gain, grad):
    inverse = inverse_rms(values)
    scaled = grad * gain
    inner = jnp.mean(scaled * values, axis=-1, keepdims=True)
    grad_values = inverse * scaled - values * (inverse * inverse * inverse * inner)
    grad_gain = jnp.sum(grad * values * inverse, axis=0, keepdims=True)
    return grad_values, grad_gain


def layer_kernel(direct, *refs):
    (tok, cot, item, pmask, titem, tlen, memory), refs = refs[:7], refs[7:]
    if direct:
        (gpad, sproj, query, keyval, tout, minput, tdown), refs = refs[:7], refs[7:]
        (out, tgrad, mgrad, red, norm), refs = refs[:5], refs[5:]
    else:
        (wall,), refs = refs[:1], refs[1:]
        (out, tgrad, mgrad, dwall), refs = refs[:4], refs[4:]
    (
        ws, mem, gains, dgains, cbias, sbias, n1, n2, n3, x1, x2,
        q3, k3, v3, o3, oT, qc3, oc3, ocT, do3, dqc3, sexps, slinv,
        kext, mv3, mT, st, eb, clse, acc,
        esend, erecv, osend, orecv, mrecv,
        send_sem, recv_sem, side_sem, wsem, msem,
    ), refs = refs[:40], refs[40:]
    links = Links()
    me, head = links.me, links.head
    other = (me, 1 - head)

    barrier = pltpu.get_barrier_semaphore()
    peers = links.peers() if direct else [other]
    for device in peers:
        pl.semaphore_signal(barrier, inc=1, device_id=device, device_id_type=MESH)
    own_memory = pltpu.make_async_copy(memory, mem.at[head], wsem.at[0])
    own_memory.start()
    if direct:
        slot1, slot2, slot3, kvs, kvr, sums, others, g_send, g_recv, s_send, s_recv, t_send, t_recv = refs
        gather = Gather(links, ws, g_send, g_recv)
        scatter = Scatter(links, ws, slot1, slot2, slot3, red, s_send, s_recv)

        def own(column, value):
            ws[links.z, links.y, links.x, :, column : column + value.shape[1]] = as_bf(value)

        own(GAIN, gpad[...])
        for i in range(3):
            own(CQ + i * HALF, sproj[i])
        for f in range(FH // FT):
            base = CM + f * 3 * FT
            for k in range(2):
                own(base + k * FT, minput[k, :, f * FT : (f + 1) * FT])
            own(base + 2 * FT, tdown[:, f * FT : (f + 1) * FT])
        for k in range(2):
            kvs[k] = jnp.where(head == 0, keyval[k, :, HALF:], keyval[k, :, :HALF])
    pl.semaphore_wait(barrier, len(peers))
    if direct:
        kv_copy = remote(kvs, kvr, side_sem.at[4], side_sem.at[5], other)
        kv_copy.start()
    mem_copy = remote(memory, mem.at[head], side_sem.at[0], side_sem.at[1], other)
    if direct:
        gather.step(LAST, 0)
        gather.step(0, 0)
        mem_copy.start()
        own(COS, tout[0])
        own(CQC, query[...])
        own(COC, tout[1])
        kv_copy.wait()
        for k in range(2):
            mine = jnp.where(head == 0, keyval[k, :, :HALF], keyval[k, :, HALF:])
            top, bottom = jnp.where(head == 0, mine, kvr[k]), jnp.where(head == 0, kvr[k], mine)
            own(CKV + k * HALF, jnp.concatenate([top, bottom], axis=0))
        gather.step(1, 0)
        gather.step(LAST, 1)
    else:
        load = pltpu.make_async_copy(wall, ws, wsem.at[1])
        load.start()
        mem_copy.start()
        load.wait()

    def flow(*steps):
        if direct:
            for part, n, number in steps:
                (gather if part == "g" else scatter).step(n, number)

    ex = Exchange(links, esend, erecv, send_sem, recv_sem)

    def w(column, width):
        return ws[:, :, :, :, column : column + width].reshape(D, width)

    def put(column, value):
        width = value.shape[1]
        ws[:, :, :, :, column : column + width] = as_bf(value).reshape(ZN, YN, XN, BLOCK, width)

    half_rows = mem.shape[1]
    patches = 2 * half_rows
    lane = lax.broadcasted_iota(jnp.int32, (TXT, 128), 1)
    mask = [as_bf(jnp.where(lane < HD, 1.0, 0.0)), as_bf(jnp.where(lane < HD, 0.0, 1.0))]
    texts = [slice(0, TXT), slice(TXT, 2 * TXT)]
    pairs = 3

    def scope(name):
        return jax.named_scope(name)

    with scope("masks"):
        row = lax.broadcasted_iota(jnp.int32, (128, 512), 0)
        for c in range(patches // 512):
            cols = slice(c * 512, (c + 1) * 512)
            place = jnp.where(row == 0, titem[0], jnp.where(row == 1, titem[1], -1))
            seen = (place == item[:, cols]) & (pmask[:, cols] == 1)
            cbias[cols] = as_bf(jnp.where(seen, 0.0, jnp.where(row < 2, MASKED, 0.0)).T)
        key = lax.broadcasted_iota(jnp.int32, (TXT, TXT), 0)
        slot = lax.broadcasted_iota(jnp.int32, (TXT, TXT), 1)
        for t in range(2):
            sbias[t] = as_bf(jnp.where((key <= slot) & (key < tlen[t]), 0.0, MASKED))
        dgains[...] = jnp.zeros_like(dgains)

    with scope("gather_self"):
        flow(("g", 0, 1), ("g", 2, 0), ("g", 1, 1), ("g", 3, 0), ("g", 0, 2), ("g", 2, 1), ("g", 4, 0),
             ("g", LAST, 2), ("g", 1, 2), ("g", 0, 3))

    with scope("self_project"):
        gains[...] = as_f32(w(0, 128)).T[0:8]
        for rows in texts:
            x = as_f32(tok[rows])
            n1[rows] = as_bf(x * inverse_rms(x) * gains[0:1])
        for number, target in enumerate((q3, k3, v3)):
            value = as_bf(nn(n1[...], w(CQ + number * HALF, HALF)))
            if number == 0:
                value = value * jnp.asarray(HD**-0.5, BF)
            for j in range(pairs):
                target[j] = value[:, j * 128 : (j + 1) * 128]

    with scope("flow_a"):
        flow(("g", 3, 1), ("g", 5, 0))

    def self_forward(j, carry):
        for t in range(2):
            query_pair, key_pair = q3[j, texts[t]], k3[j, texts[t]]
            turned = v3[j, texts[t]].T
            parts = []
            for a in range(2):
                scores = nt(key_pair, query_pair * mask[a]) + as_f32(sbias[t])
                top = jnp.max(scores, axis=0, keepdims=True)
                expo = jnp.exp(scores - top)
                low = as_bf(expo)
                sexps[j, t, a] = low
                inverse = 1.0 / jnp.sum(expo, axis=0, keepdims=True)
                slinv[j, t, a] = jnp.broadcast_to(inverse, (8, TXT))
                parts.append(nn(turned[a * HD : (a + 1) * HD], low) * inverse)
            both = jnp.concatenate(parts, axis=0)
            oT[j, t] = as_bf(both)
            o3[j, texts[t]] = as_bf(both.T)
        return carry

    with scope("self_attention"):
        lax.fori_loop(0, pairs, self_forward, 0)

    with scope("flow_b"):
        flow(("g", 2, 2), ("g", 1, 3))

    def joined(ref, rows=slice(None)):
        return jnp.concatenate([ref[j, rows] for j in range(pairs)], axis=1)

    with scope("memory_project"):
        own_memory.wait()
        mem_copy.wait_send()
        remote(memory, mem.at[1 - head], side_sem.at[0], side_sem.at[1], other).wait_recv()

        def project(c, carry):
            for side in range(2):
                part = pl.ds(pl.multiple_of(c * 512, 512), 512)
                rows = pl.ds(pl.multiple_of(side * half_rows + c * 512, 512), 512)
                both = as_bf(nn(mem[side, part], w(CKV, 2 * HALF)))
                for j in range(pairs):
                    kext[j, rows, 0:128] = both[:, j * 128 : (j + 1) * 128]
                    kext[j, rows, 128:256] = cbias[rows]
                    mv3[j, rows] = both[:, HALF + j * 128 : HALF + (j + 1) * 128]
            return carry

        lax.fori_loop(0, half_rows // 512, project, 0)
        for j in range(pairs):
            mT[j] = mv3[j].T

    with scope("flow_c"):
        flow(("g", 4, 1), ("g", 3, 2), ("g", 2, 3))

    with scope("self_out"):
        ex.start(0, nt(joined(o3), w(COS, HALF)))
        ex.wait(0)
    with scope("cross_query"):
        for rows in texts:
            value = as_f32(tok[rows]) + ex.total(0, rows)
            x1[rows] = value
            n2[rows] = as_bf(value * inverse_rms(value) * gains[1:2])
        value = as_bf(nn(n2[...], w(CQC, HALF))) * jnp.asarray(HD**-0.5, BF)
        for j in range(pairs):
            qc3[j] = value[:, j * 128 : (j + 1) * 128]

    big, small = 512, 128

    def eb_at(a, start, size):
        return (2 * a + start // half_rows, slice(start % half_rows, start % half_rows + size))

    def eb_all(a):
        return eb[2 * a : 2 * a + 2].reshape(patches, TXT)

    def wide_query(j, t, rows, a):
        pick = as_bf(jnp.where(lane == t, 1.0, 0.0))
        return jnp.concatenate([qc3[j, rows] * mask[a], pick], axis=1)

    def cross_forward(j):
        def one(t, carry):
            rows = pl.ds(pl.multiple_of(t * TXT, TXT), TXT)
            parts = []
            for a in range(2):
                wide = wide_query(j, t, rows, a)
                top = jnp.full((8, TXT), -3e38, F32)
                for c in range(patches // big):
                    scores = nt(kext[j, c * big : (c + 1) * big], wide)
                    st[c * big : (c + 1) * big] = scores
                    top = jnp.maximum(top, jnp.max(scores.reshape(big // 8, 8, TXT), axis=0))
                top = jnp.max(top, axis=0, keepdims=True)
                total = jnp.zeros((8, TXT), F32)
                for c in range(patches // small):
                    expo = jnp.exp(st[c * small : (c + 1) * small] - top)
                    total = total + jnp.sum(expo.reshape(small // 8, 8, TXT), axis=0)
                    eb[eb_at(a, c * small, small)] = as_bf(expo)
                total = jnp.sum(total, axis=0, keepdims=True)
                clse[j, t, a] = jnp.broadcast_to(top + jnp.log(total), (8, TXT))
                parts.append(nn(mT[j, a * HD : (a + 1) * HD], eb_all(a)) * (1.0 / total))
            both = jnp.concatenate(parts, axis=0)
            ocT[j, t] = as_bf(both)
            oc3[j, rows] = as_bf(both.T)
            return carry

        lax.fori_loop(0, 2, one, 0)

    between = (
        (("g", 5, 1), ("g", 4, 2)),
        (("g", 3, 3), ("g", 5, 2)),
        (("g", 4, 3),),
    )
    for j in range(pairs):
        with scope("cross_attention"):
            cross_forward(j)
        with scope("flow_d"):
            flow(*between[j])
    with scope("cross_out"):
        ex.start(1, nt(joined(oc3), w(COC, HALF)))
        for j in range(pairs):
            mT[j] = kext[j, :, 0:128].T
        ex.wait(1)
    with scope("mlp_norm"):
        for rows in texts:
            value = x1[rows] + ex.total(1, rows)
            x2[rows] = value
            n3[rows] = as_bf(value * inverse_rms(value) * gains[2:3])
        acc[...] = jnp.zeros_like(acc)
        tgrad[...] = jnp.zeros_like(tgrad)
    root = (2.0 / jnp.pi) ** 0.5

    def mlp(f):
        base = CM + f * (3 * FT)
        gate_w, up_w, down_w = (w(base + k * FT, FT) for k in range(3))
        for rows in texts:
            gate, up = nn(n3[rows], gate_w), nn(n3[rows], up_w)
            grad = nn(cot[rows], down_w)
            square = gate * gate
            tanh = jnp.tanh(root * gate * (1.0 + 0.044715 * square))
            half = 0.5 * (1.0 + tanh)
            slope = half + 0.5 * gate * (1.0 - tanh * tanh) * (root * (1.0 + 3 * 0.044715 * square))
            active = gate * half
            osend[rows, 0:FT] = as_bf(active * up)
            osend[rows, FT : 2 * FT] = as_bf(grad * up * slope)
            osend[rows, 2 * FT : 3 * FT] = as_bf(grad * active)
        for rows in texts:
            acc[rows] += nt(osend[rows, 0:FT], down_w)
            tgrad[rows] += nt(osend[rows, FT : 2 * FT], gate_w) + nt(osend[rows, 2 * FT : 3 * FT], up_w)
        if direct:
            gather.sent(3 + f)
        put(base, tn(n3[...], osend[:, FT : 2 * FT]))
        put(base + FT, tn(n3[...], osend[:, 2 * FT : 3 * FT]))
        put(base + 2 * FT, tn(cot[...], osend[:, 0:FT]))

    before = ((), (), (("g", 5, 3),), (("g", LAST, 3),))
    after = (
        (("s", 0, 0),),
        (("s", 1, 0), ("s", 0, 1)),
        (("s", 2, 0), ("s", 1, 1)),
        (("s", 3, 0), ("s", 0, 2), ("s", 2, 1)),
    )
    for f in range(FH // FT):
        with scope("flow_e"):
            flow(*before[f])
        with scope("mlp"):
            mlp(f)
        with scope("flow_f"):
            flow(*after[f])
    with scope("mlp_out"):
        ex.start(2, tgrad[...])
        osend[...] = as_bf(acc[...])
        side = remote(osend, orecv, side_sem.at[2], side_sem.at[3], other)
        side.start()
        ex.wait(2)
        side.wait()
    with scope("mlp_norm_back"):
        for rows in texts:
            out[rows] = as_bf(x2[rows] + (as_f32(osend[rows]) + as_f32(orecv[rows])))
            grad, grad_gain = norm_back(x2[rows], gains[2:3], ex.total(2, rows))
            value = as_f32(cot[rows]) + grad
            x2[rows] = value
            dgains[2:3] += grad_gain
            back = as_bf(value)
            n3[rows] = back
            turned = as_bf(nn(back, w(COC, HALF)))
            for j in range(pairs):
                do3[j, rows] = turned[:, j * 128 : (j + 1) * 128]
        if direct:
            gather.sent(0)
            gather.sent(1)
            gather.sent(2)
        put(COC, tn(n3[...], joined(oc3)))
    with scope("flow_g"):
        flow(("s", 4, 0), ("s", 3, 1), ("s", 1, 2), ("s", 0, 3))

    def cross_back(j):
        st[...] = jnp.zeros_like(st)

        def one(t, carry):
            rows = pl.ds(pl.multiple_of(t * TXT, TXT), TXT)
            grad = do3[j, rows].T
            attended = as_f32(ocT[j, t])
            parts = []
            for a in range(2):
                keep = grad[a * HD : (a + 1) * HD]
                inner = jnp.sum(as_f32(keep) * attended[a * HD : (a + 1) * HD], axis=0, keepdims=True)
                empty = jnp.zeros_like(keep)
                low = jnp.concatenate([keep, empty] if a == 0 else [empty, keep], axis=0)
                wide = wide_query(j, t, rows, a)
                lse = clse[j, t, a, 0:1]
                for c in range(patches // big):
                    keys = slice(c * big, (c + 1) * big)
                    probs = jnp.exp(nt(kext[j, keys], wide) - lse)
                    eb[eb_at(0, c * big, big)] = as_bf(probs)
                    eb[eb_at(1, c * big, big)] = as_bf(probs * (nn(mv3[j, keys], low) - inner))
                for c in range(patches // big):
                    keys = slice(c * big, (c + 1) * big)
                    st[keys, 0:128] += nt(eb[eb_at(0, c * big, big)], low)
                    st[keys, 128:256] += nn(eb[eb_at(1, c * big, big)], wide[:, 0:128])
                parts.append(nn(mT[j, a * HD : (a + 1) * HD], eb_all(1)))
            dqc3[j, rows] = as_bf((jnp.concatenate(parts, axis=0) * HD**-0.5).T)
            return carry

        lax.fori_loop(0, 2, one, 0)
        mv3[j] = as_bf(st[:, 0:128])
        kext[j, :, 0:128] = as_bf(st[:, 128:256])

    between = (
        (("s", 4, 1), ("s", 2, 2)),
        (("s", 3, 2), ("s", 1, 3)),
        (("s", 4, 2), ("s", 2, 3)),
    )
    for j in range(pairs):
        with scope("cross_back"):
            cross_back(j)
        with scope("flow_h"):
            flow(*between[j])
    with scope("cross_query_back"):
        ex.start(3, nt(joined(dqc3), w(CQC, HALF)))

    def memory_back(c, start):
        rows = pl.ds(pl.multiple_of(start + c * 256, 256), 256)
        both = jnp.concatenate(
            [kext[j, rows, 0:128] for j in range(pairs)] + [mv3[j, rows] for j in range(pairs)], axis=1
        )
        return nt(both, w(CKV, 2 * HALF))

    with scope("memory_back_other"):

        def send_part(c, carry):
            value = as_bf(memory_back(c, (1 - head) * half_rows))
            for k in range(3):
                eb[k, pl.ds(pl.multiple_of(c * 256, 256), 256)] = value[:, k * TXT : (k + 1) * TXT]
            return carry

        lax.fori_loop(0, half_rows // 256, send_part, 0)
        mside = remote(eb.at[0:3], mrecv, side_sem.at[6], side_sem.at[7], other)
        mside.start()
    with scope("cross_query_grad"):
        ex.wait(3)
        put(CQC, tn(n2[...], joined(dqc3)))
    with scope("flow_i"):
        flow(("s", 6, 0), ("s", 3, 3))
    with scope("cross_norm_back"):
        for rows in texts:
            grad, grad_gain = norm_back(x1[rows], gains[1:2], ex.total(3, rows))
            value = x2[rows] + grad
            x1[rows] = value
            dgains[1:2] += grad_gain
            back = as_bf(value)
            n3[rows] = back
            turned = as_bf(nn(back, w(COS, HALF)))
            for j in range(pairs):
                do3[j, rows] = turned[:, j * 128 : (j + 1) * 128]
        put(COS, tn(n3[...], joined(o3)))
    with scope("flow_j"):
        flow(("s", 7, 0), ("s", 4, 3))
    with scope("memory_back_own"):
        mside.wait()
        stores = []
        for c in range(half_rows // 256):
            if c >= 2:
                stores[c - 2].wait()
            slot_rows = slice((c % 2) * 256, (c % 2 + 1) * 256)
            part = slice(c * 256, (c + 1) * 256)
            peer_part = jnp.concatenate([mrecv[k, part] for k in range(3)], axis=1)
            acc[slot_rows] = memory_back(c, head * half_rows) + as_f32(peer_part)
            store = pltpu.make_async_copy(acc.at[slot_rows], mgrad.at[pl.ds(c * 256, 256)], msem.at[c])
            store.start()
            stores.append(store)
    with scope("memory_weight_grad"):
        for number, source in enumerate((kext, mv3)):
            total = jnp.zeros((D, HALF), F32)
            for c in range(patches // 512):
                rows = slice(c * 512, (c + 1) * 512)
                part = slice(c * 512 % half_rows, c * 512 % half_rows + 512)
                both = jnp.concatenate([source[j, rows, 0:128] for j in range(pairs)], axis=1)
                total = total + tn(mem[c * 512 // half_rows, part], both)
            put(CKV + number * HALF, total)
    with scope("flow_k"):
        flow(("s", 5, 0), ("s", 6, 1), ("s", 7, 1))

    def self_back(j, carry):
        for t in range(2):
            rows = texts[t]
            grad = as_f32(do3[j, rows]).T
            attended = as_f32(oT[j, t])
            query_pair, key_pair, value_pair = q3[j, rows], k3[j, rows], v3[j, rows]
            key_turned = key_pair.T
            parts = []
            grad_key = jnp.zeros((TXT, 128), F32)
            grad_value = jnp.zeros((TXT, 128), F32)
            for a in range(2):
                keep = as_bf(grad[a * HD : (a + 1) * HD] * slinv[j, t, a, 0:1])
                inner = jnp.sum(as_f32(keep) * attended[a * HD : (a + 1) * HD], axis=0, keepdims=True)
                empty = jnp.zeros_like(keep)
                low = jnp.concatenate([keep, empty] if a == 0 else [empty, keep], axis=0)
                expo = sexps[j, t, a]
                grad_scores = as_bf(as_f32(expo) * (nn(value_pair, low) - inner))
                grad_value = grad_value + nt(expo, low)
                grad_key = grad_key + nn(grad_scores, query_pair * mask[a])
                parts.append(nn(key_turned[a * HD : (a + 1) * HD], grad_scores))
            q3[j, rows] = as_bf((jnp.concatenate(parts, axis=0) * HD**-0.5).T)
            k3[j, rows] = as_bf(grad_key)
            v3[j, rows] = as_bf(grad_value)
        return carry

    with scope("self_back"):
        lax.fori_loop(0, pairs, self_back, 0)
    with scope("flow_l"):
        flow(("s", 5, 1), ("s", 6, 2), ("s", 7, 2))
    with scope("self_project_back"):
        ex.start(
            4,
            nt(joined(q3), w(CQ, HALF))
            + nt(joined(k3), w(CQ + HALF, HALF))
            + nt(joined(v3), w(CQ + 2 * HALF, HALF)),
        )
        for number, source in enumerate((q3, k3, v3)):
            put(CQ + number * HALF, tn(n1[...], joined(source)))
    with scope("flow_m"):
        flow(("s", 8, 0))
    with scope("self_norm_back"):
        ex.wait(4)
        for rows in texts:
            grad, grad_gain = norm_back(as_f32(tok[rows]), gains[0:1], ex.total(4, rows))
            tgrad[rows] = x1[rows] + grad
            dgains[0:1] += grad_gain
        put(GAIN, dgains[...].T)
    with scope("flow_n"):
        flow(("s", 9, 0), ("s", 5, 2), ("s", 8, 1), ("s", 9, 1), ("s", 6, 3), ("s", 7, 3), ("s", 5, 3),
             ("s", 8, 2), ("s", 9, 2), ("s", 8, 3), ("s", 9, 3))
    if direct:
        with scope("norm"):
            first = red[:, 0:128]
            first = jnp.sum(first * first, axis=0, keepdims=True)
            value = jnp.where(head == 0, first, jnp.zeros_like(first))
            for column in range(128, PACK, 128):
                part = red[:, column : column + 128]
                value = value + jnp.sum(part * part, axis=0, keepdims=True)
            value = jnp.broadcast_to(jnp.sum(value, axis=1, keepdims=True), (8, 128))
            for step in range(5):
                sums[step] = value
                peer = other if step == 4 else (me ^ (1 << step), head)
                copy = remote(sums.at[step], others.at[step], t_send.at[step], t_recv.at[step], peer)
                copy.start()
                copy.wait()
                value = value + others[step]
            norm[...] = value
            scatter.sent()
    else:
        store = pltpu.make_async_copy(ws, dwall, wsem.at[1])
        store.start()
        store.wait()
    for number in (-2, -1):
        stores[number].wait()


def layer(direct, tokens, cotangent, patch_item, patch_mask, text_item, text_len, memory, weights):
    rows, half_rows = tokens.shape[0], memory.shape[0]
    patches = 2 * half_rows
    vm = pl.BlockSpec(memory_space=pltpu.VMEM)
    sm = pl.BlockSpec(memory_space=pltpu.SMEM)
    anywhere = pl.BlockSpec(memory_space=pl.ANY)
    S, DMA = pltpu.VMEM, pltpu.SemaphoreType.DMA
    heads3 = S((3, rows, 128), BF)
    scratch = [
        S((ZN, YN, XN, BLOCK, PACK), BF), S((2, half_rows, D), BF), S((8, D), F32), S((128, D), F32),
        S((patches, 128), BF), S((2, TXT, TXT), BF),
        S((rows, D), BF), S((rows, D), BF), S((rows, D), BF), S((rows, D), F32), S((rows, D), F32),
        heads3, heads3, heads3, heads3, S((3, 2, 128, TXT), BF), heads3, heads3, S((3, 2, 128, TXT), BF),
        heads3, heads3, S((3, 2, 2, TXT, TXT), BF), S((3, 2, 2, 8, TXT), F32),
        S((3, patches, 256), BF), S((3, patches, 128), BF), S((3, 128, patches), BF),
        S((patches, TXT), F32), S((4, half_rows, TXT), BF), S((3, 2, 2, 8, TXT), F32), S((rows, D), F32),
        S((2, rows, D), BF), S((2, rows, D), BF), S((rows, D), BF), S((rows, D), BF),
        S((3, half_rows, TXT), BF),
        DMA((5,)), DMA((5,)), DMA((8,)), DMA((2,)), DMA((half_rows // 256,)),
    ]
    shapes = [
        jax.ShapeDtypeStruct((rows, D), BF),
        jax.ShapeDtypeStruct((rows, D), F32),
        jax.ShapeDtypeStruct((half_rows, D), F32),
    ]
    if direct:
        scratch += [
            S((ZN, BLOCK, PACK), BF), S((2, ZN, BLOCK, PACK), BF), S((3, BLOCK, PACK), BF),
            S((2, BLOCK // 2, HALF), F32), S((2, BLOCK // 2, HALF), F32),
            S((5, 8, 128), F32), S((5, 8, 128), F32),
            DMA((len(GATHER), 7)), DMA((len(GATHER), 7)), DMA((len(SCATTER), 7)), DMA((len(SCATTER), 7)),
            DMA((5,)), DMA((5,)),
        ]
        shapes += [jax.ShapeDtypeStruct((BLOCK, PACK), F32), jax.ShapeDtypeStruct((8, 128), F32)]
        more_in, more_out = [vm] * len(weights), [vm, vm]
    else:
        shapes += [jax.ShapeDtypeStruct((ZN, YN, XN, BLOCK, PACK), BF)]
        more_in, more_out = [anywhere], [anywhere]
    return pl.pallas_call(
        functools.partial(layer_kernel, direct),
        out_shape=tuple(shapes),
        in_specs=[vm, vm, vm, vm, sm, sm, anywhere] + more_in,
        out_specs=tuple([vm, vm, anywhere] + more_out),
        scratch_shapes=scratch,
        name="layer",
        compiler_params=pltpu.CompilerParams(
            collective_id=1, has_side_effects=True, vmem_limit_bytes=VMEM_BYTES
        ),
    )(
        tokens, cotangent, patch_item.reshape(1, patches), patch_mask.reshape(1, patches),
        text_item, text_len, memory, *weights,
    )


def adam_step(weight, first, second, grad, rate, decay):
    first_new = BETA1 * first + (1.0 - BETA1) * grad
    second_new = BETA2 * second + (1.0 - BETA2) * grad * grad
    mean_hat = first_new / (1.0 - BETA1**STEP)
    square_hat = second_new / (1.0 - BETA2**STEP)
    weight_new = weight - rate * (mean_hat / (jnp.sqrt(square_hat) + ADAM_EPS) + decay * weight)
    return (weight_new, first_new, second_new)


def pack_weights(gains, self_proj, query, keyval, out_proj, mlp_input, mlp_output):
    rows = gains.shape[1]
    turned_out = jnp.swapaxes(out_proj, 1, 2)
    turned_down = mlp_output.T
    pieces = [jnp.pad(gains.T, ((0, 0), (0, 125)))]
    pieces += [self_proj[0], self_proj[1], self_proj[2], keyval[0], keyval[1]]
    pieces += [turned_out[0], query, turned_out[1]]
    for tile in range(FH // FT):
        columns = slice(tile * FT, (tile + 1) * FT)
        pieces += [mlp_input[0][:, columns], mlp_input[1][:, columns], turned_down[:, columns]]
    return jnp.concatenate([piece.astype(BF) for piece in pieces], axis=1)


def unpack_grads(red):
    def cut(start, width):
        return red[:, start : start + width]

    gains = cut(GAIN, 3).T
    self_proj = jnp.stack([cut(CQ + i * HALF, HALF) for i in range(3)])
    keyval = jnp.stack([cut(CKV + i * HALF, HALF) for i in range(2)])
    query = cut(CQC, HALF)
    out_proj = jnp.stack([cut(COS, HALF).T, cut(COC, HALF).T])
    tiles = FH // FT
    mlp = [jnp.concatenate([cut(CM + (3 * tile + k) * FT, FT) for tile in range(tiles)], axis=1) for k in range(3)]
    return gains, self_proj, query, keyval, out_proj, jnp.stack(mlp[:2]), mlp[2].T


def per_device(
    tokens, memory, cotangent, patch_item, patch_mask, text_item, text_len,
    norm_gains, gains_mean, gains_square,
    self_proj, self_proj_mean, self_proj_square,
    query_cross, query_cross_mean, query_cross_square,
    keyval_cross, keyval_cross_mean, keyval_cross_square,
    out_proj, out_proj_mean, out_proj_square,
    mlp_input, mlp_input_mean, mlp_input_square,
    mlp_output, mlp_output_mean, mlp_output_square,
):
    count = lax.axis_size("dp")
    direct = count == ZN * YN * XN
    ints = (patch_item, patch_mask, text_item, text_len)
    if direct:
        weights = (
            jnp.pad(norm_gains.T, ((0, 0), (0, 125))),
            self_proj,
            query_cross,
            keyval_cross,
            jnp.swapaxes(out_proj, 1, 2).astype(BF),
            mlp_input,
            mlp_output.T.astype(BF),
        )
        output, tokens_grad, memory_grad, red, norm = layer(True, tokens, cotangent, *ints, memory, weights)
        total = norm[0, 0]
    else:
        keyval_own = lax.all_to_all(keyval_cross.astype(BF), "head", split_axis=2, concat_axis=1, tiled=True)
        pack = pack_weights(norm_gains, self_proj, query_cross, keyval_own, out_proj, mlp_input, mlp_output)
        wall = lax.all_gather(pack, "dp", axis=0, tiled=True).reshape(ZN, YN, XN, BLOCK, PACK)
        output, tokens_grad, memory_grad, dwall = layer(False, tokens, cotangent, *ints, memory, (wall,))
        red = lax.psum_scatter(dwall.reshape(D, PACK).astype(F32), "dp", scatter_dimension=0, tiled=True)
        squares = jnp.sum(red[:, 128:] ** 2)
        squares = squares + jnp.where(lax.axis_index("head") == 0, jnp.sum(red[:, :128] ** 2), 0.0)
        total = lax.psum(squares, ("dp", "head"))
    gains_g, self_g, query_g, keyval_g, out_g, input_g, output_g = unpack_grads(red)
    keyval_g = lax.all_to_all(keyval_g, "head", split_axis=1, concat_axis=2, tiled=True)
    grad_norm = jnp.sqrt(total)
    factor = jnp.minimum(1.0, CLIP / (grad_norm + NORM_EPS))
    wide_rate = 2.0 * D ** (-0.5)
    results = [output, tokens_grad, memory_grad, grad_norm]
    for weight, first, second, grad, rate, decay in (
        (norm_gains, gains_mean, gains_square, gains_g, 0.5, 0.0),
        (self_proj, self_proj_mean, self_proj_square, self_g, wide_rate, DECAY),
        (query_cross, query_cross_mean, query_cross_square, query_g, wide_rate, DECAY),
        (keyval_cross, keyval_cross_mean, keyval_cross_square, keyval_g, wide_rate, DECAY),
        (out_proj, out_proj_mean, out_proj_square, out_g, 2.0 * (D // 16) ** (-0.5), DECAY),
        (mlp_input, mlp_input_mean, mlp_input_square, input_g, wide_rate, DECAY),
        (mlp_output, mlp_output_mean, mlp_output_square, output_g, 2.0 * FF ** (-0.5), DECAY),
    ):
        results += adam_step(weight, first, second, grad * factor, rate, decay)
    return tuple(results)


def solution(mesh):
    in_specs = (
        P("dp", None),
        P(("dp", "head"), None),
        P("dp", None),
        P("dp"),
        P("dp"),
        P("dp"),
        P("dp"),
        P(None, "dp"),
        P(None, "dp"),
        P(None, "dp"),
        P(None, "dp", "head"),
        P(None, "dp", "head"),
        P(None, "dp", "head"),
        P("dp", "head"),
        P("dp", "head"),
        P("dp", "head"),
        P(None, ("dp", "head"), None),
        P(None, ("dp", "head"), None),
        P(None, ("dp", "head"), None),
        P(None, "head", "dp"),
        P(None, "head", "dp"),
        P(None, "head", "dp"),
        P(None, "dp", "head"),
        P(None, "dp", "head"),
        P(None, "dp", "head"),
        P("head", "dp"),
        P("head", "dp"),
        P("head", "dp"),
    )
    out_specs = (
        P("dp", None),
        P("dp", None),
        P(("dp", "head"), None),
        P(),
        P(None, "dp"),
        P(None, "dp"),
        P(None, "dp"),
        P(None, "dp", "head"),
        P(None, "dp", "head"),
        P(None, "dp", "head"),
        P("dp", "head"),
        P("dp", "head"),
        P("dp", "head"),
        P(None, ("dp", "head"), None),
        P(None, ("dp", "head"), None),
        P(None, ("dp", "head"), None),
        P(None, "head", "dp"),
        P(None, "head", "dp"),
        P(None, "head", "dp"),
        P(None, "dp", "head"),
        P(None, "dp", "head"),
        P(None, "dp", "head"),
        P("head", "dp"),
        P("head", "dp"),
        P("head", "dp"),
    )
    return jax.shard_map(
        per_device, mesh=mesh, in_specs=in_specs, out_specs=out_specs, check_vma=False
    )
```

```python
import functools

import jax
import jax.numpy as jnp
from jax import lax
from jax.experimental import pallas as pl
from jax.experimental.pallas import tpu as pltpu
from jax.sharding import PartitionSpec as P

D = 768
HD = 64
FF = 2048
TXT = 256
STEP = 10

BETA1 = 0.9
BETA2 = 0.95
ADAM_EPS = 1e-08
DECAY = 0.1
CLIP = 1.0
NORM_EPS = 1e-06
MASKED = -1e30

MESH = pl.DeviceIdType.MESH
BF = jnp.bfloat16
F32 = jnp.float32
VMEM_BYTES = 63 * 2**20

HALF = D // 2
FT = 256
FH = FF // 2
GAIN = 0
CQ = 128
CKV = CQ + 3 * HALF
COS = CKV + 2 * HALF
CQC = COS + HALF
COC = CQC + HALF
CM = COC + HALF
PACK = CM + 3 * FH


def as_bf(value):
    return value.astype(BF)


def as_f32(value):
    return value.astype(F32)


def nn(left, right):
    return lax.dot_general(left, right, (((1,), (0,)), ((), ())), preferred_element_type=F32)


def nt(left, right):
    return lax.dot_general(left, right, (((1,), (1,)), ((), ())), preferred_element_type=F32)


def tn(left, right):
    return lax.dot_general(left, right, (((0,), (0,)), ((), ())), preferred_element_type=F32)


BLOCKS = (2, 2, 2, 2)
BLOCK = D // 16


def middle(low, high):
    return low + (high - low) // 256 * 128 if high - low >= 256 else high


class Links:
    def __init__(self):
        self.me, self.head = lax.axis_index("dp"), lax.axis_index("head")
        self.x, self.y = self.me & 1, (self.me >> 1) & 1
        self.z0, self.z1 = (self.me >> 2) & 1, self.me >> 3
        self.to_x, self.to_y, self.to_z0, self.to_z1 = [(self.me ^ bit, self.head) for bit in (1, 2, 4, 8)]
        self.to_core = (self.me, 1 - self.head)

    def peers(self):
        return [self.to_x, self.to_y, self.to_z0, self.to_z1, self.to_core]


def remote(source, target, send, recv, device):
    return pltpu.make_async_remote_copy(
        src_ref=source, dst_ref=target, send_sem=send, recv_sem=recv, device_id=device, device_id_type=MESH
    )


GATHER = (
    (0, 384, True),
    (384, 768, True),
    (768, 1280, False),
    (1280, 2048, True),
    (2048, 3200, True),
    (3200, 3968, True),
    (3968, 4736, True),
    (4736, 5504, True),
    (5504, 6272, False),
)

SCATTER = (
    (3200, 3968, False),
    (3968, 4736, False),
    (4736, 5504, False),
    (5504, 6272, True),
    (2816, 3200, True),
    (1280, 2048, False),
    (2432, 2816, False),
    (2048, 2432, False),
    (128, 512, False),
    (512, 896, True),
    (896, 1280, False),
    (0, 128, False),
)

SCHEDULE = (
    ("g", 0, 0), ("g", 1, 0), ("g", 2, 0), "pack_rest", ("g", 8, 0), "masks", "pack_heads", ("g", 3, 0),
    ("g", 2, 1), ("g", 0, 1), ("g", 4, 0), ("g", 8, 1), ("g", 1, 1), ("g", 0, 2), ("g", 3, 1), ("g", 2, 2),
    ("g", 1, 2), ("g", 0, 3), ("g", 3, 2), ("g", 4, 1), ("g", 0, 4), ("g", 5, 0), ("g", 1, 3), ("g", 2, 3),
    ("g", 4, 2), ("g", 1, 4), ("g", 5, 1), ("g", 3, 3), ("g", 6, 0), ("g", 2, 4), "self_project",
    "self_attention0", ("g", 4, 3), ("g", 7, 0), "self_attention1", "self_attention2", ("g", 3, 4),
    ("g", 5, 2), ("g", 6, 1), "memory_project0", ("g", 8, 2), "memory_project1", ("g", 4, 4), "self_out",
    ("g", 6, 2), "cross_query", "cross00", ("g", 7, 1), "cross01", ("g", 5, 3), "cross10", ("g", 7, 2),
    "cross11", ("g", 8, 3), "cross20", ("g", 5, 4), "cross21", ("g", 6, 3), "cross_out", ("g", 7, 3),
    "mlp_norm", "mlp0", ("g", 6, 4), ("s", 0, 0), "mlp1", ("g", 7, 4), ("g", 8, 4), ("s", 1, 0), "mlp2",
    ("s", 0, 1), "mlp3", ("s", 3, 0), "mlp_out", ("s", 1, 1), "mlp_norm_back", "cback00", "cback01",
    ("s", 4, 0), ("s", 2, 0), "cback10", "cback11", ("s", 3, 1), ("s", 2, 1), "cback20", "cback21",
    ("s", 1, 2), "cross_query_back", "memory_other", ("s", 0, 2), "query_grad", ("s", 6, 0),
    "cross_norm_back", ("s", 4, 1), ("s", 7, 0), "memory_own", ("s", 3, 2), ("s", 2, 2), ("s", 6, 1),
    "memory_grad", ("s", 3, 3), ("s", 1, 3), "sback0", ("s", 7, 1), ("s", 0, 3), "sback1", ("s", 6, 2),
    ("s", 4, 2), ("s", 3, 4), ("s", 5, 0), "sback2", ("s", 1, 4), ("s", 2, 3), "self_project_back",
    ("s", 7, 2), ("s", 4, 3), "proj_grad0", ("s", 0, 4), ("s", 8, 0), ("s", 6, 3), "proj_grad1", ("s", 9, 0),
    "proj_grad2", ("s", 10, 0), ("s", 5, 1), ("s", 4, 4), ("s", 2, 4), "self_norm_back", ("s", 6, 4),
    ("s", 7, 3), ("s", 10, 1), ("s", 9, 1), ("s", 7, 4), ("s", 11, 0), ("s", 5, 2), ("s", 8, 1), ("s", 10, 2),
    ("s", 11, 1), ("s", 5, 3), ("s", 9, 2), ("s", 8, 2), ("s", 10, 3), ("s", 11, 2), ("s", 9, 3), ("s", 8, 3),
    ("s", 5, 4), ("s", 9, 4), ("s", 11, 3), ("s", 10, 4), ("s", 8, 4), ("s", 11, 4),
)


class Gather:
    def __init__(self, links, wall, send_sem, recv_sem):
        self.links, self.wall, self.send_sem, self.recv_sem = links, wall, send_sem, recv_sem

    def where(self, n, k, received):
        low, high, z_first = GATHER[n]
        half = middle(low, high)
        links, every = self.links, slice(None)
        z1, z0, y, x = links.z1, links.z0, links.y, links.x
        flip = (lambda v: 1 - v) if received else (lambda v: v)
        if z_first:
            index, cols, device = (
                ((flip(z1), z0, y, x), (low, high), links.to_z1),
                ((every, flip(z0), y, x), (low, high), links.to_z0),
                ((every, every, y, flip(x)), (low, high), links.to_x),
                ((every, every, flip(y), x), (low, high), links.to_y),
                ((every, every, flip(y), 1 - x), (low, half), links.to_y),
                ((every, every, 1 - y, flip(x)), (half, high), links.to_x),
            )[k]
        else:
            index, cols, device = (
                ((z1, z0, y, flip(x)), (low, high), links.to_x),
                ((z1, z0, flip(y), x), (low, high), links.to_y),
                ((z1, z0, flip(y), 1 - x), (low, half), links.to_y),
                ((z1, z0, 1 - y, flip(x)), (half, high), links.to_x),
                ((flip(z1), z0, every, every), (low, high), links.to_z1),
                ((every, flip(z0), every, every), (low, high), links.to_z0),
            )[k]
        return self.wall.at[index + (every, slice(*cols))], device

    def copy(self, n, k, received=False):
        ref, device = self.where(n, k, received)
        return remote(ref, ref, self.send_sem.at[n, k], self.recv_sem.at[n, k], device)

    def step(self, n, number):
        if GATHER[n][2]:
            plan = ((None, 0),), ((0, 1),), ((1, 2), (None, 3)), ((2, 4), (3, 5)), ((4, None), (5, None))
        else:
            plan = ((None, 0), (None, 1)), ((0, 2), (1, 3)), ((2, None), (3, 4)), ((4, 5),), ((5, None),)
        for wait, start in plan[number]:
            if wait is not None:
                self.copy(n, wait, True).wait_recv()
            if start is not None:
                self.copy(n, start).start()

    def sent(self, n):
        for k in range(6):
            self.copy(n, k).wait_send()


class Scatter:
    def __init__(self, links, wall, slot1, slot2, slot3, red, send_sem, recv_sem):
        self.links, self.wall, self.red = links, wall, red
        self.slot1, self.slot2, self.slot3 = slot1, slot2, slot3
        self.send_sem, self.recv_sem = send_sem, recv_sem

    def skipped(self, n):
        low, high, z_first = SCATTER[n]
        return (3 if z_first else 1,) if middle(low, high) == high else ()

    def copy(self, n, k):
        low, high, z_first = SCATTER[n]
        half = middle(low, high)
        links, every = self.links, slice(None)
        z1, z0, y, x = links.z1, links.z0, links.y, links.x
        slot1, slot2, slot3 = self.slot1, self.slot2, self.slot3
        if z_first:
            index, slot, place, cols, device = (
                ((every, 1 - z0, every, every), slot2, (every,) * 3, (low, high), links.to_z0),
                ((1 - z1, z0, every, every), slot1, (every,) * 2, (low, high), links.to_z1),
                ((z1, z0, 1 - y, 1 - x), slot3, (0,), (low, half), links.to_y),
                ((z1, z0, 1 - y, 1 - x), slot3, (0,), (half, high), links.to_x),
                ((z1, z0, y, 1 - x), slot3, (1,), (low, high), links.to_x),
                ((z1, z0, 1 - y, x), slot3, (2,), (low, high), links.to_y),
            )[k]
        else:
            index, slot, place, cols, device = (
                ((every, every, 1 - y, 1 - x), slot1, (every,) * 2, (low, half), links.to_y),
                ((every, every, 1 - y, 1 - x), slot1, (every,) * 2, (half, high), links.to_x),
                ((every, every, y, 1 - x), slot2, (0, every, every), (low, high), links.to_x),
                ((every, every, 1 - y, x), slot2, (1, every, every), (low, high), links.to_y),
                ((every, 1 - z0, y, x), slot3, (slice(0, 2),), (low, high), links.to_z0),
                ((1 - z1, z0, y, x), slot3, (2,), (low, high), links.to_z1),
            )[k]
        tail = (every, slice(*cols))
        return remote(
            self.wall.at[index + tail], slot.at[place + tail], self.send_sem.at[n, k], self.recv_sem.at[n, k], device
        )

    def add(self, index, *others):
        self.wall[index] = as_bf(sum((as_f32(ref[at]) for ref, at in others), as_f32(self.wall[index])))

    def step(self, n, number):
        low, high, z_first = SCATTER[n]
        half = middle(low, high)
        links, every = self.links, slice(None)
        z1, z0, y, x = links.z1, links.z0, links.y, links.x
        slot1, slot2, slot3 = self.slot1, self.slot2, self.slot3
        cols, left, right = (every, slice(low, high)), (every, slice(low, half)), (every, slice(half, high))
        groups = ((0,), (1,), (2, 3), (4, 5)) if z_first else ((0, 1), (2, 3), (4,), (5,))
        skipped = self.skipped(n)
        if number > 0:
            for k in groups[number - 1]:
                if k not in skipped:
                    self.copy(n, k).wait_recv()
        if number == 4:
            value = as_f32(self.wall[(z1, z0, y, x) + cols])
            for k in (1, 2) if z_first else (2,):
                value = value + as_f32(slot3[(k,) + cols])
            self.red[:, low:high] = value
        elif z_first and number == 1:
            for a in range(2):
                for b in range(2):
                    for c in range(2):
                        self.add((a, z0, b, c) + cols, (slot2, (a, b, c) + cols))
        elif z_first and number == 2:
            for b in range(2):
                for c in range(2):
                    self.add((z1, z0, b, c) + cols, (slot1, (b, c) + cols))
        elif z_first and number == 3:
            self.add((z1, z0, y, 1 - x) + left, (slot3, (0,) + left))
            if half < high:
                self.add((z1, z0, 1 - y, x) + right, (slot3, (0,) + right))
        elif number == 1:
            for a in range(2):
                for b in range(2):
                    self.add((a, b, y, 1 - x) + left, (slot1, (a, b) + left))
                    if half < high:
                        self.add((a, b, 1 - y, x) + right, (slot1, (a, b) + right))
        elif number == 2:
            for a in range(2):
                for b in range(2):
                    self.add((a, b, y, x) + cols, (slot2, (0, a, b) + cols), (slot2, (1, a, b) + cols))
        elif number == 3:
            for a in range(2):
                self.add((a, z0, y, x) + cols, (slot3, (a,) + cols))
        if number < 4:
            for k in groups[number]:
                if k not in skipped:
                    self.copy(n, k).start()

    def sent(self):
        for n in range(len(SCATTER)):
            for k in range(6):
                if k not in self.skipped(n):
                    self.copy(n, k).wait_send()


class Exchange:
    def __init__(self, links, send, recv, send_sem, recv_sem):
        self.links = links
        self.send, self.recv, self.send_sem, self.recv_sem = send, recv, send_sem, recv_sem

    def copy(self, number):
        slot = number % 2
        return remote(
            self.send.at[slot],
            self.recv.at[slot],
            self.send_sem.at[number],
            self.recv_sem.at[number],
            self.links.to_core,
        )

    def start(self, number, value):
        self.send[number % 2] = as_bf(value)
        self.copy(number).start()

    def wait(self, number):
        self.copy(number).wait()

    def total(self, number, rows=slice(None)):
        slot = number % 2
        return as_f32(self.send[slot, rows]) + as_f32(self.recv[slot, rows])


def inverse_rms(values):
    return lax.rsqrt(jnp.mean(values * values, axis=-1, keepdims=True) + NORM_EPS)


def norm_back(values, gain, grad):
    inverse = inverse_rms(values)
    scaled = grad * gain
    inner = jnp.mean(scaled * values, axis=-1, keepdims=True)
    grad_values = inverse * scaled - values * (inverse * inverse * inverse * inner)
    grad_gain = jnp.sum(grad * values * inverse, axis=0, keepdims=True)
    return grad_values, grad_gain


def layer_kernel(direct, *refs):
    (tok, cot, item, pmask, titem, tlen, memory), refs = refs[:7], refs[7:]
    if direct:
        (gshard, sproj, query, keyval, tout, minput, tdown), refs = refs[:7], refs[7:]
        (out, tgrad, mgrad, red, kvgrad, norm), refs = refs[:6], refs[6:]
    else:
        (wall,), refs = refs[:1], refs[1:]
        (out, tgrad, mgrad, dwall), refs = refs[:4], refs[4:]
    (
        ws, mem, gains, dgains, cbias, sbias, n1, n2, n3, x1, x2,
        q3, k3, v3, o3, oT, qc3, oc3, ocT, do3, dqc3, sexps, slinv,
        kext, mv3, mT, st, eb, clse, acc,
        esend, erecv, osend, orecv, mrecv,
        send_sem, recv_sem, side_sem, wsem, msem,
    ), refs = refs[:40], refs[40:]
    links = Links()
    head, other = links.head, links.to_core

    barrier = pltpu.get_barrier_semaphore()
    peers = links.peers() if direct else [other]
    for device in peers:
        pl.semaphore_signal(barrier, inc=1, device_id=device, device_id_type=MESH)
    own_memory = pltpu.make_async_copy(memory, mem.at[head], wsem.at[0])
    own_memory.start()
    mem_copy = remote(memory, mem.at[head], side_sem.at[0], side_sem.at[1], other)
    if direct:
        slot1, slot2, slot3, kvs, kvr, kgs, kgr, sums, others, g_send, g_recv, s_send, s_recv, t_send, t_recv = refs
        gather = Gather(links, ws, g_send, g_recv)
        scatter = Scatter(links, ws, slot1, slot2, slot3, red, s_send, s_recv)
        here = (links.z1, links.z0, links.y, links.x, slice(None))

        def own(column, value):
            ws[here + (slice(column, column + value.shape[1]),)] = as_bf(value)

        for k in range(2):
            kvs[k] = jnp.where(head == 0, keyval[k, :, HALF:], keyval[k, :, :HALF])
        dgains[...] = jnp.zeros_like(dgains)
        dgains[0:3, 0:BLOCK] = gshard[...]
        own(GAIN, dgains[:, 0:128].T[0:BLOCK])
        for i in range(3):
            own(CQ + i * HALF, sproj[i])
        pl.semaphore_wait(barrier, len(peers))
        kv_copy = remote(kvs, kvr, side_sem.at[4], side_sem.at[5], other)
        kv_copy.start()

        def pack_rest():
            for f in range(FH // FT):
                base = CM + f * 3 * FT
                for k in range(2):
                    own(base + k * FT, minput[k, :, f * FT : (f + 1) * FT])
                own(base + 2 * FT, tdown[:, f * FT : (f + 1) * FT])

        def pack_heads():
            own(COS, tout[0])
            own(CQC, query[...])
            own(COC, tout[1])
            mem_copy.start()
            kv_copy.wait()
            for k in range(2):
                mine = jnp.where(head == 0, keyval[k, :, :HALF], keyval[k, :, HALF:])
                top, bottom = jnp.where(head == 0, mine, kvr[k]), jnp.where(head == 0, kvr[k], mine)
                own(CKV + k * HALF, jnp.concatenate([top, bottom], axis=0))
    else:
        pl.semaphore_wait(barrier, len(peers))
        load = pltpu.make_async_copy(wall, ws, wsem.at[1])
        load.start()
        mem_copy.start()
        load.wait()

    ex = Exchange(links, esend, erecv, send_sem, recv_sem)

    def w(column, width):
        return ws[:, :, :, :, :, column : column + width].reshape(D, width)

    def put(column, value):
        width = value.shape[1]
        ws[:, :, :, :, :, column : column + width] = as_bf(value).reshape(BLOCKS + (BLOCK, width))

    def sent(column):
        if direct:
            for n, (low, high, _) in enumerate(GATHER):
                if low <= column < high and n not in done:
                    done.add(n)
                    gather.sent(n)

    done = set()
    half_rows = mem.shape[1]
    patches = 2 * half_rows
    lane = lax.broadcasted_iota(jnp.int32, (TXT, 128), 1)
    mask = [as_bf(jnp.where(lane < HD, 1.0, 0.0)), as_bf(jnp.where(lane < HD, 0.0, 1.0))]
    texts = [slice(0, TXT), slice(TXT, 2 * TXT)]
    pairs = 3
    pieces = {}

    def piece(name, *numbers):
        def keep(function):
            pieces[name] = functools.partial(function, *numbers)
            return function

        return keep

    def joined(ref, rows=slice(None)):
        return jnp.concatenate([ref[j, rows] for j in range(pairs)], axis=1)

    def spread(target, rows, value):
        for j in range(pairs):
            target[j, rows] = value[:, j * 128 : (j + 1) * 128]

    if direct:
        piece("pack_heads")(pack_heads)
        piece("pack_rest")(pack_rest)

    @piece("masks")
    def _():
        row = lax.broadcasted_iota(jnp.int32, (128, 512), 0)
        for c in range(patches // 512):
            cols = slice(c * 512, (c + 1) * 512)
            place = jnp.where(row == 0, titem[0], jnp.where(row == 1, titem[1], -1))
            seen = (place == item[:, cols]) & (pmask[:, cols] == 1)
            cbias[cols] = as_bf(jnp.where(seen, 0.0, jnp.where(row < 2, MASKED, 0.0)).T)
        key = lax.broadcasted_iota(jnp.int32, (TXT, TXT), 0)
        slot = lax.broadcasted_iota(jnp.int32, (TXT, TXT), 1)
        for t in range(2):
            sbias[t] = as_bf(jnp.where((key <= slot) & (key < tlen[t]), 0.0, MASKED))
        dgains[...] = jnp.zeros_like(dgains)
        acc[...] = jnp.zeros_like(acc)
        tgrad[...] = jnp.zeros_like(tgrad)

    @piece("self_project")
    def _():
        gains[...] = as_f32(w(0, 128)).T[0:8]
        for rows in texts:
            x = as_f32(tok[rows])
            n1[rows] = as_bf(x * inverse_rms(x) * gains[0:1])
        for number, target in enumerate((q3, k3, v3)):
            value = as_bf(nn(n1[...], w(CQ + number * HALF, HALF)))
            if number == 0:
                value = value * jnp.asarray(HD**-0.5, BF)
            spread(target, slice(None), value)

    def self_forward(j):
        for t in range(2):
            query_pair, key_pair = q3[j, texts[t]], k3[j, texts[t]]
            turned = v3[j, texts[t]].T
            parts = []
            for a in range(2):
                scores = nt(key_pair, query_pair * mask[a]) + as_f32(sbias[t])
                top = jnp.max(scores, axis=0, keepdims=True)
                expo = jnp.exp(scores - top)
                low = as_bf(expo)
                sexps[j, t, a] = low
                inverse = 1.0 / jnp.sum(expo, axis=0, keepdims=True)
                slinv[j, t, a] = jnp.broadcast_to(inverse, (8, TXT))
                parts.append(nn(turned[a * HD : (a + 1) * HD], low) * inverse)
            both = jnp.concatenate(parts, axis=0)
            oT[j, t] = as_bf(both)
            o3[j, texts[t]] = as_bf(both.T)

    for j in range(pairs):
        piece(f"self_attention{j}", j)(self_forward)

    def project(side):
        if side == 0:
            own_memory.wait()
            mem_copy.wait_send()
            remote(memory, mem.at[1 - head], side_sem.at[0], side_sem.at[1], other).wait_recv()
        for c in range(half_rows // 512):
            part = slice(c * 512, (c + 1) * 512)
            rows = slice(side * half_rows + c * 512, side * half_rows + (c + 1) * 512)
            both = as_bf(nn(mem[side, part], w(CKV, 2 * HALF)))
            for j in range(pairs):
                kext[j, rows, 0:128] = both[:, j * 128 : (j + 1) * 128]
                kext[j, rows, 128:256] = cbias[rows]
                mv3[j, rows] = both[:, HALF + j * 128 : HALF + (j + 1) * 128]
        side_rows = slice(side * half_rows, (side + 1) * half_rows)
        for j in range(pairs):
            mT[j, :, side_rows] = mv3[j, side_rows].T

    for side in range(2):
        piece(f"memory_project{side}", side)(project)

    @piece("self_out")
    def _():
        ex.start(0, nt(joined(o3), w(COS, HALF)))

    @piece("cross_query")
    def _():
        ex.wait(0)
        for rows in texts:
            value = as_f32(tok[rows]) + ex.total(0, rows)
            x1[rows] = value
            n2[rows] = as_bf(value * inverse_rms(value) * gains[1:2])
        spread(qc3, slice(None), as_bf(nn(n2[...], w(CQC, HALF))) * jnp.asarray(HD**-0.5, BF))

    big, small = 512, 128

    def eb_at(a, start, size):
        return (2 * a + start // half_rows, slice(start % half_rows, start % half_rows + size))

    def eb_all(a):
        return eb[2 * a : 2 * a + 2].reshape(patches, TXT)

    def wide_query(j, t, a):
        pick = as_bf(jnp.where(lane == t, 1.0, 0.0))
        return jnp.concatenate([qc3[j, texts[t]] * mask[a], pick], axis=1)

    def cross_forward(j, t):
        parts = []
        for a in range(2):
            wide = wide_query(j, t, a)
            top = jnp.full((8, TXT), -3e38, F32)
            for c in range(patches // big):
                scores = nt(kext[j, c * big : (c + 1) * big], wide)
                st[c * big : (c + 1) * big] = scores
                top = jnp.maximum(top, jnp.max(scores.reshape(big // 8, 8, TXT), axis=0))
            top = jnp.max(top, axis=0, keepdims=True)
            total = jnp.zeros((8, TXT), F32)
            for c in range(patches // small):
                expo = jnp.exp(st[c * small : (c + 1) * small] - top)
                total = total + jnp.sum(expo.reshape(small // 8, 8, TXT), axis=0)
                eb[eb_at(a, c * small, small)] = as_bf(expo)
            total = jnp.sum(total, axis=0, keepdims=True)
            clse[j, t, a] = jnp.broadcast_to(top + jnp.log(total), (8, TXT))
            parts.append(nn(mT[j, a * HD : (a + 1) * HD], eb_all(a)) * (1.0 / total))
        both = jnp.concatenate(parts, axis=0)
        ocT[j, t] = as_bf(both)
        oc3[j, texts[t]] = as_bf(both.T)

    for j in range(pairs):
        for t in range(2):
            piece(f"cross{j}{t}", j, t)(cross_forward)

    @piece("cross_out")
    def _():
        ex.start(1, nt(joined(oc3), w(COC, HALF)))
        for j in range(pairs):
            mT[j] = kext[j, :, 0:128].T

    @piece("mlp_norm")
    def _():
        ex.wait(1)
        for rows in texts:
            value = x1[rows] + ex.total(1, rows)
            x2[rows] = value
            n3[rows] = as_bf(value * inverse_rms(value) * gains[2:3])

    root = (2.0 / jnp.pi) ** 0.5

    def mlp(f):
        base = CM + f * (3 * FT)
        gate_w, up_w, down_w = (w(base + k * FT, FT) for k in range(3))
        for rows in texts:
            gate, up = nn(n3[rows], gate_w), nn(n3[rows], up_w)
            grad = nn(cot[rows], down_w)
            square = gate * gate
            tanh = jnp.tanh(root * gate * (1.0 + 0.044715 * square))
            half = 0.5 * (1.0 + tanh)
            slope = half + 0.5 * gate * (1.0 - tanh * tanh) * (root * (1.0 + 3 * 0.044715 * square))
            active = gate * half
            osend[rows, 0:FT] = as_bf(active * up)
            osend[rows, FT : 2 * FT] = as_bf(grad * up * slope)
            osend[rows, 2 * FT : 3 * FT] = as_bf(grad * active)
        for rows in texts:
            acc[rows] += nt(osend[rows, 0:FT], down_w)
            tgrad[rows] += nt(osend[rows, FT : 2 * FT], gate_w) + nt(osend[rows, 2 * FT : 3 * FT], up_w)
        sent(base)
        put(base, tn(n3[...], osend[:, FT : 2 * FT]))
        put(base + FT, tn(n3[...], osend[:, 2 * FT : 3 * FT]))
        put(base + 2 * FT, tn(cot[...], osend[:, 0:FT]))

    for f in range(FH // FT):
        piece(f"mlp{f}", f)(mlp)

    side = remote(osend, orecv, side_sem.at[2], side_sem.at[3], other)

    @piece("mlp_out")
    def _():
        ex.start(2, tgrad[...])
        osend[...] = as_bf(acc[...])
        side.start()

    @piece("mlp_norm_back")
    def _():
        ex.wait(2)
        for rows in texts:
            grad, grad_gain = norm_back(x2[rows], gains[2:3], ex.total(2, rows))
            value = as_f32(cot[rows]) + grad
            acc[rows] = x2[rows]
            x2[rows] = value
            dgains[2:3] += grad_gain
            back = as_bf(value)
            n3[rows] = back
            spread(do3, rows, as_bf(nn(back, w(COC, HALF))))
        sent(COC)
        put(COC, tn(n3[...], joined(oc3)))
        side.wait()
        for rows in texts:
            out[rows] = as_bf(acc[rows] + (as_f32(osend[rows]) + as_f32(orecv[rows])))

    def cross_back(j, t):
        rows = texts[t]
        grad = do3[j, rows].T
        attended = as_f32(ocT[j, t])
        parts = []
        for a in range(2):
            keep = grad[a * HD : (a + 1) * HD]
            inner = jnp.sum(as_f32(keep) * attended[a * HD : (a + 1) * HD], axis=0, keepdims=True)
            empty = jnp.zeros_like(keep)
            low = jnp.concatenate([keep, empty] if a == 0 else [empty, keep], axis=0)
            wide = wide_query(j, t, a)
            lse = clse[j, t, a, 0:1]
            for c in range(patches // big):
                keys = slice(c * big, (c + 1) * big)
                probs = jnp.exp(nt(kext[j, keys], wide) - lse)
                eb[eb_at(0, c * big, big)] = as_bf(probs)
                eb[eb_at(1, c * big, big)] = as_bf(probs * (nn(mv3[j, keys], low) - inner))
            for c in range(patches // big):
                keys = slice(c * big, (c + 1) * big)
                grad_value = nt(eb[eb_at(0, c * big, big)], low)
                grad_key = nn(eb[eb_at(1, c * big, big)], wide[:, 0:128])
                if t == 0 and a == 0:
                    st[keys, 0:128] = grad_value
                    st[keys, 128:256] = grad_key
                else:
                    st[keys, 0:128] += grad_value
                    st[keys, 128:256] += grad_key
            parts.append(nn(mT[j, a * HD : (a + 1) * HD], eb_all(1)))
        dqc3[j, rows] = as_bf((jnp.concatenate(parts, axis=0) * HD**-0.5).T)
        if t == 1:
            mv3[j] = as_bf(st[:, 0:128])
            kext[j, :, 0:128] = as_bf(st[:, 128:256])

    for j in range(pairs):
        for t in range(2):
            piece(f"cback{j}{t}", j, t)(cross_back)

    @piece("cross_query_back")
    def _():
        ex.start(3, nt(joined(dqc3), w(CQC, HALF)))

    def memory_back(c, start):
        rows = pl.ds(pl.multiple_of(start + c * 256, 256), 256)
        both = jnp.concatenate(
            [kext[j, rows, 0:128] for j in range(pairs)] + [mv3[j, rows] for j in range(pairs)], axis=1
        )
        return nt(both, w(CKV, 2 * HALF))

    mside = remote(eb.at[0:3], mrecv, side_sem.at[6], side_sem.at[7], other)

    @piece("memory_other")
    def _():
        def send_part(c, carry):
            value = as_bf(memory_back(c, (1 - head) * half_rows))
            for k in range(3):
                eb[k, pl.ds(pl.multiple_of(c * 256, 256), 256)] = value[:, k * TXT : (k + 1) * TXT]
            return carry

        lax.fori_loop(0, half_rows // 256, send_part, 0)
        mside.start()

    @piece("query_grad")
    def _():
        sent(CQC)
        put(CQC, tn(n2[...], joined(dqc3)))
        ex.wait(3)

    @piece("cross_norm_back")
    def _():
        for rows in texts:
            grad, grad_gain = norm_back(x1[rows], gains[1:2], ex.total(3, rows))
            value = x2[rows] + grad
            x1[rows] = value
            dgains[1:2] += grad_gain
            back = as_bf(value)
            n3[rows] = back
            spread(do3, rows, as_bf(nn(back, w(COS, HALF))))
        sent(COS)
        put(COS, tn(n3[...], joined(o3)))

    stores = []

    @piece("memory_own")
    def _():
        mside.wait()
        for c in range(half_rows // 256):
            if c >= 2:
                stores[c - 2].wait()
            slot_rows = slice((c % 2) * 256, (c % 2 + 1) * 256)
            part = slice(c * 256, (c + 1) * 256)
            peer_part = jnp.concatenate([mrecv[k, part] for k in range(3)], axis=1)
            acc[slot_rows] = memory_back(c, head * half_rows) + as_f32(peer_part)
            store = pltpu.make_async_copy(acc.at[slot_rows], mgrad.at[pl.ds(c * 256, 256)], msem.at[c])
            store.start()
            stores.append(store)

    @piece("memory_grad")
    def _():
        sent(CKV)
        for number, source in enumerate((kext, mv3)):
            total = jnp.zeros((D, HALF), F32)
            for c in range(patches // 512):
                rows = slice(c * 512, (c + 1) * 512)
                part = slice(c * 512 % half_rows, c * 512 % half_rows + 512)
                both = jnp.concatenate([source[j, rows, 0:128] for j in range(pairs)], axis=1)
                total = total + tn(mem[c * 512 // half_rows, part], both)
            put(CKV + number * HALF, total)

    def self_back(j):
        for t in range(2):
            rows = texts[t]
            grad = as_f32(do3[j, rows]).T
            attended = as_f32(oT[j, t])
            query_pair, key_pair, value_pair = q3[j, rows], k3[j, rows], v3[j, rows]
            key_turned = key_pair.T
            parts = []
            grad_key = jnp.zeros((TXT, 128), F32)
            grad_value = jnp.zeros((TXT, 128), F32)
            for a in range(2):
                keep = as_bf(grad[a * HD : (a + 1) * HD] * slinv[j, t, a, 0:1])
                inner = jnp.sum(as_f32(keep) * attended[a * HD : (a + 1) * HD], axis=0, keepdims=True)
                empty = jnp.zeros_like(keep)
                low = jnp.concatenate([keep, empty] if a == 0 else [empty, keep], axis=0)
                expo = sexps[j, t, a]
                grad_scores = as_bf(as_f32(expo) * (nn(value_pair, low) - inner))
                grad_value = grad_value + nt(expo, low)
                grad_key = grad_key + nn(grad_scores, query_pair * mask[a])
                parts.append(nn(key_turned[a * HD : (a + 1) * HD], grad_scores))
            q3[j, rows] = as_bf((jnp.concatenate(parts, axis=0) * HD**-0.5).T)
            k3[j, rows] = as_bf(grad_key)
            v3[j, rows] = as_bf(grad_value)

    for j in range(pairs):
        piece(f"sback{j}", j)(self_back)

    @piece("self_project_back")
    def _():
        ex.start(
            4,
            nt(joined(q3), w(CQ, HALF))
            + nt(joined(k3), w(CQ + HALF, HALF))
            + nt(joined(v3), w(CQ + 2 * HALF, HALF)),
        )
        for number in range(3):
            sent(CQ + number * HALF)

    def projection_grad(number):
        put(CQ + number * HALF, tn(n1[...], joined((q3, k3, v3)[number])))

    for number in range(3):
        piece(f"proj_grad{number}", number)(projection_grad)

    @piece("self_norm_back")
    def _():
        ex.wait(4)
        for rows in texts:
            grad, grad_gain = norm_back(as_f32(tok[rows]), gains[0:1], ex.total(4, rows))
            tgrad[rows] = x1[rows] + grad
            dgains[0:1] += grad_gain
        sent(GAIN)
        put(GAIN, dgains[...].T)

    kv_group = [n for n, group in enumerate(SCATTER) if group[0] == CKV][0]
    kv_back = remote(kgs, kgr, side_sem.at[8], side_sem.at[9], other) if direct else None

    def send_keyval():
        kgs[...] = jnp.where(head == 0, red[BLOCK // 2 :, CKV:COS], red[: BLOCK // 2, CKV:COS])
        kv_back.start()

    def finish_keyval():
        kv_back.wait()
        mine = jnp.where(head == 0, red[: BLOCK // 2, CKV:COS], red[BLOCK // 2 :, CKV:COS])
        for k in range(2):
            cols = slice(k * HALF, (k + 1) * HALF)
            first, second = mine[:, cols], kgr[:, cols]
            kvgrad[k, :, :HALF] = jnp.where(head == 0, first, second)
            kvgrad[k, :, HALF:] = jnp.where(head == 0, second, first)

    order = SCHEDULE if direct else [entry for entry in SCHEDULE if isinstance(entry, str)]
    for entry in order:
        if isinstance(entry, str):
            if direct or entry not in ("pack_heads", "pack_rest"):
                with jax.named_scope(entry):
                    pieces[entry]()
        else:
            part, n, number = entry
            with jax.named_scope("flow"):
                (gather if part == "g" else scatter).step(n, number)
            if part == "s" and n == kv_group and number == 4:
                send_keyval()

    if direct:
        with jax.named_scope("norm"):
            first = red[:, 0:128]
            first = jnp.sum(first * first, axis=0, keepdims=True)
            value = jnp.where(head == 0, first, jnp.zeros_like(first))
            for column in range(128, PACK, 128):
                part = red[:, column : column + 128]
                value = value + jnp.sum(part * part, axis=0, keepdims=True)
            value = jnp.broadcast_to(jnp.sum(value, axis=1, keepdims=True), (8, 128))
            for step, peer in enumerate((other, links.to_x, links.to_y, links.to_z0, links.to_z1)):
                sums[step] = value
                copy = remote(sums.at[step], others.at[step], t_send.at[step], t_recv.at[step], peer)
                copy.start()
                if step == 0:
                    finish_keyval()
                if step == 1:
                    scatter.sent()
                copy.wait()
                value = value + others[step]
            norm[...] = value
    else:
        store = pltpu.make_async_copy(ws, dwall, wsem.at[1])
        store.start()
        store.wait()
    for number in (-2, -1):
        stores[number].wait()


def layer(direct, tokens, cotangent, patch_item, patch_mask, text_item, text_len, memory, weights):
    rows, half_rows = tokens.shape[0], memory.shape[0]
    patches = 2 * half_rows
    vm = pl.BlockSpec(memory_space=pltpu.VMEM)
    sm = pl.BlockSpec(memory_space=pltpu.SMEM)
    anywhere = pl.BlockSpec(memory_space=pl.ANY)
    S, DMA = pltpu.VMEM, pltpu.SemaphoreType.DMA
    heads3 = S((3, rows, 128), BF)
    scratch = [
        S(BLOCKS + (BLOCK, PACK), BF), S((2, half_rows, D), BF), S((8, D), F32), S((128, D), F32),
        S((patches, 128), BF), S((2, TXT, TXT), BF),
        S((rows, D), BF), S((rows, D), BF), S((rows, D), BF), S((rows, D), F32), S((rows, D), F32),
        heads3, heads3, heads3, heads3, S((3, 2, 128, TXT), BF), heads3, heads3, S((3, 2, 128, TXT), BF),
        heads3, heads3, S((3, 2, 2, TXT, TXT), BF), S((3, 2, 2, 8, TXT), F32),
        S((3, patches, 256), BF), S((3, patches, 128), BF), S((3, 128, patches), BF),
        S((patches, TXT), F32), S((4, half_rows, TXT), BF), S((3, 2, 2, 8, TXT), F32), S((rows, D), F32),
        S((2, rows, D), BF), S((2, rows, D), BF), S((rows, D), BF), S((rows, D), BF),
        S((3, half_rows, TXT), BF),
        DMA((5,)), DMA((5,)), DMA((10,)), DMA((2,)), DMA((half_rows // 256,)),
    ]
    shapes = [
        jax.ShapeDtypeStruct((rows, D), BF),
        jax.ShapeDtypeStruct((rows, D), F32),
        jax.ShapeDtypeStruct((half_rows, D), F32),
    ]
    if direct:
        scratch += [
            S((2, 2, BLOCK, PACK), BF), S((2, 2, 2, BLOCK, PACK), BF), S((3, BLOCK, PACK), BF),
            S((2, BLOCK // 2, HALF), F32), S((2, BLOCK // 2, HALF), F32),
            S((BLOCK // 2, 2 * HALF), F32), S((BLOCK // 2, 2 * HALF), F32),
            S((5, 8, 128), F32), S((5, 8, 128), F32),
            DMA((len(GATHER), 6)), DMA((len(GATHER), 6)), DMA((len(SCATTER), 6)), DMA((len(SCATTER), 6)),
            DMA((5,)), DMA((5,)),
        ]
        shapes += [
            jax.ShapeDtypeStruct((BLOCK, PACK), F32),
            jax.ShapeDtypeStruct((2, BLOCK // 2, D), F32),
            jax.ShapeDtypeStruct((8, 128), F32),
        ]
        more_in, more_out = [vm] * len(weights), [vm] * 3
    else:
        shapes += [jax.ShapeDtypeStruct(BLOCKS + (BLOCK, PACK), BF)]
        more_in, more_out = [anywhere], [anywhere]
    return pl.pallas_call(
        functools.partial(layer_kernel, direct),
        out_shape=tuple(shapes),
        in_specs=[vm, vm, vm, vm, sm, sm, anywhere] + more_in,
        out_specs=tuple([vm, vm, anywhere] + more_out),
        scratch_shapes=scratch,
        name="layer",
        compiler_params=pltpu.CompilerParams(
            collective_id=1, has_side_effects=True, vmem_limit_bytes=VMEM_BYTES
        ),
    )(
        tokens, cotangent, patch_item.reshape(1, patches), patch_mask.reshape(1, patches),
        text_item, text_len, memory, *weights,
    )


def adam_step(weight, first, second, grad, rate, decay):
    first_new = BETA1 * first + (1.0 - BETA1) * grad
    second_new = BETA2 * second + (1.0 - BETA2) * grad * grad
    mean_hat = first_new / (1.0 - BETA1**STEP)
    square_hat = second_new / (1.0 - BETA2**STEP)
    weight_new = weight - rate * (mean_hat / (jnp.sqrt(square_hat) + ADAM_EPS) + decay * weight)
    return (weight_new, first_new, second_new)


RATES = (
    (0.5, 0.0),
    (2.0 * D**-0.5, DECAY),
    (2.0 * D**-0.5, DECAY),
    (2.0 * D**-0.5, DECAY),
    (2.0 * (D // 16) ** -0.5, DECAY),
    (2.0 * D**-0.5, DECAY),
    (2.0 * FF**-0.5, DECAY),
)


def finish_kernel(*refs):
    (red, kvgrad, norm), refs = refs[:3], refs[3:]
    states, refs = refs[:21], refs[21:]
    passed, refs = refs[:3], refs[3:]
    kept, refs = refs[:3], refs[3:]
    (grad_norm,), refs = refs[:1], refs[1:]
    results, (pad, sem, *held) = refs[:21], refs[21:]
    loads = [pltpu.make_async_copy(passed[i], held[i], sem.at[i]) for i in range(3)]
    stores = [pltpu.make_async_copy(held[i], kept[i], sem.at[3 + i]) for i in range(3)]
    for load in loads:
        load.start()
    value = jnp.sqrt(norm[0:1, 0:1])
    grad_norm[0, 0] = value[0, 0]
    factor = jnp.minimum(1.0, CLIP / (value + NORM_EPS))
    pad[...] = jnp.zeros_like(pad)
    pad[0:BLOCK] = red[:, 0:128]

    def update(number, index, grad):
        rate, decay = RATES[number]
        old = [states[3 * number + i][index] for i in range(3)]
        for i, new in enumerate(adam_step(*old, grad * factor, rate, decay)):
            results[3 * number + i][index] = new

    def cut(column, width):
        return red[:, column : column + width]

    update(0, ..., pad[...].T[0:3, 0:BLOCK])
    for load, store in zip(loads, stores):
        load.wait()
        store.start()
    for i in range(3):
        update(1, i, cut(CQ + i * HALF, HALF))
    update(2, ..., cut(CQC, HALF))
    for i in range(2):
        update(3, i, kvgrad[i])
        update(4, i, cut((COS, COC)[i], HALF))
    for f in range(FH // FT):
        cols = slice(f * FT, (f + 1) * FT)
        base = CM + f * 3 * FT
        for i in range(2):
            update(5, (i, slice(None), cols), cut(base + i * FT, FT))
        update(6, (slice(None), cols), cut(base + 2 * FT, FT))
    for store in stores:
        store.wait()


def finish(red, kvgrad, norm, states, passed):
    vm = pl.BlockSpec(memory_space=pltpu.VMEM)
    anywhere = pl.BlockSpec(memory_space=pl.ANY)
    shapes = [jax.ShapeDtypeStruct(value.shape, value.dtype) for value in passed]
    shapes += [jax.ShapeDtypeStruct((1, 1), F32)]
    shapes += [jax.ShapeDtypeStruct(value.shape, F32) for value in states]
    return pl.pallas_call(
        finish_kernel,
        out_shape=tuple(shapes),
        in_specs=[vm] * 24 + [anywhere] * 3,
        out_specs=tuple([anywhere] * 3 + [pl.BlockSpec(memory_space=pltpu.SMEM)] + [vm] * 21),
        scratch_shapes=[pltpu.VMEM((128, 128), F32), pltpu.SemaphoreType.DMA((6,))]
        + [pltpu.VMEM(value.shape, value.dtype) for value in passed],
        name="finish",
        compiler_params=pltpu.CompilerParams(vmem_limit_bytes=VMEM_BYTES),
    )(red, kvgrad, norm, *states, *passed)


def pack_weights(gains, self_proj, query, keyval, out_proj, mlp_input, mlp_output):
    rows = gains.shape[1]
    turned_out = jnp.swapaxes(out_proj, 1, 2)
    turned_down = mlp_output.T
    pieces = [jnp.pad(gains.T, ((0, 0), (0, 125)))]
    pieces += [self_proj[0], self_proj[1], self_proj[2], keyval[0], keyval[1]]
    pieces += [turned_out[0], query, turned_out[1]]
    for tile in range(FH // FT):
        columns = slice(tile * FT, (tile + 1) * FT)
        pieces += [mlp_input[0][:, columns], mlp_input[1][:, columns], turned_down[:, columns]]
    return jnp.concatenate([piece.astype(BF) for piece in pieces], axis=1)


def unpack_grads(red):
    def cut(start, width):
        return red[:, start : start + width]

    gains = cut(GAIN, 3).T
    self_proj = jnp.stack([cut(CQ + i * HALF, HALF) for i in range(3)])
    keyval = jnp.stack([cut(CKV + i * HALF, HALF) for i in range(2)])
    query = cut(CQC, HALF)
    out_proj = jnp.stack([cut(COS, HALF).T, cut(COC, HALF).T])
    tiles = FH // FT
    mlp = [jnp.concatenate([cut(CM + (3 * tile + k) * FT, FT) for tile in range(tiles)], axis=1) for k in range(3)]
    return gains, self_proj, query, keyval, out_proj, jnp.stack(mlp[:2]), mlp[2].T


def per_device(
    tokens, memory, cotangent, patch_item, patch_mask, text_item, text_len,
    norm_gains, gains_mean, gains_square,
    self_proj, self_proj_mean, self_proj_square,
    query_cross, query_cross_mean, query_cross_square,
    keyval_cross, keyval_cross_mean, keyval_cross_square,
    out_proj, out_proj_mean, out_proj_square,
    mlp_input, mlp_input_mean, mlp_input_square,
    mlp_output, mlp_output_mean, mlp_output_square,
):
    count = lax.axis_size("dp")
    direct = count == 16
    ints = (patch_item, patch_mask, text_item, text_len)
    states = [
        norm_gains, gains_mean, gains_square,
        self_proj, self_proj_mean, self_proj_square,
        query_cross, query_cross_mean, query_cross_square,
        keyval_cross, keyval_cross_mean, keyval_cross_square,
        out_proj, out_proj_mean, out_proj_square,
        mlp_input, mlp_input_mean, mlp_input_square,
        mlp_output, mlp_output_mean, mlp_output_square,
    ]
    if direct:
        for i in range(12, 15):
            states[i] = jnp.swapaxes(states[i], 1, 2)
        for i in range(18, 21):
            states[i] = states[i].T
        output, tokens_grad, memory_grad, red, kvgrad, norm = layer(
            True, tokens, cotangent, *ints, memory, states[::3]
        )
        results = list(finish(red, kvgrad, norm, states, (output, tokens_grad, memory_grad)))
        results[3] = results[3].reshape(())
        for i in range(16, 19):
            results[i] = jnp.swapaxes(results[i], 1, 2)
        for i in range(22, 25):
            results[i] = results[i].T
        return tuple(results)
    keyval_own = lax.all_to_all(keyval_cross.astype(BF), "head", split_axis=2, concat_axis=1, tiled=True)
    pack = pack_weights(norm_gains, self_proj, query_cross, keyval_own, out_proj, mlp_input, mlp_output)
    wall = lax.all_gather(pack, "dp", axis=0, tiled=True).reshape(BLOCKS + (BLOCK, PACK))
    output, tokens_grad, memory_grad, dwall = layer(False, tokens, cotangent, *ints, memory, (wall,))
    red = lax.psum_scatter(dwall.reshape(D, PACK).astype(F32), "dp", scatter_dimension=0, tiled=True)
    squares = jnp.sum(red[:, 128:] ** 2)
    squares = squares + jnp.where(lax.axis_index("head") == 0, jnp.sum(red[:, :128] ** 2), 0.0)
    total = lax.psum(squares, ("dp", "head"))
    gains_g, self_g, query_g, keyval_g, out_g, input_g, output_g = unpack_grads(red)
    keyval_g = lax.all_to_all(keyval_g, "head", split_axis=1, concat_axis=2, tiled=True)
    grad_norm = jnp.sqrt(total)
    factor = jnp.minimum(1.0, CLIP / (grad_norm + NORM_EPS))
    results = [output, tokens_grad, memory_grad, grad_norm]
    grads = (gains_g, self_g, query_g, keyval_g, out_g, input_g, output_g)
    for i, (grad, (rate, decay)) in enumerate(zip(grads, RATES)):
        results += adam_step(*states[3 * i : 3 * i + 3], grad * factor, rate, decay)
    return tuple(results)


def solution(mesh):
    in_specs = (
        P("dp", None),
        P(("dp", "head"), None),
        P("dp", None),
        P("dp"),
        P("dp"),
        P("dp"),
        P("dp"),
        P(None, "dp"),
        P(None, "dp"),
        P(None, "dp"),
        P(None, "dp", "head"),
        P(None, "dp", "head"),
        P(None, "dp", "head"),
        P("dp", "head"),
        P("dp", "head"),
        P("dp", "head"),
        P(None, ("dp", "head"), None),
        P(None, ("dp", "head"), None),
        P(None, ("dp", "head"), None),
        P(None, "head", "dp"),
        P(None, "head", "dp"),
        P(None, "head", "dp"),
        P(None, "dp", "head"),
        P(None, "dp", "head"),
        P(None, "dp", "head"),
        P("head", "dp"),
        P("head", "dp"),
        P("head", "dp"),
    )
    out_specs = (
        P("dp", None),
        P("dp", None),
        P(("dp", "head"), None),
        P(),
        P(None, "dp"),
        P(None, "dp"),
        P(None, "dp"),
        P(None, "dp", "head"),
        P(None, "dp", "head"),
        P(None, "dp", "head"),
        P("dp", "head"),
        P("dp", "head"),
        P("dp", "head"),
        P(None, ("dp", "head"), None),
        P(None, ("dp", "head"), None),
        P(None, ("dp", "head"), None),
        P(None, "head", "dp"),
        P(None, "head", "dp"),
        P(None, "head", "dp"),
        P(None, "dp", "head"),
        P(None, "dp", "head"),
        P(None, "dp", "head"),
        P("head", "dp"),
        P("head", "dp"),
        P("head", "dp"),
    )
    return jax.shard_map(
        per_device, mesh=mesh, in_specs=in_specs, out_specs=out_specs, check_vma=False
    )
```

```python
import functools

import jax
import jax.numpy as jnp
from jax import lax
from jax.experimental import pallas as pl
from jax.experimental.pallas import tpu as pltpu
from jax.sharding import PartitionSpec as P

D = 768
HD = 64
FF = 2048
TXT = 256
STEP = 10

BETA1 = 0.9
BETA2 = 0.95
ADAM_EPS = 1e-08
DECAY = 0.1
CLIP = 1.0
NORM_EPS = 1e-06
MASKED = -1e30

MESH = pl.DeviceIdType.MESH
BF = jnp.bfloat16
F32 = jnp.float32
VMEM_BYTES = 63 * 2**20

HALF = D // 2
FT = 256
FH = FF // 2
GAIN = 0
CQ = 128
CKV = CQ + 3 * HALF
COS = CKV + 2 * HALF
CQC = COS + HALF
COC = CQC + HALF
CM = COC + HALF
PACK = CM + 3 * FH


def as_bf(value):
    return value.astype(BF)


def as_f32(value):
    return value.astype(F32)


def nn(left, right):
    return lax.dot_general(left, right, (((1,), (0,)), ((), ())), preferred_element_type=F32)


def nt(left, right):
    return lax.dot_general(left, right, (((1,), (1,)), ((), ())), preferred_element_type=F32)


def tn(left, right):
    return lax.dot_general(left, right, (((0,), (0,)), ((), ())), preferred_element_type=F32)


BLOCKS = (2, 2, 2, 2)
BLOCK = D // 16


def middle(low, high):
    return low + (high - low) // 256 * 128 if high - low >= 256 else high


class Links:
    def __init__(self):
        self.me, self.head = lax.axis_index("dp"), lax.axis_index("head")
        self.x, self.y = self.me & 1, (self.me >> 1) & 1
        self.z0, self.z1 = (self.me >> 2) & 1, self.me >> 3
        self.to_x, self.to_y, self.to_z0, self.to_z1 = [(self.me ^ bit, self.head) for bit in (1, 2, 4, 8)]
        self.to_core = (self.me, 1 - self.head)

    def hops(self, slots, more):
        first = [
            (d, (self.me ^ (((d >> 2) & 1) * 8 + ((d >> 1) & 1) * 4), self.head ^ (d & 1))) for d in range(1, 8)
        ]
        second = [(d, (self.me ^ d, self.head)) for d in range(1, 4)]
        return (
            (slots, self.z1 * 4 + self.z0 * 2 + self.head, first),
            (more, self.y * 2 + self.x, second),
        )

    def peers(self):
        return [device for _, _, devices in self.hops(None, None) for _, device in devices]


def remote(source, target, send, recv, device):
    return pltpu.make_async_remote_copy(
        src_ref=source, dst_ref=target, send_sem=send, recv_sem=recv, device_id=device, device_id_type=MESH
    )


GATHER = (
    (0, 384, True),
    (384, 768, True),
    (768, 1280, False),
    (1280, 2048, True),
    (2048, 3200, True),
    (3200, 3968, True),
    (3968, 4736, True),
    (4736, 5504, True),
    (5504, 6272, False),
)

SCATTER = (
    (3200, 3968, False),
    (3968, 4736, False),
    (4736, 5504, False),
    (5504, 6272, True),
    (2816, 3200, True),
    (1280, 2048, False),
    (2432, 2816, False),
    (2048, 2432, False),
    (128, 512, False),
    (512, 896, True),
    (896, 1280, False),
    (0, 128, False),
)

SCHEDULE = (
    (0, 0, 0), (0, 1, 0), (0, 2, 0), 1, (0, 8, 0), 2, 0, (0, 3, 0), (0, 2, 1), (0, 0, 1), (0, 4, 0),
    (0, 8, 1), (0, 1, 1), (0, 0, 2), (0, 3, 1), (0, 2, 2), (0, 1, 2), (0, 0, 3), (0, 3, 2), (0, 4, 1),
    (0, 0, 4), (0, 5, 0), (0, 1, 3), (0, 2, 3), (0, 4, 2), (0, 1, 4), (0, 5, 1), (0, 3, 3), (0, 6, 0),
    (0, 2, 4), 3, 4, (0, 4, 3), (0, 7, 0), 5, 6, (0, 3, 4), (0, 5, 2), (0, 6, 1), 7, (0, 8, 2), 8, (0, 4, 4),
    9, (0, 6, 2), 10, 11, (0, 7, 1), 12, (0, 5, 3), 13, (0, 7, 2), 14, (0, 8, 3), 15, (0, 5, 4), 16,
    (0, 6, 3), 17, (0, 7, 3), 18, 19, (0, 6, 4), (1, 0, 0), 20, (0, 7, 4), (0, 8, 4), (1, 1, 0), 21,
    (1, 0, 1), 22, (1, 3, 0), 23, (1, 1, 1), 24, 25, 26, (1, 4, 0), (1, 2, 0), 27, 28, (1, 3, 1), (1, 2, 1),
    29, 30, (1, 1, 2), 31, 32, (1, 0, 2), 33, (1, 6, 0), 34, (1, 4, 1), (1, 7, 0), 35, (1, 3, 2), (1, 2, 2),
    (1, 6, 1), 36, (1, 3, 3), (1, 1, 3), 37, (1, 7, 1), (1, 0, 3), 38, (1, 6, 2), (1, 4, 2), (1, 3, 4),
    (1, 5, 0), 39, (1, 1, 4), (1, 2, 3), 40, (1, 7, 2), (1, 4, 3), 41, (1, 0, 4), (1, 8, 0), (1, 6, 3), 42,
    (1, 9, 0), 43, (1, 10, 0), (1, 5, 1), (1, 4, 4), (1, 2, 4), 44, (1, 6, 4), (1, 7, 3), (1, 10, 1),
    (1, 9, 1), (1, 7, 4), (1, 11, 0), (1, 5, 2), (1, 8, 1), (1, 10, 2), (1, 11, 1), (1, 5, 3), (1, 9, 2),
    (1, 8, 2), (1, 10, 3), (1, 11, 2), (1, 9, 3), (1, 8, 3), (1, 5, 4), (1, 9, 4), (1, 11, 3), (1, 10, 4),
    (1, 8, 4), (1, 11, 4),
)


class Gather:
    def __init__(self, links, wall, send_sem, recv_sem):
        self.links, self.wall, self.send_sem, self.recv_sem = links, wall, send_sem, recv_sem

    def where(self, n, k, received):
        low, high, z_first = GATHER[n]
        half = middle(low, high)
        links, every = self.links, slice(None)
        z1, z0, y, x = links.z1, links.z0, links.y, links.x
        flip = (lambda v: 1 - v) if received else (lambda v: v)
        if z_first:
            index, cols, device = (
                ((flip(z1), z0, y, x), (low, high), links.to_z1),
                ((every, flip(z0), y, x), (low, high), links.to_z0),
                ((every, every, y, flip(x)), (low, high), links.to_x),
                ((every, every, flip(y), x), (low, high), links.to_y),
                ((every, every, flip(y), 1 - x), (low, half), links.to_y),
                ((every, every, 1 - y, flip(x)), (half, high), links.to_x),
            )[k]
        else:
            index, cols, device = (
                ((z1, z0, y, flip(x)), (low, high), links.to_x),
                ((z1, z0, flip(y), x), (low, high), links.to_y),
                ((z1, z0, flip(y), 1 - x), (low, half), links.to_y),
                ((z1, z0, 1 - y, flip(x)), (half, high), links.to_x),
                ((flip(z1), z0, every, every), (low, high), links.to_z1),
                ((every, flip(z0), every, every), (low, high), links.to_z0),
            )[k]
        return self.wall.at[index + (every, slice(*cols))], device

    def copy(self, n, k, received=False):
        ref, device = self.where(n, k, received)
        return remote(ref, ref, self.send_sem.at[n, k], self.recv_sem.at[n, k], device)

    def step(self, n, number):
        if GATHER[n][2]:
            plan = ((None, 0),), ((0, 1),), ((1, 2), (None, 3)), ((2, 4), (3, 5)), ((4, None), (5, None))
        else:
            plan = ((None, 0), (None, 1)), ((0, 2), (1, 3)), ((2, None), (3, 4)), ((4, 5),), ((5, None),)
        for wait, start in plan[number]:
            if wait is not None:
                self.copy(n, wait, True).wait_recv()
            if start is not None:
                self.copy(n, start).start()

    def sent(self, n):
        for k in range(6):
            self.copy(n, k).wait_send()


class Scatter:
    def __init__(self, links, wall, slot1, slot2, slot3, red, send_sem, recv_sem):
        self.links, self.wall, self.red = links, wall, red
        self.slot1, self.slot2, self.slot3 = slot1, slot2, slot3
        self.send_sem, self.recv_sem = send_sem, recv_sem

    def skipped(self, n):
        low, high, z_first = SCATTER[n]
        return (3 if z_first else 1,) if middle(low, high) == high else ()

    def copy(self, n, k):
        low, high, z_first = SCATTER[n]
        half = middle(low, high)
        links, every = self.links, slice(None)
        z1, z0, y, x = links.z1, links.z0, links.y, links.x
        slot1, slot2, slot3 = self.slot1, self.slot2, self.slot3
        if z_first:
            index, slot, place, cols, device = (
                ((every, 1 - z0, every, every), slot2, (every,) * 3, (low, high), links.to_z0),
                ((1 - z1, z0, every, every), slot1, (every,) * 2, (low, high), links.to_z1),
                ((z1, z0, 1 - y, 1 - x), slot3, (0,), (low, half), links.to_y),
                ((z1, z0, 1 - y, 1 - x), slot3, (0,), (half, high), links.to_x),
                ((z1, z0, y, 1 - x), slot3, (1,), (low, high), links.to_x),
                ((z1, z0, 1 - y, x), slot3, (2,), (low, high), links.to_y),
            )[k]
        else:
            index, slot, place, cols, device = (
                ((every, every, 1 - y, 1 - x), slot1, (every,) * 2, (low, half), links.to_y),
                ((every, every, 1 - y, 1 - x), slot1, (every,) * 2, (half, high), links.to_x),
                ((every, every, y, 1 - x), slot2, (0, every, every), (low, high), links.to_x),
                ((every, every, 1 - y, x), slot2, (1, every, every), (low, high), links.to_y),
                ((every, 1 - z0, y, x), slot3, (slice(0, 2),), (low, high), links.to_z0),
                ((1 - z1, z0, y, x), slot3, (2,), (low, high), links.to_z1),
            )[k]
        tail = (every, slice(*cols))
        return remote(
            self.wall.at[index + tail], slot.at[place + tail], self.send_sem.at[n, k], self.recv_sem.at[n, k], device
        )

    def add(self, index, *others):
        self.wall[index] = as_bf(sum((as_f32(ref[at]) for ref, at in others), as_f32(self.wall[index])))

    def step(self, n, number):
        low, high, z_first = SCATTER[n]
        half = middle(low, high)
        links, every = self.links, slice(None)
        z1, z0, y, x = links.z1, links.z0, links.y, links.x
        slot1, slot2, slot3 = self.slot1, self.slot2, self.slot3
        cols, left, right = (every, slice(low, high)), (every, slice(low, half)), (every, slice(half, high))
        groups = ((0,), (1,), (2, 3), (4, 5)) if z_first else ((0, 1), (2, 3), (4,), (5,))
        skipped = self.skipped(n)
        if number > 0:
            for k in groups[number - 1]:
                if k not in skipped:
                    self.copy(n, k).wait_recv()
        if number == 4:
            value = as_f32(self.wall[(z1, z0, y, x) + cols])
            for k in (1, 2) if z_first else (2,):
                value = value + as_f32(slot3[(k,) + cols])
            self.red[:, low:high] = value
        elif z_first and number == 1:
            for a in range(2):
                for b in range(2):
                    for c in range(2):
                        self.add((a, z0, b, c) + cols, (slot2, (a, b, c) + cols))
        elif z_first and number == 2:
            for b in range(2):
                for c in range(2):
                    self.add((z1, z0, b, c) + cols, (slot1, (b, c) + cols))
        elif z_first and number == 3:
            self.add((z1, z0, y, 1 - x) + left, (slot3, (0,) + left))
            if half < high:
                self.add((z1, z0, 1 - y, x) + right, (slot3, (0,) + right))
        elif number == 1:
            for a in range(2):
                for b in range(2):
                    self.add((a, b, y, 1 - x) + left, (slot1, (a, b) + left))
                    if half < high:
                        self.add((a, b, 1 - y, x) + right, (slot1, (a, b) + right))
        elif number == 2:
            for a in range(2):
                for b in range(2):
                    self.add((a, b, y, x) + cols, (slot2, (0, a, b) + cols), (slot2, (1, a, b) + cols))
        elif number == 3:
            for a in range(2):
                self.add((a, z0, y, x) + cols, (slot3, (a,) + cols))
        if number < 4:
            for k in groups[number]:
                if k not in skipped:
                    self.copy(n, k).start()

    def sent(self):
        for n in range(len(SCATTER)):
            for k in range(6):
                if k not in self.skipped(n):
                    self.copy(n, k).wait_send()


class Exchange:
    def __init__(self, links, send, recv, send_sem, recv_sem):
        self.links = links
        self.send, self.recv, self.send_sem, self.recv_sem = send, recv, send_sem, recv_sem

    def copy(self, number):
        slot = number % 2
        return remote(
            self.send.at[slot],
            self.recv.at[slot],
            self.send_sem.at[number],
            self.recv_sem.at[number],
            self.links.to_core,
        )

    def start(self, number, value):
        self.send[number % 2] = as_bf(value)
        self.copy(number).start()

    def wait(self, number):
        self.copy(number).wait()

    def total(self, number, rows=slice(None)):
        slot = number % 2
        return as_f32(self.send[slot, rows]) + as_f32(self.recv[slot, rows])


def inverse_rms(values):
    return lax.rsqrt(jnp.mean(values * values, axis=-1, keepdims=True) + NORM_EPS)


def norm_back(values, gain, grad):
    inverse = inverse_rms(values)
    scaled = grad * gain
    inner = jnp.mean(scaled * values, axis=-1, keepdims=True)
    grad_values = inverse * scaled - values * (inverse * inverse * inverse * inner)
    grad_gain = jnp.sum(grad * values * inverse, axis=0, keepdims=True)
    return grad_values, grad_gain


def layer_kernel(direct, *refs):
    (tok_in, cot_in, item, pmask, titem, tlen, memory), refs = refs[:7], refs[7:]
    if direct:
        (gshard, sproj_in, query_in, keyval, tout_in, minput_in, tdown_in), refs = refs[:7], refs[7:]
        (out_to, tgrad_to, mgrad, red, kvgrad, norm), refs = refs[:6], refs[6:]
    else:
        (wall,), refs = refs[:1], refs[1:]
        (out_to, tgrad_to, mgrad, dwall), refs = refs[:4], refs[4:]
    (
        ws, mem, gains, dgains, cbias, sbias, n1, n2, n3, x1, x2,
        q3, k3, v3, o3, oT, qc3, oc3, ocT, do3, dqc3, sexps, slinv,
        kext, mv3, mT, st, eb, clse, acc,
        esend, erecv, osend, orecv, mrecv,
        tok, cot, out, tgrad, send_sem, recv_sem, side_sem, wsem, msem,
    ), refs = refs[:44], refs[44:]
    links = Links()
    head, other = links.head, links.to_core

    barrier = pltpu.get_barrier_semaphore()
    peers = links.peers() if direct else [other]
    for device in peers:
        pl.semaphore_signal(barrier, inc=1, device_id=device, device_id_type=MESH)
    load_tok = pltpu.make_async_copy(tok_in, tok, wsem.at[2])
    load_cot = pltpu.make_async_copy(cot_in, cot, wsem.at[3])
    store_out = pltpu.make_async_copy(out, out_to, wsem.at[4])
    store_tgrad = pltpu.make_async_copy(tgrad, tgrad_to, wsem.at[5])
    own_memory = pltpu.make_async_copy(memory, mem.at[head], wsem.at[0])
    mem_copy = remote(memory, mem.at[head], side_sem.at[0], side_sem.at[1], other)
    if direct:
        sproj, query, tout, minput, tdown, refs = *refs[:5], refs[5:]
        slot1, slot2, slot3, kvs, kvr, kgs, kgr, sums, others, g_send, g_recv, s_send, s_recv, t_send, t_recv, l_sem = refs
        pairs_in = ((sproj_in, sproj), (tout_in, tout), (query_in, query), (minput_in, minput), (tdown_in, tdown))
        loads = [pltpu.make_async_copy(source, target, l_sem.at[i]) for i, (source, target) in enumerate(pairs_in)]
        for load in loads:
            load.start()
        load_tok.start()
        own_memory.start()
        load_cot.start()
        gather = Gather(links, ws, g_send, g_recv)
        scatter = Scatter(links, ws, slot1, slot2, slot3, red, s_send, s_recv)
        here = (links.z1, links.z0, links.y, links.x, slice(None))

        def own(column, value):
            ws[here + (slice(column, column + value.shape[1]),)] = as_bf(value)

        for k in range(2):
            kvs[k] = jnp.where(head == 0, keyval[k, :, HALF:], keyval[k, :, :HALF])
        dgains[...] = jnp.zeros_like(dgains)
        dgains[0:3, 0:BLOCK] = gshard[...]
        own(GAIN, dgains[:, 0:128].T[0:BLOCK])
        loads[0].wait()
        for i in range(3):
            own(CQ + i * HALF, sproj[i])
        pl.semaphore_wait(barrier, len(peers))
        kv_copy = remote(kvs, kvr, side_sem.at[4], side_sem.at[5], other)
        kv_copy.start()

        def pack_rest():
            loads[3].wait()
            loads[4].wait()
            for f in range(FH // FT):
                base = CM + f * 3 * FT
                for k in range(2):
                    own(base + k * FT, minput[k, :, f * FT : (f + 1) * FT])
                own(base + 2 * FT, tdown[:, f * FT : (f + 1) * FT])

        def pack_heads():
            loads[1].wait()
            loads[2].wait()
            own(COS, tout[0])
            own(CQC, query[...])
            own(COC, tout[1])
            mem_copy.start()
            kv_copy.wait()
            for k in range(2):
                mine = jnp.where(head == 0, keyval[k, :, :HALF], keyval[k, :, HALF:])
                top, bottom = jnp.where(head == 0, mine, kvr[k]), jnp.where(head == 0, kvr[k], mine)
                own(CKV + k * HALF, jnp.concatenate([top, bottom], axis=0))
    else:
        pl.semaphore_wait(barrier, len(peers))
        load_tok.start()
        own_memory.start()
        load_cot.start()
        load = pltpu.make_async_copy(wall, ws, wsem.at[1])
        load.start()
        mem_copy.start()
        load.wait()

    ex = Exchange(links, esend, erecv, send_sem, recv_sem)

    def w(column, width):
        return ws[:, :, :, :, :, column : column + width].reshape(D, width)

    def put(column, value):
        width = value.shape[1]
        ws[:, :, :, :, :, column : column + width] = as_bf(value).reshape(BLOCKS + (BLOCK, width))

    def sent(column):
        if direct:
            for n, (low, high, _) in enumerate(GATHER):
                if low <= column < high and n not in done:
                    done.add(n)
                    gather.sent(n)

    done = set()
    half_rows = mem.shape[1]
    patches = 2 * half_rows
    lane = lax.broadcasted_iota(jnp.int32, (TXT, 128), 1)
    mask = [as_bf(jnp.where(lane < HD, 1.0, 0.0)), as_bf(jnp.where(lane < HD, 0.0, 1.0))]
    texts = [slice(0, TXT), slice(TXT, 2 * TXT)]
    pairs = 3
    pieces = []

    def piece(*numbers):
        def keep(function):
            pieces.append(functools.partial(function, *numbers))
            return function

        return keep

    def joined(ref, rows=slice(None)):
        return jnp.concatenate([ref[j, rows] for j in range(pairs)], axis=1)

    def spread(target, rows, value):
        for j in range(pairs):
            target[j, rows] = value[:, j * 128 : (j + 1) * 128]

    pieces += [pack_heads, pack_rest] if direct else [None, None]

    @piece()
    def _():
        row = lax.broadcasted_iota(jnp.int32, (128, 512), 0)
        for c in range(patches // 512):
            cols = slice(c * 512, (c + 1) * 512)
            place = jnp.where(row == 0, titem[0], jnp.where(row == 1, titem[1], -1))
            seen = (place == item[:, cols]) & (pmask[:, cols] == 1)
            cbias[cols] = as_bf(jnp.where(seen, 0.0, jnp.where(row < 2, MASKED, 0.0)).T)
        key = lax.broadcasted_iota(jnp.int32, (TXT, TXT), 0)
        slot = lax.broadcasted_iota(jnp.int32, (TXT, TXT), 1)
        for t in range(2):
            sbias[t] = as_bf(jnp.where((key <= slot) & (key < tlen[t]), 0.0, MASKED))
        dgains[...] = jnp.zeros_like(dgains)
        acc[...] = jnp.zeros_like(acc)
        tgrad[...] = jnp.zeros_like(tgrad)

    @piece()
    def _():
        load_tok.wait()
        gains[...] = as_f32(w(0, 128)).T[0:8]
        for rows in texts:
            x = as_f32(tok[rows])
            n1[rows] = as_bf(x * inverse_rms(x) * gains[0:1])
        for number, target in enumerate((q3, k3, v3)):
            value = as_bf(nn(n1[...], w(CQ + number * HALF, HALF)))
            if number == 0:
                value = value * jnp.asarray(HD**-0.5, BF)
            spread(target, slice(None), value)

    def self_forward(j):
        for t in range(2):
            query_pair, key_pair = q3[j, texts[t]], k3[j, texts[t]]
            turned = v3[j, texts[t]].T
            parts = []
            for a in range(2):
                scores = nt(key_pair, query_pair * mask[a]) + as_f32(sbias[t])
                top = jnp.max(scores, axis=0, keepdims=True)
                expo = jnp.exp(scores - top)
                low = as_bf(expo)
                sexps[j, t, a] = low
                inverse = 1.0 / jnp.sum(expo, axis=0, keepdims=True)
                slinv[j, t, a] = jnp.broadcast_to(inverse, (8, TXT))
                parts.append(nn(turned[a * HD : (a + 1) * HD], low) * inverse)
            both = jnp.concatenate(parts, axis=0)
            oT[j, t] = as_bf(both)
            o3[j, texts[t]] = as_bf(both.T)

    for j in range(pairs):
        piece(j)(self_forward)

    def project(side):
        if side == 0:
            own_memory.wait()
            mem_copy.wait_send()
            remote(memory, mem.at[1 - head], side_sem.at[0], side_sem.at[1], other).wait_recv()
        for c in range(half_rows // 512):
            part = slice(c * 512, (c + 1) * 512)
            rows = slice(side * half_rows + c * 512, side * half_rows + (c + 1) * 512)
            both = as_bf(nn(mem[side, part], w(CKV, 2 * HALF)))
            for j in range(pairs):
                kext[j, rows, 0:128] = both[:, j * 128 : (j + 1) * 128]
                kext[j, rows, 128:256] = cbias[rows]
                mv3[j, rows] = both[:, HALF + j * 128 : HALF + (j + 1) * 128]
        side_rows = slice(side * half_rows, (side + 1) * half_rows)
        for j in range(pairs):
            mT[j, :, side_rows] = mv3[j, side_rows].T

    for side in range(2):
        piece(side)(project)

    @piece()
    def _():
        ex.start(0, nt(joined(o3), w(COS, HALF)))

    @piece()
    def _():
        ex.wait(0)
        for rows in texts:
            value = as_f32(tok[rows]) + ex.total(0, rows)
            x1[rows] = value
            n2[rows] = as_bf(value * inverse_rms(value) * gains[1:2])
        spread(qc3, slice(None), as_bf(nn(n2[...], w(CQC, HALF))) * jnp.asarray(HD**-0.5, BF))

    big, small = 512, 128

    def eb_at(a, start, size):
        return (2 * a + start // half_rows, slice(start % half_rows, start % half_rows + size))

    def eb_all(a):
        return eb[2 * a : 2 * a + 2].reshape(patches, TXT)

    def wide_query(j, t, a):
        pick = as_bf(jnp.where(lane == t, 1.0, 0.0))
        return jnp.concatenate([qc3[j, texts[t]] * mask[a], pick], axis=1)

    def cross_forward(j, t):
        parts = []
        for a in range(2):
            wide = wide_query(j, t, a)
            top = jnp.full((8, TXT), -3e38, F32)
            for c in range(patches // big):
                scores = nt(kext[j, c * big : (c + 1) * big], wide)
                st[c * big : (c + 1) * big] = scores
                top = jnp.maximum(top, jnp.max(scores.reshape(big // 8, 8, TXT), axis=0))
            top = jnp.max(top, axis=0, keepdims=True)
            total = jnp.zeros((8, TXT), F32)
            for c in range(patches // small):
                expo = jnp.exp(st[c * small : (c + 1) * small] - top)
                total = total + jnp.sum(expo.reshape(small // 8, 8, TXT), axis=0)
                eb[eb_at(a, c * small, small)] = as_bf(expo)
            total = jnp.sum(total, axis=0, keepdims=True)
            clse[j, t, a] = jnp.broadcast_to(top + jnp.log(total), (8, TXT))
            parts.append(nn(mT[j, a * HD : (a + 1) * HD], eb_all(a)) * (1.0 / total))
        both = jnp.concatenate(parts, axis=0)
        ocT[j, t] = as_bf(both)
        oc3[j, texts[t]] = as_bf(both.T)

    for j in range(pairs):
        for t in range(2):
            piece(j, t)(cross_forward)

    @piece()
    def _():
        ex.start(1, nt(joined(oc3), w(COC, HALF)))
        for j in range(pairs):
            mT[j] = kext[j, :, 0:128].T

    @piece()
    def _():
        ex.wait(1)
        for rows in texts:
            value = x1[rows] + ex.total(1, rows)
            x2[rows] = value
            n3[rows] = as_bf(value * inverse_rms(value) * gains[2:3])

    root = (2.0 / jnp.pi) ** 0.5

    def mlp(f):
        if f == 0:
            load_cot.wait()
        base = CM + f * (3 * FT)
        gate_w, up_w, down_w = (w(base + k * FT, FT) for k in range(3))
        for rows in texts:
            gate, up = nn(n3[rows], gate_w), nn(n3[rows], up_w)
            grad = nn(cot[rows], down_w)
            square = gate * gate
            tanh = jnp.tanh(root * gate * (1.0 + 0.044715 * square))
            half = 0.5 * (1.0 + tanh)
            slope = half + 0.5 * gate * (1.0 - tanh * tanh) * (root * (1.0 + 3 * 0.044715 * square))
            active = gate * half
            osend[rows, 0:FT] = as_bf(active * up)
            osend[rows, FT : 2 * FT] = as_bf(grad * up * slope)
            osend[rows, 2 * FT : 3 * FT] = as_bf(grad * active)
        for rows in texts:
            acc[rows] += nt(osend[rows, 0:FT], down_w)
            tgrad[rows] += nt(osend[rows, FT : 2 * FT], gate_w) + nt(osend[rows, 2 * FT : 3 * FT], up_w)
        sent(base)
        put(base, tn(n3[...], osend[:, FT : 2 * FT]))
        put(base + FT, tn(n3[...], osend[:, 2 * FT : 3 * FT]))
        put(base + 2 * FT, tn(cot[...], osend[:, 0:FT]))

    for f in range(FH // FT):
        piece(f)(mlp)

    side = remote(osend, orecv, side_sem.at[2], side_sem.at[3], other)

    @piece()
    def _():
        ex.start(2, tgrad[...])
        osend[...] = as_bf(acc[...])
        side.start()

    @piece()
    def _():
        ex.wait(2)
        for rows in texts:
            grad, grad_gain = norm_back(x2[rows], gains[2:3], ex.total(2, rows))
            value = as_f32(cot[rows]) + grad
            acc[rows] = x2[rows]
            x2[rows] = value
            dgains[2:3] += grad_gain
            back = as_bf(value)
            n3[rows] = back
            spread(do3, rows, as_bf(nn(back, w(COC, HALF))))
        sent(COC)
        put(COC, tn(n3[...], joined(oc3)))
        side.wait()
        for rows in texts:
            out[rows] = as_bf(acc[rows] + (as_f32(osend[rows]) + as_f32(orecv[rows])))
        store_out.start()

    def cross_back(j, t):
        rows = texts[t]
        grad = do3[j, rows].T
        attended = as_f32(ocT[j, t])
        parts = []
        for a in range(2):
            keep = grad[a * HD : (a + 1) * HD]
            inner = jnp.sum(as_f32(keep) * attended[a * HD : (a + 1) * HD], axis=0, keepdims=True)
            empty = jnp.zeros_like(keep)
            low = jnp.concatenate([keep, empty] if a == 0 else [empty, keep], axis=0)
            wide = wide_query(j, t, a)
            lse = clse[j, t, a, 0:1]
            for c in range(patches // big):
                keys = slice(c * big, (c + 1) * big)
                probs = jnp.exp(nt(kext[j, keys], wide) - lse)
                eb[eb_at(0, c * big, big)] = as_bf(probs)
                eb[eb_at(1, c * big, big)] = as_bf(probs * (nn(mv3[j, keys], low) - inner))
            for c in range(patches // big):
                keys = slice(c * big, (c + 1) * big)
                grad_value = nt(eb[eb_at(0, c * big, big)], low)
                grad_key = nn(eb[eb_at(1, c * big, big)], wide[:, 0:128])
                if t == 0 and a == 0:
                    st[keys, 0:128] = grad_value
                    st[keys, 128:256] = grad_key
                else:
                    st[keys, 0:128] += grad_value
                    st[keys, 128:256] += grad_key
            parts.append(nn(mT[j, a * HD : (a + 1) * HD], eb_all(1)))
        dqc3[j, rows] = as_bf((jnp.concatenate(parts, axis=0) * HD**-0.5).T)
        if t == 1:
            mv3[j] = as_bf(st[:, 0:128])
            kext[j, :, 0:128] = as_bf(st[:, 128:256])

    for j in range(pairs):
        for t in range(2):
            piece(j, t)(cross_back)

    @piece()
    def _():
        ex.start(3, nt(joined(dqc3), w(CQC, HALF)))

    def memory_back(c, start):
        rows = pl.ds(pl.multiple_of(start + c * 256, 256), 256)
        both = jnp.concatenate(
            [kext[j, rows, 0:128] for j in range(pairs)] + [mv3[j, rows] for j in range(pairs)], axis=1
        )
        return nt(both, w(CKV, 2 * HALF))

    mside = remote(eb.at[0:3], mrecv, side_sem.at[6], side_sem.at[7], other)

    @piece()
    def _():
        def send_part(c, carry):
            value = as_bf(memory_back(c, (1 - head) * half_rows))
            for k in range(3):
                eb[k, pl.ds(pl.multiple_of(c * 256, 256), 256)] = value[:, k * TXT : (k + 1) * TXT]
            return carry

        lax.fori_loop(0, half_rows // 256, send_part, 0)
        mside.start()

    @piece()
    def _():
        sent(CQC)
        put(CQC, tn(n2[...], joined(dqc3)))
        ex.wait(3)

    @piece()
    def _():
        for rows in texts:
            grad, grad_gain = norm_back(x1[rows], gains[1:2], ex.total(3, rows))
            value = x2[rows] + grad
            x1[rows] = value
            dgains[1:2] += grad_gain
            back = as_bf(value)
            n3[rows] = back
            spread(do3, rows, as_bf(nn(back, w(COS, HALF))))
        sent(COS)
        put(COS, tn(n3[...], joined(o3)))

    stores = []

    @piece()
    def _():
        mside.wait()
        for c in range(half_rows // 256):
            if c >= 2:
                stores[c - 2].wait()
            slot_rows = slice((c % 2) * 256, (c % 2 + 1) * 256)
            part = slice(c * 256, (c + 1) * 256)
            peer_part = jnp.concatenate([mrecv[k, part] for k in range(3)], axis=1)
            acc[slot_rows] = memory_back(c, head * half_rows) + as_f32(peer_part)
            store = pltpu.make_async_copy(acc.at[slot_rows], mgrad.at[pl.ds(c * 256, 256)], msem.at[c])
            store.start()
            stores.append(store)

    @piece()
    def _():
        sent(CKV)
        for number, source in enumerate((kext, mv3)):
            total = jnp.zeros((D, HALF), F32)
            for c in range(patches // 512):
                rows = slice(c * 512, (c + 1) * 512)
                part = slice(c * 512 % half_rows, c * 512 % half_rows + 512)
                both = jnp.concatenate([source[j, rows, 0:128] for j in range(pairs)], axis=1)
                total = total + tn(mem[c * 512 // half_rows, part], both)
            put(CKV + number * HALF, total)

    def self_back(j):
        for t in range(2):
            rows = texts[t]
            grad = as_f32(do3[j, rows]).T
            attended = as_f32(oT[j, t])
            query_pair, key_pair, value_pair = q3[j, rows], k3[j, rows], v3[j, rows]
            key_turned = key_pair.T
            parts = []
            grad_key = jnp.zeros((TXT, 128), F32)
            grad_value = jnp.zeros((TXT, 128), F32)
            for a in range(2):
                keep = as_bf(grad[a * HD : (a + 1) * HD] * slinv[j, t, a, 0:1])
                inner = jnp.sum(as_f32(keep) * attended[a * HD : (a + 1) * HD], axis=0, keepdims=True)
                empty = jnp.zeros_like(keep)
                low = jnp.concatenate([keep, empty] if a == 0 else [empty, keep], axis=0)
                expo = sexps[j, t, a]
                grad_scores = as_bf(as_f32(expo) * (nn(value_pair, low) - inner))
                grad_value = grad_value + nt(expo, low)
                grad_key = grad_key + nn(grad_scores, query_pair * mask[a])
                parts.append(nn(key_turned[a * HD : (a + 1) * HD], grad_scores))
            q3[j, rows] = as_bf((jnp.concatenate(parts, axis=0) * HD**-0.5).T)
            k3[j, rows] = as_bf(grad_key)
            v3[j, rows] = as_bf(grad_value)

    for j in range(pairs):
        piece(j)(self_back)

    @piece()
    def _():
        ex.start(
            4,
            nt(joined(q3), w(CQ, HALF))
            + nt(joined(k3), w(CQ + HALF, HALF))
            + nt(joined(v3), w(CQ + 2 * HALF, HALF)),
        )
        for number in range(3):
            sent(CQ + number * HALF)

    def projection_grad(number):
        put(CQ + number * HALF, tn(n1[...], joined((q3, k3, v3)[number])))

    for number in range(3):
        piece(number)(projection_grad)

    @piece()
    def _():
        ex.wait(4)
        for rows in texts:
            grad, grad_gain = norm_back(as_f32(tok[rows]), gains[0:1], ex.total(4, rows))
            tgrad[rows] = x1[rows] + grad
            dgains[0:1] += grad_gain
        store_tgrad.start()
        sent(GAIN)
        put(GAIN, dgains[...].T)

    kv_group = [n for n, group in enumerate(SCATTER) if group[0] == CKV][0]
    kv_back = remote(kgs, kgr, side_sem.at[8], side_sem.at[9], other) if direct else None

    def send_keyval():
        kgs[...] = jnp.where(head == 0, red[BLOCK // 2 :, CKV:COS], red[: BLOCK // 2, CKV:COS])
        kv_back.start()

    def finish_keyval():
        kv_back.wait()
        mine = jnp.where(head == 0, red[: BLOCK // 2, CKV:COS], red[BLOCK // 2 :, CKV:COS])
        for k in range(2):
            cols = slice(k * HALF, (k + 1) * HALF)
            first, second = mine[:, cols], kgr[:, cols]
            kvgrad[k, :, :HALF] = jnp.where(head == 0, first, second)
            kvgrad[k, :, HALF:] = jnp.where(head == 0, second, first)

    for entry in SCHEDULE if direct else range(2, len(pieces)):
        if isinstance(entry, int):
            pieces[entry]()
        else:
            part, n, number = entry
            (gather, scatter)[part].step(n, number)
            if part == 1 and n == kv_group and number == 4:
                send_keyval()

    if direct:
        if True:
            first = red[:, 0:128]
            first = jnp.sum(first * first, axis=0, keepdims=True)
            value = jnp.where(head == 0, first, jnp.zeros_like(first))
            for column in range(128, PACK, 128):
                part = red[:, column : column + 128]
                value = value + jnp.sum(part * part, axis=0, keepdims=True)
            value = jnp.broadcast_to(jnp.sum(value, axis=1, keepdims=True), (8, 128))
            for hop, (slots, place, peers) in enumerate(links.hops(sums, others)):
                slots[place] = value
                copies = [
                    (
                        remote(slots.at[place], slots.at[place], t_send.at[hop, d], t_recv.at[hop, d], device),
                        remote(slots.at[place ^ d], slots.at[place ^ d], t_send.at[hop, d], t_recv.at[hop, d], device),
                    )
                    for d, device in peers
                ]
                for copy, _ in copies:
                    copy.start()
                if hop == 0:
                    finish_keyval()
                    scatter.sent()
                for copy, arrived in copies:
                    copy.wait_send()
                    arrived.wait_recv()
                value = slots[0]
                for d in range(1, len(peers) + 1):
                    value = value + slots[d]
            norm[...] = value
    else:
        store = pltpu.make_async_copy(ws, dwall, wsem.at[1])
        store.start()
        store.wait()
    for number in (-2, -1):
        stores[number].wait()
    store_out.wait()
    store_tgrad.wait()


def layer(direct, tokens, cotangent, patch_item, patch_mask, text_item, text_len, memory, weights):
    rows, half_rows = tokens.shape[0], memory.shape[0]
    patches = 2 * half_rows
    vm = pl.BlockSpec(memory_space=pltpu.VMEM)
    sm = pl.BlockSpec(memory_space=pltpu.SMEM)
    anywhere = pl.BlockSpec(memory_space=pl.ANY)
    S, DMA = pltpu.VMEM, pltpu.SemaphoreType.DMA
    heads3 = S((3, rows, 128), BF)
    scratch = [
        S(BLOCKS + (BLOCK, PACK), BF), S((2, half_rows, D), BF), S((8, D), F32), S((128, D), F32),
        S((patches, 128), BF), S((2, TXT, TXT), BF),
        S((rows, D), BF), S((rows, D), BF), S((rows, D), BF), S((rows, D), F32), S((rows, D), F32),
        heads3, heads3, heads3, heads3, S((3, 2, 128, TXT), BF), heads3, heads3, S((3, 2, 128, TXT), BF),
        heads3, heads3, S((3, 2, 2, TXT, TXT), BF), S((3, 2, 2, 8, TXT), F32),
        S((3, patches, 256), BF), S((3, patches, 128), BF), S((3, 128, patches), BF),
        S((patches, TXT), F32), S((4, half_rows, TXT), BF), S((3, 2, 2, 8, TXT), F32), S((rows, D), F32),
        S((2, rows, D), BF), S((2, rows, D), BF), S((rows, D), BF), S((rows, D), BF),
        S((3, half_rows, TXT), BF),
        S((rows, D), BF), S((rows, D), BF), S((rows, D), BF), S((rows, D), F32),
        DMA((5,)), DMA((5,)), DMA((10,)), DMA((6,)), DMA((half_rows // 256,)),
    ]
    shapes = [
        jax.ShapeDtypeStruct((rows, D), BF),
        jax.ShapeDtypeStruct((rows, D), F32),
        jax.ShapeDtypeStruct((half_rows, D), F32),
    ]
    if direct:
        scratch += [S(weights[i].shape, F32) for i in (1, 2, 4, 5, 6)]
        scratch += [
            S((2, 2, BLOCK, PACK), BF), S((2, 2, 2, BLOCK, PACK), BF), S((3, BLOCK, PACK), BF),
            S((2, BLOCK // 2, HALF), F32), S((2, BLOCK // 2, HALF), F32),
            S((BLOCK // 2, 2 * HALF), F32), S((BLOCK // 2, 2 * HALF), F32),
            S((8, 8, 128), F32), S((4, 8, 128), F32),
            DMA((len(GATHER), 6)), DMA((len(GATHER), 6)), DMA((len(SCATTER), 6)), DMA((len(SCATTER), 6)),
            DMA((2, 8)), DMA((2, 8)), DMA((5,)),
        ]
        shapes += [
            jax.ShapeDtypeStruct((BLOCK, PACK), F32),
            jax.ShapeDtypeStruct((2, BLOCK // 2, D), F32),
            jax.ShapeDtypeStruct((8, 128), F32),
        ]
        more_in, more_out = [vm, anywhere, anywhere, vm, anywhere, anywhere, anywhere], [vm] * 3
    else:
        shapes += [jax.ShapeDtypeStruct(BLOCKS + (BLOCK, PACK), BF)]
        more_in, more_out = [anywhere], [anywhere]
    return pl.pallas_call(
        functools.partial(layer_kernel, direct),
        out_shape=tuple(shapes),
        in_specs=[anywhere, anywhere, vm, vm, sm, sm, anywhere] + more_in,
        out_specs=tuple([anywhere] * 3 + more_out),
        scratch_shapes=scratch,
        name="layer",
        compiler_params=pltpu.CompilerParams(
            collective_id=1, has_side_effects=True, vmem_limit_bytes=VMEM_BYTES
        ),
    )(
        tokens, cotangent, patch_item.reshape(1, patches), patch_mask.reshape(1, patches),
        text_item, text_len, memory, *weights,
    )


def adam_step(weight, first, second, grad, rate, decay):
    first_new = BETA1 * first + (1.0 - BETA1) * grad
    second_new = BETA2 * second + (1.0 - BETA2) * grad * grad
    mean_hat = first_new / (1.0 - BETA1**STEP)
    square_hat = second_new / (1.0 - BETA2**STEP)
    weight_new = weight - rate * (mean_hat / (jnp.sqrt(square_hat) + ADAM_EPS) + decay * weight)
    return (weight_new, first_new, second_new)


RATES = (
    (0.5, 0.0),
    (2.0 * D**-0.5, DECAY),
    (2.0 * D**-0.5, DECAY),
    (2.0 * D**-0.5, DECAY),
    (2.0 * (D // 16) ** -0.5, DECAY),
    (2.0 * D**-0.5, DECAY),
    (2.0 * FF**-0.5, DECAY),
)


def finish_kernel(*refs):
    (red, kvgrad, norm), refs = refs[:3], refs[3:]
    states_in, refs = refs[:21], refs[21:]
    passed, refs = refs[:3], refs[3:]
    kept, refs = refs[:3], refs[3:]
    (grad_norm,), refs = refs[:1], refs[1:]
    results_to, refs = refs[:21], refs[21:]
    (pad, load_sem, store_sem), held = refs[:3], refs[3:6]
    states, results = refs[6:27], refs[27:48]
    loads = [
        pltpu.make_async_copy(source, target, load_sem.at[i])
        for i, (source, target) in enumerate(zip(states_in + passed, states + held))
    ]
    stores = [
        pltpu.make_async_copy(source, target, store_sem.at[i])
        for i, (source, target) in enumerate(zip(results + held, results_to + kept))
    ]
    order = (23, 22, 21, 15, 16, 17, 18, 19, 20, 3, 4, 5, 12, 13, 14, 9, 10, 11, 6, 7, 8, 0, 1, 2)
    for i in order:
        loads[i].start()
    value = jnp.sqrt(norm[0:1, 0:1])
    grad_norm[0, 0] = value[0, 0]
    factor = jnp.minimum(1.0, CLIP / (value + NORM_EPS))
    pad[...] = jnp.zeros_like(pad)
    pad[0:BLOCK] = red[:, 0:128]
    for i in order[:3]:
        loads[i].wait()
        stores[i].start()

    def update(number, index, grad):
        rate, decay = RATES[number]
        old = [states[3 * number + i][index] for i in range(3)]
        for i, new in enumerate(adam_step(*old, grad * factor, rate, decay)):
            results[3 * number + i][index] = new

    def cut(column, width):
        return red[:, column : column + width]

    def tensor(number, *updates):
        for i in range(3):
            loads[3 * number + i].wait()
        for index, grad in updates:
            update(number, index, grad)
        for i in range(3):
            stores[3 * number + i].start()

    tiles = [(slice(f * FT, (f + 1) * FT), CM + f * 3 * FT) for f in range(FH // FT)]
    every = slice(None)
    tensor(5, *[((i, every, cols), cut(base + i * FT, FT)) for cols, base in tiles for i in range(2)])
    tensor(6, *[((every, cols), cut(base + 2 * FT, FT)) for cols, base in tiles])
    tensor(1, *[(i, cut(CQ + i * HALF, HALF)) for i in range(3)])
    tensor(4, *[(i, cut((COS, COC)[i], HALF)) for i in range(2)])
    tensor(3, *[(i, kvgrad[i]) for i in range(2)])
    tensor(2, (..., cut(CQC, HALF)))
    tensor(0, (..., pad[...].T[0:3, 0:BLOCK]))
    for store in stores:
        store.wait()


def finish(red, kvgrad, norm, states, passed):
    vm = pl.BlockSpec(memory_space=pltpu.VMEM)
    anywhere = pl.BlockSpec(memory_space=pl.ANY)
    shapes = [jax.ShapeDtypeStruct(value.shape, value.dtype) for value in passed]
    shapes += [jax.ShapeDtypeStruct((1, 1), F32)]
    shapes += [jax.ShapeDtypeStruct(value.shape, F32) for value in states]
    return pl.pallas_call(
        finish_kernel,
        out_shape=tuple(shapes),
        in_specs=[vm] * 3 + [anywhere] * 24,
        out_specs=tuple([anywhere] * 3 + [pl.BlockSpec(memory_space=pltpu.SMEM)] + [anywhere] * 21),
        scratch_shapes=[pltpu.VMEM((128, 128), F32), pltpu.SemaphoreType.DMA((24,)), pltpu.SemaphoreType.DMA((24,))]
        + [pltpu.VMEM(value.shape, value.dtype) for value in (*passed, *states, *states)],
        name="finish",
        compiler_params=pltpu.CompilerParams(vmem_limit_bytes=VMEM_BYTES),
    )(red, kvgrad, norm, *states, *passed)


def pack_weights(gains, self_proj, query, keyval, out_proj, mlp_input, mlp_output):
    rows = gains.shape[1]
    turned_out = jnp.swapaxes(out_proj, 1, 2)
    turned_down = mlp_output.T
    pieces = [jnp.pad(gains.T, ((0, 0), (0, 125)))]
    pieces += [self_proj[0], self_proj[1], self_proj[2], keyval[0], keyval[1]]
    pieces += [turned_out[0], query, turned_out[1]]
    for tile in range(FH // FT):
        columns = slice(tile * FT, (tile + 1) * FT)
        pieces += [mlp_input[0][:, columns], mlp_input[1][:, columns], turned_down[:, columns]]
    return jnp.concatenate([piece.astype(BF) for piece in pieces], axis=1)


def unpack_grads(red):
    def cut(start, width):
        return red[:, start : start + width]

    gains = cut(GAIN, 3).T
    self_proj = jnp.stack([cut(CQ + i * HALF, HALF) for i in range(3)])
    keyval = jnp.stack([cut(CKV + i * HALF, HALF) for i in range(2)])
    query = cut(CQC, HALF)
    out_proj = jnp.stack([cut(COS, HALF).T, cut(COC, HALF).T])
    tiles = FH // FT
    mlp = [jnp.concatenate([cut(CM + (3 * tile + k) * FT, FT) for tile in range(tiles)], axis=1) for k in range(3)]
    return gains, self_proj, query, keyval, out_proj, jnp.stack(mlp[:2]), mlp[2].T


def per_device(
    tokens, memory, cotangent, patch_item, patch_mask, text_item, text_len,
    norm_gains, gains_mean, gains_square,
    self_proj, self_proj_mean, self_proj_square,
    query_cross, query_cross_mean, query_cross_square,
    keyval_cross, keyval_cross_mean, keyval_cross_square,
    out_proj, out_proj_mean, out_proj_square,
    mlp_input, mlp_input_mean, mlp_input_square,
    mlp_output, mlp_output_mean, mlp_output_square,
):
    count = lax.axis_size("dp")
    direct = count == 16
    ints = (patch_item, patch_mask, text_item, text_len)
    states = [
        norm_gains, gains_mean, gains_square,
        self_proj, self_proj_mean, self_proj_square,
        query_cross, query_cross_mean, query_cross_square,
        keyval_cross, keyval_cross_mean, keyval_cross_square,
        out_proj, out_proj_mean, out_proj_square,
        mlp_input, mlp_input_mean, mlp_input_square,
        mlp_output, mlp_output_mean, mlp_output_square,
    ]
    if direct:
        for i in range(12, 15):
            states[i] = jnp.swapaxes(states[i], 1, 2)
        for i in range(18, 21):
            states[i] = states[i].T
        output, tokens_grad, memory_grad, red, kvgrad, norm = layer(
            True, tokens, cotangent, *ints, memory, states[::3]
        )
        results = list(finish(red, kvgrad, norm, states, (output, tokens_grad, memory_grad)))
        results[3] = results[3].reshape(())
        for i in range(16, 19):
            results[i] = jnp.swapaxes(results[i], 1, 2)
        for i in range(22, 25):
            results[i] = results[i].T
        return tuple(results)
    keyval_own = lax.all_to_all(keyval_cross.astype(BF), "head", split_axis=2, concat_axis=1, tiled=True)
    pack = pack_weights(norm_gains, self_proj, query_cross, keyval_own, out_proj, mlp_input, mlp_output)
    wall = lax.all_gather(pack, "dp", axis=0, tiled=True).reshape(BLOCKS + (BLOCK, PACK))
    output, tokens_grad, memory_grad, dwall = layer(False, tokens, cotangent, *ints, memory, (wall,))
    red = lax.psum_scatter(dwall.reshape(D, PACK).astype(F32), "dp", scatter_dimension=0, tiled=True)
    squares = jnp.sum(red[:, 128:] ** 2)
    squares = squares + jnp.where(lax.axis_index("head") == 0, jnp.sum(red[:, :128] ** 2), 0.0)
    total = lax.psum(squares, ("dp", "head"))
    gains_g, self_g, query_g, keyval_g, out_g, input_g, output_g = unpack_grads(red)
    keyval_g = lax.all_to_all(keyval_g, "head", split_axis=1, concat_axis=2, tiled=True)
    grad_norm = jnp.sqrt(total)
    factor = jnp.minimum(1.0, CLIP / (grad_norm + NORM_EPS))
    results = [output, tokens_grad, memory_grad, grad_norm]
    grads = (gains_g, self_g, query_g, keyval_g, out_g, input_g, output_g)
    for i, (grad, (rate, decay)) in enumerate(zip(grads, RATES)):
        results += adam_step(*states[3 * i : 3 * i + 3], grad * factor, rate, decay)
    return tuple(results)


def solution(mesh):
    in_specs = (
        P("dp", None),
        P(("dp", "head"), None),
        P("dp", None),
        P("dp"),
        P("dp"),
        P("dp"),
        P("dp"),
        P(None, "dp"),
        P(None, "dp"),
        P(None, "dp"),
        P(None, "dp", "head"),
        P(None, "dp", "head"),
        P(None, "dp", "head"),
        P("dp", "head"),
        P("dp", "head"),
        P("dp", "head"),
        P(None, ("dp", "head"), None),
        P(None, ("dp", "head"), None),
        P(None, ("dp", "head"), None),
        P(None, "head", "dp"),
        P(None, "head", "dp"),
        P(None, "head", "dp"),
        P(None, "dp", "head"),
        P(None, "dp", "head"),
        P(None, "dp", "head"),
        P("head", "dp"),
        P("head", "dp"),
        P("head", "dp"),
    )
    out_specs = (
        P("dp", None),
        P("dp", None),
        P(("dp", "head"), None),
        P(),
        P(None, "dp"),
        P(None, "dp"),
        P(None, "dp"),
        P(None, "dp", "head"),
        P(None, "dp", "head"),
        P(None, "dp", "head"),
        P("dp", "head"),
        P("dp", "head"),
        P("dp", "head"),
        P(None, ("dp", "head"), None),
        P(None, ("dp", "head"), None),
        P(None, ("dp", "head"), None),
        P(None, "head", "dp"),
        P(None, "head", "dp"),
        P(None, "head", "dp"),
        P(None, "dp", "head"),
        P(None, "dp", "head"),
        P(None, "dp", "head"),
        P("head", "dp"),
        P("head", "dp"),
        P("head", "dp"),
    )
    return jax.shard_map(
        per_device, mesh=mesh, in_specs=in_specs, out_specs=out_specs, check_vma=False
    )
```

```python
import functools

import jax
import jax.numpy as jnp
from jax import lax
from jax.experimental import pallas as pl
from jax.experimental.pallas import tpu as pltpu
from jax.sharding import PartitionSpec as P

D = 768
HD = 64
FF = 2048
TXT = 256
STEP = 10

BETA1 = 0.9
BETA2 = 0.95
ADAM_EPS = 1e-08
DECAY = 0.1
CLIP = 1.0
NORM_EPS = 1e-06
MASKED = -1e30

MESH = pl.DeviceIdType.MESH
BF = jnp.bfloat16
F32 = jnp.float32
VMEM_BYTES = 63 * 2**20

HALF = D // 2
FT = 256
FH = FF // 2
GAIN = 0
CQ = 128
CKV = CQ + 3 * HALF
COS = CKV + 2 * HALF
CQC = COS + HALF
COC = CQC + HALF
CM = COC + HALF
PACK = CM + 3 * FH


def as_bf(value):
    return value.astype(BF)


def as_f32(value):
    return value.astype(F32)


def nn(left, right):
    return lax.dot_general(left, right, (((1,), (0,)), ((), ())), preferred_element_type=F32)


def nt(left, right):
    return lax.dot_general(left, right, (((1,), (1,)), ((), ())), preferred_element_type=F32)


def tn(left, right):
    return lax.dot_general(left, right, (((0,), (0,)), ((), ())), preferred_element_type=F32)


BLOCKS = (2, 2, 2, 2)
BLOCK = D // 16


def middle(low, high):
    return low + (high - low) // 256 * 128 if high - low >= 256 else high


class Links:
    def __init__(self):
        self.me, self.head = lax.axis_index("dp"), lax.axis_index("head")
        self.x, self.y = self.me & 1, (self.me >> 1) & 1
        self.z0, self.z1 = (self.me >> 2) & 1, self.me >> 3
        self.to_x, self.to_y, self.to_z0, self.to_z1 = [(self.me ^ bit, self.head) for bit in (1, 2, 4, 8)]
        self.to_core = (self.me, 1 - self.head)

    def hops(self, slots, more):
        first = [
            (d, (self.me ^ (((d >> 2) & 1) * 8 + ((d >> 1) & 1) * 4), self.head ^ (d & 1))) for d in range(1, 8)
        ]
        second = [(d, (self.me ^ d, self.head)) for d in range(1, 4)]
        return (
            (slots, self.z1 * 4 + self.z0 * 2 + self.head, first),
            (more, self.y * 2 + self.x, second),
        )

    def peers(self):
        return [device for _, _, devices in self.hops(None, None) for _, device in devices]


def remote(source, target, send, recv, device):
    return pltpu.make_async_remote_copy(
        src_ref=source, dst_ref=target, send_sem=send, recv_sem=recv, device_id=device, device_id_type=MESH
    )


GATHER = (
    (0, 384, True),
    (384, 768, True),
    (768, 1280, False),
    (1280, 2048, True),
    (2048, 3200, True),
    (3200, 3968, True),
    (3968, 4736, True),
    (4736, 5504, False),
    (5504, 6272, True),
)

SCATTER = (
    (3200, 3968, True),
    (3968, 4736, False),
    (4736, 5504, False),
    (5504, 6272, False),
    (2816, 3200, True),
    (1280, 2048, False),
    (2432, 2816, False),
    (2048, 2432, False),
    (128, 512, True),
    (512, 896, False),
    (896, 1280, False),
    (0, 128, False),
)

SCHEDULE = (
    (0, 0, 0), (0, 1, 0), (0, 2, 0), 1, (0, 7, 0), 2, 0, (0, 3, 0), (0, 2, 1), (0, 0, 1), (0, 4, 0),
    (0, 7, 1), (0, 1, 1), (0, 0, 2), (0, 3, 1), (0, 2, 2), (0, 1, 2), (0, 0, 3), (0, 3, 2), (0, 4, 1),
    (0, 0, 4), (0, 5, 0), (0, 1, 3), (0, 2, 3), (0, 4, 2), (0, 1, 4), (0, 5, 1), (0, 3, 3), (0, 6, 0),
    (0, 2, 4), 3, 4, (0, 4, 3), (0, 8, 0), 5, 6, (0, 3, 4), (0, 5, 2), (0, 6, 1), 7, (0, 7, 2), 8, (0, 4, 4),
    9, (0, 6, 2), 10, 11, (0, 8, 1), 12, (0, 5, 3), 13, 14, (0, 6, 3), (0, 7, 3), 15, (0, 5, 4), (0, 8, 2),
    16, (0, 6, 4), 17, 18, 19, (0, 8, 3), (1, 0, 0), 20, (0, 7, 4), (1, 1, 0), 21, (0, 8, 4), (1, 2, 0), 22,
    (1, 3, 0), 23, (1, 1, 1), 24, (1, 4, 0), 25, 26, (1, 2, 1), (1, 0, 1), 27, 28, (1, 1, 2), (1, 3, 1), 29,
    (1, 2, 2), 30, (1, 4, 1), 31, 32, (1, 0, 2), (1, 3, 2), 33, (1, 6, 0), 34, (1, 2, 3), (1, 0, 3),
    (1, 7, 0), 35, (1, 6, 1), (1, 1, 3), 36, (1, 2, 4), (1, 5, 0), (1, 0, 4), (1, 3, 3), 37, (1, 4, 2),
    (1, 6, 2), (1, 1, 4), (1, 7, 1), 38, 39, (1, 5, 1), (1, 6, 3), (1, 3, 4), 40, 41, (1, 8, 0), 42, 43,
    (1, 6, 4), 44, (1, 4, 3), (1, 9, 0), (1, 7, 2), (1, 10, 0), (1, 5, 2), (1, 11, 0), (1, 4, 4), (1, 9, 1),
    (1, 8, 1), (1, 10, 1), (1, 11, 1), (1, 9, 2), (1, 5, 3), (1, 10, 2), (1, 9, 3), (1, 8, 2), (1, 11, 2),
    (1, 7, 3), (1, 8, 3), (1, 5, 4), (1, 10, 3), (1, 11, 3), (1, 9, 4), (1, 8, 4), (1, 7, 4), (1, 10, 4),
    (1, 11, 4),
)


class Gather:
    def __init__(self, links, wall, send_sem, recv_sem):
        self.links, self.wall, self.send_sem, self.recv_sem = links, wall, send_sem, recv_sem

    def where(self, n, k, received):
        low, high, z_first = GATHER[n]
        half = middle(low, high)
        links, every = self.links, slice(None)
        z1, z0, y, x = links.z1, links.z0, links.y, links.x
        flip = (lambda v: 1 - v) if received else (lambda v: v)
        if z_first:
            index, cols, device = (
                ((flip(z1), z0, y, x), (low, high), links.to_z1),
                ((every, flip(z0), y, x), (low, high), links.to_z0),
                ((every, every, y, flip(x)), (low, high), links.to_x),
                ((every, every, flip(y), x), (low, high), links.to_y),
                ((every, every, flip(y), 1 - x), (low, half), links.to_y),
                ((every, every, 1 - y, flip(x)), (half, high), links.to_x),
            )[k]
        else:
            index, cols, device = (
                ((z1, z0, y, flip(x)), (low, high), links.to_x),
                ((z1, z0, flip(y), x), (low, high), links.to_y),
                ((z1, z0, flip(y), 1 - x), (low, half), links.to_y),
                ((z1, z0, 1 - y, flip(x)), (half, high), links.to_x),
                ((flip(z1), z0, every, every), (low, high), links.to_z1),
                ((every, flip(z0), every, every), (low, high), links.to_z0),
            )[k]
        return self.wall.at[index + (every, slice(*cols))], device

    def copy(self, n, k, received=False):
        ref, device = self.where(n, k, received)
        return remote(ref, ref, self.send_sem.at[n, k], self.recv_sem.at[n, k], device)

    def step(self, n, number):
        if GATHER[n][2]:
            plan = ((None, 0),), ((0, 1),), ((1, 2), (None, 3)), ((2, 4), (3, 5)), ((4, None), (5, None))
        else:
            plan = ((None, 0), (None, 1)), ((0, 2), (1, 3)), ((2, None), (3, 4)), ((4, 5),), ((5, None),)
        for wait, start in plan[number]:
            if wait is not None:
                self.copy(n, wait, True).wait_recv()
            if start is not None:
                self.copy(n, start).start()

    def sent(self, n):
        for k in range(6):
            self.copy(n, k).wait_send()


class Scatter:
    def __init__(self, links, wall, slot1, slot2, slot3, red, send_sem, recv_sem):
        self.links, self.wall, self.red = links, wall, red
        self.slot1, self.slot2, self.slot3 = slot1, slot2, slot3
        self.send_sem, self.recv_sem = send_sem, recv_sem

    def skipped(self, n):
        low, high, z_first = SCATTER[n]
        return (3 if z_first else 1,) if middle(low, high) == high else ()

    def copy(self, n, k):
        low, high, z_first = SCATTER[n]
        half = middle(low, high)
        links, every = self.links, slice(None)
        z1, z0, y, x = links.z1, links.z0, links.y, links.x
        slot1, slot2, slot3 = self.slot1, self.slot2, self.slot3
        if z_first:
            index, slot, place, cols, device = (
                ((every, 1 - z0, every, every), slot2, (every,) * 3, (low, high), links.to_z0),
                ((1 - z1, z0, every, every), slot1, (every,) * 2, (low, high), links.to_z1),
                ((z1, z0, 1 - y, 1 - x), slot3, (0,), (low, half), links.to_y),
                ((z1, z0, 1 - y, 1 - x), slot3, (0,), (half, high), links.to_x),
                ((z1, z0, y, 1 - x), slot3, (1,), (low, high), links.to_x),
                ((z1, z0, 1 - y, x), slot3, (2,), (low, high), links.to_y),
            )[k]
        else:
            index, slot, place, cols, device = (
                ((every, every, 1 - y, 1 - x), slot1, (every,) * 2, (low, half), links.to_y),
                ((every, every, 1 - y, 1 - x), slot1, (every,) * 2, (half, high), links.to_x),
                ((every, every, y, 1 - x), slot2, (0, every, every), (low, high), links.to_x),
                ((every, every, 1 - y, x), slot2, (1, every, every), (low, high), links.to_y),
                ((every, 1 - z0, y, x), slot3, (slice(0, 2),), (low, high), links.to_z0),
                ((1 - z1, z0, y, x), slot3, (2,), (low, high), links.to_z1),
            )[k]
        tail = (every, slice(*cols))
        return remote(
            self.wall.at[index + tail], slot.at[place + tail], self.send_sem.at[n, k], self.recv_sem.at[n, k], device
        )

    def add(self, index, *others):
        self.wall[index] = as_bf(sum((as_f32(ref[at]) for ref, at in others), as_f32(self.wall[index])))

    def step(self, n, number):
        low, high, z_first = SCATTER[n]
        half = middle(low, high)
        links, every = self.links, slice(None)
        z1, z0, y, x = links.z1, links.z0, links.y, links.x
        slot1, slot2, slot3 = self.slot1, self.slot2, self.slot3
        cols, left, right = (every, slice(low, high)), (every, slice(low, half)), (every, slice(half, high))
        groups = ((0,), (1,), (2, 3), (4, 5)) if z_first else ((0, 1), (2, 3), (4,), (5,))
        skipped = self.skipped(n)
        if number > 0:
            for k in groups[number - 1]:
                if k not in skipped:
                    self.copy(n, k).wait_recv()
        if number == 4:
            value = as_f32(self.wall[(z1, z0, y, x) + cols])
            for k in (1, 2) if z_first else (2,):
                value = value + as_f32(slot3[(k,) + cols])
            self.red[:, low:high] = value
        elif z_first and number == 1:
            for a in range(2):
                for b in range(2):
                    for c in range(2):
                        self.add((a, z0, b, c) + cols, (slot2, (a, b, c) + cols))
        elif z_first and number == 2:
            for b in range(2):
                for c in range(2):
                    self.add((z1, z0, b, c) + cols, (slot1, (b, c) + cols))
        elif z_first and number == 3:
            self.add((z1, z0, y, 1 - x) + left, (slot3, (0,) + left))
            if half < high:
                self.add((z1, z0, 1 - y, x) + right, (slot3, (0,) + right))
        elif number == 1:
            for a in range(2):
                for b in range(2):
                    self.add((a, b, y, 1 - x) + left, (slot1, (a, b) + left))
                    if half < high:
                        self.add((a, b, 1 - y, x) + right, (slot1, (a, b) + right))
        elif number == 2:
            for a in range(2):
                for b in range(2):
                    self.add((a, b, y, x) + cols, (slot2, (0, a, b) + cols), (slot2, (1, a, b) + cols))
        elif number == 3:
            for a in range(2):
                self.add((a, z0, y, x) + cols, (slot3, (a,) + cols))
        if number < 4:
            for k in groups[number]:
                if k not in skipped:
                    self.copy(n, k).start()

    def sent(self):
        for n in range(len(SCATTER)):
            for k in range(6):
                if k not in self.skipped(n):
                    self.copy(n, k).wait_send()


class Exchange:
    def __init__(self, links, send, recv, send_sem, recv_sem):
        self.links = links
        self.send, self.recv, self.send_sem, self.recv_sem = send, recv, send_sem, recv_sem

    def copy(self, number):
        slot = number % 2
        return remote(
            self.send.at[slot],
            self.recv.at[slot],
            self.send_sem.at[number],
            self.recv_sem.at[number],
            self.links.to_core,
        )

    def start(self, number, value):
        self.send[number % 2] = as_bf(value)
        self.copy(number).start()

    def wait(self, number):
        self.copy(number).wait()

    def total(self, number, rows=slice(None)):
        slot = number % 2
        return as_f32(self.send[slot, rows]) + as_f32(self.recv[slot, rows])


def inverse_rms(values):
    return lax.rsqrt(jnp.mean(values * values, axis=-1, keepdims=True) + NORM_EPS)


def norm_back(values, gain, grad):
    inverse = inverse_rms(values)
    scaled = grad * gain
    inner = jnp.mean(scaled * values, axis=-1, keepdims=True)
    grad_values = inverse * scaled - values * (inverse * inverse * inverse * inner)
    grad_gain = jnp.sum(grad * values * inverse, axis=0, keepdims=True)
    return grad_values, grad_gain


def layer_kernel(direct, *refs):
    (tok_in, cot_in, item, pmask, titem, tlen, memory), refs = refs[:7], refs[7:]
    if direct:
        (gshard, sproj_in, query_in, keyval, tout_in, minput_in, tdown_in), refs = refs[:7], refs[7:]
        (out_to, tgrad_to, mgrad, red, kvgrad, norm), refs = refs[:6], refs[6:]
    else:
        (wall,), refs = refs[:1], refs[1:]
        (out_to, tgrad_to, mgrad, dwall), refs = refs[:4], refs[4:]
    (
        ws, mem, gains, dgains, cbias, sbias, n1, n2, n3, x1, x2,
        q3, k3, v3, o3, oT, qc3, oc3, ocT, do3, dqc3, sexps, slinv,
        kext, mv3, mT, st, eb, clse, acc,
        esend, erecv, osend, orecv, mrecv,
        tok, cot, out, tgrad, send_sem, recv_sem, side_sem, wsem, msem,
    ), refs = refs[:44], refs[44:]
    links = Links()
    head, other = links.head, links.to_core

    barrier = pltpu.get_barrier_semaphore()
    peers = links.peers() if direct else [other]
    for device in peers:
        pl.semaphore_signal(barrier, inc=1, device_id=device, device_id_type=MESH)
    load_tok = pltpu.make_async_copy(tok_in, tok, wsem.at[2])
    load_cot = pltpu.make_async_copy(cot_in, cot, wsem.at[3])
    store_out = pltpu.make_async_copy(out, out_to, wsem.at[4])
    store_tgrad = pltpu.make_async_copy(tgrad, tgrad_to, wsem.at[5])
    own_memory = pltpu.make_async_copy(memory, mem.at[head], wsem.at[0])
    mem_copy = remote(memory, mem.at[head], side_sem.at[0], side_sem.at[1], other)
    if direct:
        sproj, query, tout, minput, tdown, refs = *refs[:5], refs[5:]
        slot1, slot2, slot3, kvs, kvr, kgs, kgr, sums, others, g_send, g_recv, s_send, s_recv, t_send, t_recv, l_sem = refs
        pairs_in = ((sproj_in, sproj), (tout_in, tout), (query_in, query), (minput_in, minput), (tdown_in, tdown))
        loads = [pltpu.make_async_copy(source, target, l_sem.at[i]) for i, (source, target) in enumerate(pairs_in)]
        for load in loads:
            load.start()
        load_tok.start()
        own_memory.start()
        load_cot.start()
        gather = Gather(links, ws, g_send, g_recv)
        scatter = Scatter(links, ws, slot1, slot2, slot3, red, s_send, s_recv)
        here = (links.z1, links.z0, links.y, links.x, slice(None))

        def own(column, value):
            ws[here + (slice(column, column + value.shape[1]),)] = as_bf(value)

        for k in range(2):
            kvs[k] = jnp.where(head == 0, keyval[k, :, HALF:], keyval[k, :, :HALF])
        dgains[...] = jnp.zeros_like(dgains)
        dgains[0:3, 0:BLOCK] = gshard[...]
        own(GAIN, dgains[:, 0:128].T[0:BLOCK])
        loads[0].wait()
        for i in range(3):
            own(CQ + i * HALF, sproj[i])
        pl.semaphore_wait(barrier, len(peers))
        kv_copy = remote(kvs, kvr, side_sem.at[4], side_sem.at[5], other)
        kv_copy.start()

        def pack_rest():
            loads[3].wait()
            loads[4].wait()
            for f in range(FH // FT):
                base = CM + f * 3 * FT
                for k in range(2):
                    own(base + k * FT, minput[k, :, f * FT : (f + 1) * FT])
                own(base + 2 * FT, tdown[:, f * FT : (f + 1) * FT])

        def pack_heads():
            loads[1].wait()
            loads[2].wait()
            own(COS, tout[0])
            own(CQC, query[...])
            own(COC, tout[1])
            mem_copy.start()
            kv_copy.wait()
            for k in range(2):
                mine = jnp.where(head == 0, keyval[k, :, :HALF], keyval[k, :, HALF:])
                top, bottom = jnp.where(head == 0, mine, kvr[k]), jnp.where(head == 0, kvr[k], mine)
                own(CKV + k * HALF, jnp.concatenate([top, bottom], axis=0))
    else:
        pl.semaphore_wait(barrier, len(peers))
        load_tok.start()
        own_memory.start()
        load_cot.start()
        load = pltpu.make_async_copy(wall, ws, wsem.at[1])
        load.start()
        mem_copy.start()
        load.wait()

    ex = Exchange(links, esend, erecv, send_sem, recv_sem)

    def w(column, width):
        return ws[:, :, :, :, :, column : column + width].reshape(D, width)

    def put(column, value):
        width = value.shape[1]
        ws[:, :, :, :, :, column : column + width] = as_bf(value).reshape(BLOCKS + (BLOCK, width))

    def sent(column):
        if direct:
            for n, (low, high, _) in enumerate(GATHER):
                if low <= column < high and n not in done:
                    done.add(n)
                    gather.sent(n)

    done = set()
    half_rows = mem.shape[1]
    patches = 2 * half_rows
    lane = lax.broadcasted_iota(jnp.int32, (TXT, 128), 1)
    mask = [as_bf(jnp.where(lane < HD, 1.0, 0.0)), as_bf(jnp.where(lane < HD, 0.0, 1.0))]
    texts = [slice(0, TXT), slice(TXT, 2 * TXT)]
    pairs = 3
    pieces = []

    def piece(*numbers):
        def keep(function):
            pieces.append(functools.partial(function, *numbers))
            return function

        return keep

    def joined(ref, rows=slice(None)):
        return jnp.concatenate([ref[j, rows] for j in range(pairs)], axis=1)

    def spread(target, rows, value):
        for j in range(pairs):
            target[j, rows] = value[:, j * 128 : (j + 1) * 128]

    pieces += [pack_heads, pack_rest] if direct else [None, None]

    @piece()
    def _():
        row = lax.broadcasted_iota(jnp.int32, (128, 512), 0)
        for c in range(patches // 512):
            cols = slice(c * 512, (c + 1) * 512)
            place = jnp.where(row == 0, titem[0], jnp.where(row == 1, titem[1], -1))
            seen = (place == item[:, cols]) & (pmask[:, cols] == 1)
            cbias[cols] = as_bf(jnp.where(seen, 0.0, jnp.where(row < 2, MASKED, 0.0)).T)
        key = lax.broadcasted_iota(jnp.int32, (TXT, TXT), 0)
        slot = lax.broadcasted_iota(jnp.int32, (TXT, TXT), 1)
        for t in range(2):
            sbias[t] = as_bf(jnp.where((key <= slot) & (key < tlen[t]), 0.0, MASKED))
        dgains[...] = jnp.zeros_like(dgains)
        acc[...] = jnp.zeros_like(acc)
        tgrad[...] = jnp.zeros_like(tgrad)

    @piece()
    def _():
        load_tok.wait()
        gains[...] = as_f32(w(0, 128)).T[0:8]
        for rows in texts:
            x = as_f32(tok[rows])
            n1[rows] = as_bf(x * inverse_rms(x) * gains[0:1])
        for number, target in enumerate((q3, k3, v3)):
            value = as_bf(nn(n1[...], w(CQ + number * HALF, HALF)))
            if number == 0:
                value = value * jnp.asarray(HD**-0.5, BF)
            spread(target, slice(None), value)

    def self_forward(j):
        for t in range(2):
            query_pair, key_pair = q3[j, texts[t]], k3[j, texts[t]]
            turned = v3[j, texts[t]].T
            parts = []
            for a in range(2):
                scores = nt(key_pair, query_pair * mask[a]) + as_f32(sbias[t])
                top = jnp.max(scores, axis=0, keepdims=True)
                expo = jnp.exp(scores - top)
                low = as_bf(expo)
                sexps[j, t, a] = low
                inverse = 1.0 / jnp.sum(expo, axis=0, keepdims=True)
                slinv[j, t, a] = jnp.broadcast_to(inverse, (8, TXT))
                parts.append(nn(turned[a * HD : (a + 1) * HD], low) * inverse)
            both = jnp.concatenate(parts, axis=0)
            oT[j, t] = as_bf(both)
            o3[j, texts[t]] = as_bf(both.T)

    for j in range(pairs):
        piece(j)(self_forward)

    def project(side):
        if side == 0:
            own_memory.wait()
            mem_copy.wait_send()
            remote(memory, mem.at[1 - head], side_sem.at[0], side_sem.at[1], other).wait_recv()
        for c in range(half_rows // 512):
            part = slice(c * 512, (c + 1) * 512)
            rows = slice(side * half_rows + c * 512, side * half_rows + (c + 1) * 512)
            both = as_bf(nn(mem[side, part], w(CKV, 2 * HALF)))
            for j in range(pairs):
                kext[j, rows, 0:128] = both[:, j * 128 : (j + 1) * 128]
                kext[j, rows, 128:256] = cbias[rows]
                mv3[j, rows] = both[:, HALF + j * 128 : HALF + (j + 1) * 128]
        side_rows = slice(side * half_rows, (side + 1) * half_rows)
        for j in range(pairs):
            mT[j, :, side_rows] = mv3[j, side_rows].T

    for side in range(2):
        piece(side)(project)

    @piece()
    def _():
        ex.start(0, nt(joined(o3), w(COS, HALF)))

    @piece()
    def _():
        ex.wait(0)
        for rows in texts:
            value = as_f32(tok[rows]) + ex.total(0, rows)
            x1[rows] = value
            n2[rows] = as_bf(value * inverse_rms(value) * gains[1:2])
        spread(qc3, slice(None), as_bf(nn(n2[...], w(CQC, HALF))) * jnp.asarray(HD**-0.5, BF))

    big, small = 512, 128

    def eb_at(a, start, size):
        return (2 * a + start // half_rows, slice(start % half_rows, start % half_rows + size))

    def eb_all(a):
        return eb[2 * a : 2 * a + 2].reshape(patches, TXT)

    def wide_query(j, t, a):
        pick = as_bf(jnp.where(lane == t, 1.0, 0.0))
        return jnp.concatenate([qc3[j, texts[t]] * mask[a], pick], axis=1)

    def cross_forward(j, t):
        parts = []
        for a in range(2):
            wide = wide_query(j, t, a)
            top = jnp.full((8, TXT), -3e38, F32)
            for c in range(patches // big):
                scores = nt(kext[j, c * big : (c + 1) * big], wide)
                st[c * big : (c + 1) * big] = scores
                top = jnp.maximum(top, jnp.max(scores.reshape(big // 8, 8, TXT), axis=0))
            top = jnp.max(top, axis=0, keepdims=True)
            total = jnp.zeros((8, TXT), F32)
            for c in range(patches // small):
                expo = jnp.exp(st[c * small : (c + 1) * small] - top)
                total = total + jnp.sum(expo.reshape(small // 8, 8, TXT), axis=0)
                eb[eb_at(a, c * small, small)] = as_bf(expo)
            total = jnp.sum(total, axis=0, keepdims=True)
            clse[j, t, a] = jnp.broadcast_to(top + jnp.log(total), (8, TXT))
            parts.append(nn(mT[j, a * HD : (a + 1) * HD], eb_all(a)) * (1.0 / total))
        both = jnp.concatenate(parts, axis=0)
        ocT[j, t] = as_bf(both)
        oc3[j, texts[t]] = as_bf(both.T)

    for j in range(pairs):
        for t in range(2):
            piece(j, t)(cross_forward)

    @piece()
    def _():
        ex.start(1, nt(joined(oc3), w(COC, HALF)))
        for j in range(pairs):
            mT[j] = kext[j, :, 0:128].T

    @piece()
    def _():
        ex.wait(1)
        for rows in texts:
            value = x1[rows] + ex.total(1, rows)
            x2[rows] = value
            n3[rows] = as_bf(value * inverse_rms(value) * gains[2:3])

    root = (2.0 / jnp.pi) ** 0.5

    def mlp(f):
        if f == 0:
            load_cot.wait()
        base = CM + f * (3 * FT)
        gate_w, up_w, down_w = (w(base + k * FT, FT) for k in range(3))
        for rows in texts:
            gate, up = nn(n3[rows], gate_w), nn(n3[rows], up_w)
            grad = nn(cot[rows], down_w)
            square = gate * gate
            tanh = jnp.tanh(root * gate * (1.0 + 0.044715 * square))
            half = 0.5 * (1.0 + tanh)
            slope = half + 0.5 * gate * (1.0 - tanh * tanh) * (root * (1.0 + 3 * 0.044715 * square))
            active = gate * half
            osend[rows, 0:FT] = as_bf(active * up)
            osend[rows, FT : 2 * FT] = as_bf(grad * up * slope)
            osend[rows, 2 * FT : 3 * FT] = as_bf(grad * active)
        for rows in texts:
            acc[rows] += nt(osend[rows, 0:FT], down_w)
            tgrad[rows] += nt(osend[rows, FT : 2 * FT], gate_w) + nt(osend[rows, 2 * FT : 3 * FT], up_w)
        sent(base)
        put(base, tn(n3[...], osend[:, FT : 2 * FT]))
        put(base + FT, tn(n3[...], osend[:, 2 * FT : 3 * FT]))
        put(base + 2 * FT, tn(cot[...], osend[:, 0:FT]))

    for f in range(FH // FT):
        piece(f)(mlp)

    side = remote(osend, orecv, side_sem.at[2], side_sem.at[3], other)

    @piece()
    def _():
        ex.start(2, tgrad[...])
        osend[...] = as_bf(acc[...])
        side.start()

    @piece()
    def _():
        ex.wait(2)
        for rows in texts:
            grad, grad_gain = norm_back(x2[rows], gains[2:3], ex.total(2, rows))
            value = as_f32(cot[rows]) + grad
            acc[rows] = x2[rows]
            x2[rows] = value
            dgains[2:3] += grad_gain
            back = as_bf(value)
            n3[rows] = back
            spread(do3, rows, as_bf(nn(back, w(COC, HALF))))
        sent(COC)
        put(COC, tn(n3[...], joined(oc3)))
        side.wait()
        for rows in texts:
            out[rows] = as_bf(acc[rows] + (as_f32(osend[rows]) + as_f32(orecv[rows])))
        store_out.start()

    def cross_back(j, t):
        rows = texts[t]
        grad = do3[j, rows].T
        attended = as_f32(ocT[j, t])
        parts = []
        for a in range(2):
            keep = grad[a * HD : (a + 1) * HD]
            inner = jnp.sum(as_f32(keep) * attended[a * HD : (a + 1) * HD], axis=0, keepdims=True)
            empty = jnp.zeros_like(keep)
            low = jnp.concatenate([keep, empty] if a == 0 else [empty, keep], axis=0)
            wide = wide_query(j, t, a)
            lse = clse[j, t, a, 0:1]
            for c in range(patches // big):
                keys = slice(c * big, (c + 1) * big)
                probs = jnp.exp(nt(kext[j, keys], wide) - lse)
                eb[eb_at(0, c * big, big)] = as_bf(probs)
                eb[eb_at(1, c * big, big)] = as_bf(probs * (nn(mv3[j, keys], low) - inner))
            for c in range(patches // big):
                keys = slice(c * big, (c + 1) * big)
                grad_value = nt(eb[eb_at(0, c * big, big)], low)
                grad_key = nn(eb[eb_at(1, c * big, big)], wide[:, 0:128])
                if t == 0 and a == 0:
                    st[keys, 0:128] = grad_value
                    st[keys, 128:256] = grad_key
                else:
                    st[keys, 0:128] += grad_value
                    st[keys, 128:256] += grad_key
            parts.append(nn(mT[j, a * HD : (a + 1) * HD], eb_all(1)))
        dqc3[j, rows] = as_bf((jnp.concatenate(parts, axis=0) * HD**-0.5).T)
        if t == 1:
            mv3[j] = as_bf(st[:, 0:128])
            kext[j, :, 0:128] = as_bf(st[:, 128:256])

    for j in range(pairs):
        for t in range(2):
            piece(j, t)(cross_back)

    @piece()
    def _():
        ex.start(3, nt(joined(dqc3), w(CQC, HALF)))

    def memory_back(c, start):
        rows = pl.ds(pl.multiple_of(start + c * 256, 256), 256)
        both = jnp.concatenate(
            [kext[j, rows, 0:128] for j in range(pairs)] + [mv3[j, rows] for j in range(pairs)], axis=1
        )
        return nt(both, w(CKV, 2 * HALF))

    mside = remote(eb.at[0:3], mrecv, side_sem.at[6], side_sem.at[7], other)

    @piece()
    def _():
        def send_part(c, carry):
            value = as_bf(memory_back(c, (1 - head) * half_rows))
            for k in range(3):
                eb[k, pl.ds(pl.multiple_of(c * 256, 256), 256)] = value[:, k * TXT : (k + 1) * TXT]
            return carry

        lax.fori_loop(0, half_rows // 256, send_part, 0)
        mside.start()

    @piece()
    def _():
        sent(CQC)
        put(CQC, tn(n2[...], joined(dqc3)))
        ex.wait(3)

    @piece()
    def _():
        for rows in texts:
            grad, grad_gain = norm_back(x1[rows], gains[1:2], ex.total(3, rows))
            value = x2[rows] + grad
            x1[rows] = value
            dgains[1:2] += grad_gain
            back = as_bf(value)
            n3[rows] = back
            spread(do3, rows, as_bf(nn(back, w(COS, HALF))))
        sent(COS)
        put(COS, tn(n3[...], joined(o3)))

    stores = []

    @piece()
    def _():
        mside.wait()
        for c in range(half_rows // 256):
            if c >= 2:
                stores[c - 2].wait()
            slot_rows = slice((c % 2) * 256, (c % 2 + 1) * 256)
            part = slice(c * 256, (c + 1) * 256)
            peer_part = jnp.concatenate([mrecv[k, part] for k in range(3)], axis=1)
            acc[slot_rows] = memory_back(c, head * half_rows) + as_f32(peer_part)
            store = pltpu.make_async_copy(acc.at[slot_rows], mgrad.at[pl.ds(c * 256, 256)], msem.at[c])
            store.start()
            stores.append(store)

    @piece()
    def _():
        sent(CKV)
        for number, source in enumerate((kext, mv3)):
            total = jnp.zeros((D, HALF), F32)
            for c in range(patches // 512):
                rows = slice(c * 512, (c + 1) * 512)
                part = slice(c * 512 % half_rows, c * 512 % half_rows + 512)
                both = jnp.concatenate([source[j, rows, 0:128] for j in range(pairs)], axis=1)
                total = total + tn(mem[c * 512 // half_rows, part], both)
            put(CKV + number * HALF, total)

    def self_back(j):
        for t in range(2):
            rows = texts[t]
            grad = as_f32(do3[j, rows]).T
            attended = as_f32(oT[j, t])
            query_pair, key_pair, value_pair = q3[j, rows], k3[j, rows], v3[j, rows]
            key_turned = key_pair.T
            parts = []
            grad_key = jnp.zeros((TXT, 128), F32)
            grad_value = jnp.zeros((TXT, 128), F32)
            for a in range(2):
                keep = as_bf(grad[a * HD : (a + 1) * HD] * slinv[j, t, a, 0:1])
                inner = jnp.sum(as_f32(keep) * attended[a * HD : (a + 1) * HD], axis=0, keepdims=True)
                empty = jnp.zeros_like(keep)
                low = jnp.concatenate([keep, empty] if a == 0 else [empty, keep], axis=0)
                expo = sexps[j, t, a]
                grad_scores = as_bf(as_f32(expo) * (nn(value_pair, low) - inner))
                grad_value = grad_value + nt(expo, low)
                grad_key = grad_key + nn(grad_scores, query_pair * mask[a])
                parts.append(nn(key_turned[a * HD : (a + 1) * HD], grad_scores))
            q3[j, rows] = as_bf((jnp.concatenate(parts, axis=0) * HD**-0.5).T)
            k3[j, rows] = as_bf(grad_key)
            v3[j, rows] = as_bf(grad_value)

    for j in range(pairs):
        piece(j)(self_back)

    @piece()
    def _():
        ex.start(
            4,
            nt(joined(q3), w(CQ, HALF))
            + nt(joined(k3), w(CQ + HALF, HALF))
            + nt(joined(v3), w(CQ + 2 * HALF, HALF)),
        )
        for number in range(3):
            sent(CQ + number * HALF)

    def projection_grad(number):
        put(CQ + number * HALF, tn(n1[...], joined((q3, k3, v3)[number])))

    for number in range(3):
        piece(number)(projection_grad)

    @piece()
    def _():
        ex.wait(4)
        for rows in texts:
            grad, grad_gain = norm_back(as_f32(tok[rows]), gains[0:1], ex.total(4, rows))
            tgrad[rows] = x1[rows] + grad
            dgains[0:1] += grad_gain
        store_tgrad.start()
        sent(GAIN)
        put(GAIN, dgains[...].T)

    kv_group = [n for n, group in enumerate(SCATTER) if group[0] == CKV][0]
    kv_back = remote(kgs, kgr, side_sem.at[8], side_sem.at[9], other) if direct else None

    def send_keyval():
        kgs[...] = jnp.where(head == 0, red[BLOCK // 2 :, CKV:COS], red[: BLOCK // 2, CKV:COS])
        kv_back.start()

    def finish_keyval():
        kv_back.wait()
        mine = jnp.where(head == 0, red[: BLOCK // 2, CKV:COS], red[BLOCK // 2 :, CKV:COS])
        for k in range(2):
            cols = slice(k * HALF, (k + 1) * HALF)
            first, second = mine[:, cols], kgr[:, cols]
            kvgrad[k, :, :HALF] = jnp.where(head == 0, first, second)
            kvgrad[k, :, HALF:] = jnp.where(head == 0, second, first)

    for entry in SCHEDULE if direct else range(2, len(pieces)):
        if isinstance(entry, int):
            pieces[entry]()
        else:
            part, n, number = entry
            (gather, scatter)[part].step(n, number)
            if part == 1 and n == kv_group and number == 4:
                send_keyval()

    if direct:
        if True:
            first = red[:, 0:128]
            first = jnp.sum(first * first, axis=0, keepdims=True)
            value = jnp.where(head == 0, first, jnp.zeros_like(first))
            for column in range(128, PACK, 128):
                part = red[:, column : column + 128]
                value = value + jnp.sum(part * part, axis=0, keepdims=True)
            value = jnp.broadcast_to(jnp.sum(value, axis=1, keepdims=True), (8, 128))
            for hop, (slots, place, peers) in enumerate(links.hops(sums, others)):
                slots[place] = value
                copies = [
                    (
                        remote(slots.at[place], slots.at[place], t_send.at[hop, d], t_recv.at[hop, d], device),
                        remote(slots.at[place ^ d], slots.at[place ^ d], t_send.at[hop, d], t_recv.at[hop, d], device),
                    )
                    for d, device in peers
                ]
                for copy, _ in copies:
                    copy.start()
                if hop == 0:
                    finish_keyval()
                    scatter.sent()
                for copy, arrived in copies:
                    copy.wait_send()
                    arrived.wait_recv()
                value = slots[0]
                for d in range(1, len(peers) + 1):
                    value = value + slots[d]
            norm[...] = value
    else:
        store = pltpu.make_async_copy(ws, dwall, wsem.at[1])
        store.start()
        store.wait()
    for number in (-2, -1):
        stores[number].wait()
    store_out.wait()
    store_tgrad.wait()


def layer(direct, tokens, cotangent, patch_item, patch_mask, text_item, text_len, memory, weights):
    rows, half_rows = tokens.shape[0], memory.shape[0]
    patches = 2 * half_rows
    vm = pl.BlockSpec(memory_space=pltpu.VMEM)
    sm = pl.BlockSpec(memory_space=pltpu.SMEM)
    anywhere = pl.BlockSpec(memory_space=pl.ANY)
    S, DMA = pltpu.VMEM, pltpu.SemaphoreType.DMA
    heads3 = S((3, rows, 128), BF)
    scratch = [
        S(BLOCKS + (BLOCK, PACK), BF), S((2, half_rows, D), BF), S((8, D), F32), S((128, D), F32),
        S((patches, 128), BF), S((2, TXT, TXT), BF),
        S((rows, D), BF), S((rows, D), BF), S((rows, D), BF), S((rows, D), F32), S((rows, D), F32),
        heads3, heads3, heads3, heads3, S((3, 2, 128, TXT), BF), heads3, heads3, S((3, 2, 128, TXT), BF),
        heads3, heads3, S((3, 2, 2, TXT, TXT), BF), S((3, 2, 2, 8, TXT), F32),
        S((3, patches, 256), BF), S((3, patches, 128), BF), S((3, 128, patches), BF),
        S((patches, TXT), F32), S((4, half_rows, TXT), BF), S((3, 2, 2, 8, TXT), F32), S((rows, D), F32),
        S((2, rows, D), BF), S((2, rows, D), BF), S((rows, D), BF), S((rows, D), BF),
        S((3, half_rows, TXT), BF),
        S((rows, D), BF), S((rows, D), BF), S((rows, D), BF), S((rows, D), F32),
        DMA((5,)), DMA((5,)), DMA((10,)), DMA((6,)), DMA((half_rows // 256,)),
    ]
    shapes = [
        jax.ShapeDtypeStruct((rows, D), BF),
        jax.ShapeDtypeStruct((rows, D), F32),
        jax.ShapeDtypeStruct((half_rows, D), F32),
    ]
    if direct:
        scratch += [S(weights[i].shape, F32) for i in (1, 2, 4, 5, 6)]
        scratch += [
            S((2, 2, BLOCK, PACK), BF), S((2, 2, 2, BLOCK, PACK), BF), S((3, BLOCK, PACK), BF),
            S((2, BLOCK // 2, HALF), F32), S((2, BLOCK // 2, HALF), F32),
            S((BLOCK // 2, 2 * HALF), F32), S((BLOCK // 2, 2 * HALF), F32),
            S((8, 8, 128), F32), S((4, 8, 128), F32),
            DMA((len(GATHER), 6)), DMA((len(GATHER), 6)), DMA((len(SCATTER), 6)), DMA((len(SCATTER), 6)),
            DMA((2, 8)), DMA((2, 8)), DMA((5,)),
        ]
        shapes += [
            jax.ShapeDtypeStruct((BLOCK, PACK), F32),
            jax.ShapeDtypeStruct((2, BLOCK // 2, D), F32),
            jax.ShapeDtypeStruct((8, 128), F32),
        ]
        more_in, more_out = [vm, anywhere, anywhere, vm, anywhere, anywhere, anywhere], [vm] * 3
    else:
        shapes += [jax.ShapeDtypeStruct(BLOCKS + (BLOCK, PACK), BF)]
        more_in, more_out = [anywhere], [anywhere]
    return pl.pallas_call(
        functools.partial(layer_kernel, direct),
        out_shape=tuple(shapes),
        in_specs=[anywhere, anywhere, vm, vm, sm, sm, anywhere] + more_in,
        out_specs=tuple([anywhere] * 3 + more_out),
        scratch_shapes=scratch,
        name="layer",
        compiler_params=pltpu.CompilerParams(
            collective_id=1, has_side_effects=True, vmem_limit_bytes=VMEM_BYTES
        ),
    )(
        tokens, cotangent, patch_item.reshape(1, patches), patch_mask.reshape(1, patches),
        text_item, text_len, memory, *weights,
    )


def adam_step(weight, first, second, grad, rate, decay):
    first_new = BETA1 * first + (1.0 - BETA1) * grad
    second_new = BETA2 * second + (1.0 - BETA2) * grad * grad
    mean_hat = first_new / (1.0 - BETA1**STEP)
    square_hat = second_new / (1.0 - BETA2**STEP)
    weight_new = weight - rate * (mean_hat / (jnp.sqrt(square_hat) + ADAM_EPS) + decay * weight)
    return (weight_new, first_new, second_new)


RATES = (
    (0.5, 0.0),
    (2.0 * D**-0.5, DECAY),
    (2.0 * D**-0.5, DECAY),
    (2.0 * D**-0.5, DECAY),
    (2.0 * (D // 16) ** -0.5, DECAY),
    (2.0 * D**-0.5, DECAY),
    (2.0 * FF**-0.5, DECAY),
)


def finish_kernel(*refs):
    (red, kvgrad, norm), refs = refs[:3], refs[3:]
    states_in, refs = refs[:21], refs[21:]
    passed, refs = refs[:3], refs[3:]
    kept, refs = refs[:3], refs[3:]
    (grad_norm,), refs = refs[:1], refs[1:]
    results_to, refs = refs[:21], refs[21:]
    (pad, load_sem, store_sem), held = refs[:3], refs[3:6]
    states, results = refs[6:27], refs[27:48]
    loads = [
        pltpu.make_async_copy(source, target, load_sem.at[i])
        for i, (source, target) in enumerate(zip(states_in + passed, states + held))
    ]
    stores = [
        pltpu.make_async_copy(source, target, store_sem.at[i])
        for i, (source, target) in enumerate(zip(results + held, results_to + kept))
    ]
    order = (23, 22, 21, 15, 16, 17, 18, 19, 20, 3, 4, 5, 12, 13, 14, 9, 10, 11, 6, 7, 8, 0, 1, 2)
    for i in order:
        loads[i].start()
    value = jnp.sqrt(norm[0:1, 0:1])
    grad_norm[0, 0] = value[0, 0]
    factor = jnp.minimum(1.0, CLIP / (value + NORM_EPS))
    pad[...] = jnp.zeros_like(pad)
    pad[0:BLOCK] = red[:, 0:128]
    for i in order[:3]:
        loads[i].wait()
        stores[i].start()

    def update(number, index, grad):
        rate, decay = RATES[number]
        old = [states[3 * number + i][index] for i in range(3)]
        for i, new in enumerate(adam_step(*old, grad * factor, rate, decay)):
            results[3 * number + i][index] = new

    def cut(column, width):
        return red[:, column : column + width]

    def tensor(number, *updates):
        for i in range(3):
            loads[3 * number + i].wait()
        for index, grad in updates:
            update(number, index, grad)
        for i in range(3):
            stores[3 * number + i].start()

    tiles = [(slice(f * FT, (f + 1) * FT), CM + f * 3 * FT) for f in range(FH // FT)]
    every = slice(None)
    tensor(5, *[((i, every, cols), cut(base + i * FT, FT)) for cols, base in tiles for i in range(2)])
    tensor(6, *[((every, cols), cut(base + 2 * FT, FT)) for cols, base in tiles])
    tensor(1, *[(i, cut(CQ + i * HALF, HALF)) for i in range(3)])
    tensor(4, *[(i, cut((COS, COC)[i], HALF)) for i in range(2)])
    tensor(3, *[(i, kvgrad[i]) for i in range(2)])
    tensor(2, (..., cut(CQC, HALF)))
    tensor(0, (..., pad[...].T[0:3, 0:BLOCK]))
    for store in stores:
        store.wait()


def finish(red, kvgrad, norm, states, passed):
    vm = pl.BlockSpec(memory_space=pltpu.VMEM)
    anywhere = pl.BlockSpec(memory_space=pl.ANY)
    shapes = [jax.ShapeDtypeStruct(value.shape, value.dtype) for value in passed]
    shapes += [jax.ShapeDtypeStruct((1, 1), F32)]
    shapes += [jax.ShapeDtypeStruct(value.shape, F32) for value in states]
    return pl.pallas_call(
        finish_kernel,
        out_shape=tuple(shapes),
        in_specs=[vm] * 3 + [anywhere] * 24,
        out_specs=tuple([anywhere] * 3 + [pl.BlockSpec(memory_space=pltpu.SMEM)] + [anywhere] * 21),
        scratch_shapes=[pltpu.VMEM((128, 128), F32), pltpu.SemaphoreType.DMA((24,)), pltpu.SemaphoreType.DMA((24,))]
        + [pltpu.VMEM(value.shape, value.dtype) for value in (*passed, *states, *states)],
        name="finish",
        compiler_params=pltpu.CompilerParams(vmem_limit_bytes=VMEM_BYTES),
    )(red, kvgrad, norm, *states, *passed)


def pack_weights(gains, self_proj, query, keyval, out_proj, mlp_input, mlp_output):
    rows = gains.shape[1]
    turned_out = jnp.swapaxes(out_proj, 1, 2)
    turned_down = mlp_output.T
    pieces = [jnp.pad(gains.T, ((0, 0), (0, 125)))]
    pieces += [self_proj[0], self_proj[1], self_proj[2], keyval[0], keyval[1]]
    pieces += [turned_out[0], query, turned_out[1]]
    for tile in range(FH // FT):
        columns = slice(tile * FT, (tile + 1) * FT)
        pieces += [mlp_input[0][:, columns], mlp_input[1][:, columns], turned_down[:, columns]]
    return jnp.concatenate([piece.astype(BF) for piece in pieces], axis=1)


def unpack_grads(red):
    def cut(start, width):
        return red[:, start : start + width]

    gains = cut(GAIN, 3).T
    self_proj = jnp.stack([cut(CQ + i * HALF, HALF) for i in range(3)])
    keyval = jnp.stack([cut(CKV + i * HALF, HALF) for i in range(2)])
    query = cut(CQC, HALF)
    out_proj = jnp.stack([cut(COS, HALF).T, cut(COC, HALF).T])
    tiles = FH // FT
    mlp = [jnp.concatenate([cut(CM + (3 * tile + k) * FT, FT) for tile in range(tiles)], axis=1) for k in range(3)]
    return gains, self_proj, query, keyval, out_proj, jnp.stack(mlp[:2]), mlp[2].T


def per_device(
    tokens, memory, cotangent, patch_item, patch_mask, text_item, text_len,
    norm_gains, gains_mean, gains_square,
    self_proj, self_proj_mean, self_proj_square,
    query_cross, query_cross_mean, query_cross_square,
    keyval_cross, keyval_cross_mean, keyval_cross_square,
    out_proj, out_proj_mean, out_proj_square,
    mlp_input, mlp_input_mean, mlp_input_square,
    mlp_output, mlp_output_mean, mlp_output_square,
):
    count = lax.axis_size("dp")
    direct = count == 16
    ints = (patch_item, patch_mask, text_item, text_len)
    states = [
        norm_gains, gains_mean, gains_square,
        self_proj, self_proj_mean, self_proj_square,
        query_cross, query_cross_mean, query_cross_square,
        keyval_cross, keyval_cross_mean, keyval_cross_square,
        out_proj, out_proj_mean, out_proj_square,
        mlp_input, mlp_input_mean, mlp_input_square,
        mlp_output, mlp_output_mean, mlp_output_square,
    ]
    if direct:
        for i in range(12, 15):
            states[i] = jnp.swapaxes(states[i], 1, 2)
        for i in range(18, 21):
            states[i] = states[i].T
        output, tokens_grad, memory_grad, red, kvgrad, norm = layer(
            True, tokens, cotangent, *ints, memory, states[::3]
        )
        results = list(finish(red, kvgrad, norm, states, (output, tokens_grad, memory_grad)))
        results[3] = results[3].reshape(())
        for i in range(16, 19):
            results[i] = jnp.swapaxes(results[i], 1, 2)
        for i in range(22, 25):
            results[i] = results[i].T
        return tuple(results)
    keyval_own = lax.all_to_all(keyval_cross.astype(BF), "head", split_axis=2, concat_axis=1, tiled=True)
    pack = pack_weights(norm_gains, self_proj, query_cross, keyval_own, out_proj, mlp_input, mlp_output)
    wall = lax.all_gather(pack, "dp", axis=0, tiled=True).reshape(BLOCKS + (BLOCK, PACK))
    output, tokens_grad, memory_grad, dwall = layer(False, tokens, cotangent, *ints, memory, (wall,))
    red = lax.psum_scatter(dwall.reshape(D, PACK).astype(F32), "dp", scatter_dimension=0, tiled=True)
    squares = jnp.sum(red[:, 128:] ** 2)
    squares = squares + jnp.where(lax.axis_index("head") == 0, jnp.sum(red[:, :128] ** 2), 0.0)
    total = lax.psum(squares, ("dp", "head"))
    gains_g, self_g, query_g, keyval_g, out_g, input_g, output_g = unpack_grads(red)
    keyval_g = lax.all_to_all(keyval_g, "head", split_axis=1, concat_axis=2, tiled=True)
    grad_norm = jnp.sqrt(total)
    factor = jnp.minimum(1.0, CLIP / (grad_norm + NORM_EPS))
    results = [output, tokens_grad, memory_grad, grad_norm]
    grads = (gains_g, self_g, query_g, keyval_g, out_g, input_g, output_g)
    for i, (grad, (rate, decay)) in enumerate(zip(grads, RATES)):
        results += adam_step(*states[3 * i : 3 * i + 3], grad * factor, rate, decay)
    return tuple(results)


def solution(mesh):
    in_specs = (
        P("dp", None),
        P(("dp", "head"), None),
        P("dp", None),
        P("dp"),
        P("dp"),
        P("dp"),
        P("dp"),
        P(None, "dp"),
        P(None, "dp"),
        P(None, "dp"),
        P(None, "dp", "head"),
        P(None, "dp", "head"),
        P(None, "dp", "head"),
        P("dp", "head"),
        P("dp", "head"),
        P("dp", "head"),
        P(None, ("dp", "head"), None),
        P(None, ("dp", "head"), None),
        P(None, ("dp", "head"), None),
        P(None, "head", "dp"),
        P(None, "head", "dp"),
        P(None, "head", "dp"),
        P(None, "dp", "head"),
        P(None, "dp", "head"),
        P(None, "dp", "head"),
        P("head", "dp"),
        P("head", "dp"),
        P("head", "dp"),
    )
    out_specs = (
        P("dp", None),
        P("dp", None),
        P(("dp", "head"), None),
        P(),
        P(None, "dp"),
        P(None, "dp"),
        P(None, "dp"),
        P(None, "dp", "head"),
        P(None, "dp", "head"),
        P(None, "dp", "head"),
        P("dp", "head"),
        P("dp", "head"),
        P("dp", "head"),
        P(None, ("dp", "head"), None),
        P(None, ("dp", "head"), None),
        P(None, ("dp", "head"), None),
        P(None, "head", "dp"),
        P(None, "head", "dp"),
        P(None, "head", "dp"),
        P(None, "dp", "head"),
        P(None, "dp", "head"),
        P(None, "dp", "head"),
        P("head", "dp"),
        P("head", "dp"),
        P("head", "dp"),
    )
    return jax.shard_map(
        per_device, mesh=mesh, in_specs=in_specs, out_specs=out_specs, check_vma=False
    )
```
